512 devices in a mesh: band: 16 (over z_hi, y), domain: 32 (over x, z_lo, core).
Axes of the slice: x: 4, y: 8, z: 8 (z_hi: 2, z_lo: 4; z = z_hi * 4 + z_lo), core: 2. Of those that a mesh axis runs over, the one named last changes fastest.
Arguments:
- orbitals: float32 [128, 128, 64, 128], P('band', 'domain'), may hold values from -160 to 160
- potential: float32 [128, 64, 128], P('domain'), may hold values from -2.5 to 0.5
Outputs:
- basis_out: float32 [128, 128, 64, 128], P('band', 'domain')
- residual: float32 [128, 128, 64, 128], P('band', 'domain')
The draws below stay inside these ranges and needn't reach their ends.
All inputs are finite; a program needn't handle non-finite values.
Results may differ from the reference program's by a relative error of at most 0.00015.
Values sent between devices are 32-bit elements; how exact they have to be, the bound alone decides.
No kernel may reach another device: no remote copies, remote signals or barrier semaphores. Data moves between devices by JAX's collectives and lax.ppermute only.
A program may use at most 128 MiB of HBM per device.

```python
import math
import jax
import jax.numpy as jnp
from jax import lax

BLK = 8
NY = 64
NZ = 128
STEPS = 2
NORB = 128
NX = 128
N_BAND = 16


def draw_orbitals(key, part):
    key = jax.random.fold_in(key, 5)
    keys_all = jax.random.split(key, 5)
    private = jnp.clip(jax.random.normal(keys_all[0], (NORB, NX, NY, NZ)), -4.0, 4.0)
    common = jnp.clip(jax.random.normal(keys_all[1], (BLK, NX, NY, NZ)), -4.0, 4.0)
    global_part = jnp.clip(jax.random.normal(keys_all[2], (1, NX, NY, NZ)), -4.0, 4.0)
    common_weight = 0.8
    top_scale = 4.0
    orbital_scale = jnp.exp(jax.random.uniform(keys_all[3], (NORB, 1, 1, 1), minval=0.0, maxval=math.log(top_scale)))
    cell_scale = jnp.exp(jax.random.uniform(keys_all[4], (1, NX, NY, NZ), minval=math.log(0.5), maxval=math.log(2.0)))
    position = jnp.arange(NX).astype(jnp.float32).reshape(1, NX, 1, 1)
    cell_scale = cell_scale * (1.0 + 0.8 * position / NX)
    mixed = private + common_weight * jnp.tile(common, (NORB // BLK, 1, 1, 1)) + 0.5 * global_part
    return (orbital_scale * cell_scale * mixed).astype(jnp.float32)


def draw_potential(key, part):
    key = jax.random.fold_in(key, 7)
    position = jnp.arange(NX).astype(jnp.float32).reshape(NX, 1, 1)
    slope_part = -2.0 + 2.0 * position / NX
    rough_part = jax.random.uniform(key, (NX, NY, NZ), minval=-0.5, maxval=0.5)
    return (slope_part + rough_part).astype(jnp.float32)


def setup_inputs(seed: int = 0) -> dict:
    keys = jax.random.split(jax.random.key(seed), 3)
    return {
        "orbitals": draw_orbitals(jax.random.fold_in(keys[2], 71), 0),
        "potential": draw_potential(jax.random.fold_in(keys[2], 71), 0),
    }


stencil_weights = (-205.0 / 72.0, 8.0 / 5.0, -1.0 / 5.0, 8.0 / 315.0, -1.0 / 560.0)

def cholesky_lower(matrix):
    size_now = matrix.shape[0]
    positions = jnp.arange(size_now, dtype=jnp.int32)

    def column_step(column_index, lower_now):
        unit = (positions == column_index).astype(matrix.dtype)
        row_part = jnp.dot(unit, lower_now, precision=lax.Precision.HIGHEST)
        column_part = jnp.dot(matrix, unit, precision=lax.Precision.HIGHEST)
        partial_column = column_part - jnp.dot(lower_now, row_part, precision=lax.Precision.HIGHEST)
        pivot = jnp.sqrt(jnp.dot(unit, partial_column, precision=lax.Precision.HIGHEST))
        fresh = jnp.where(positions >= column_index, partial_column / pivot, jnp.zeros_like(partial_column))
        return lower_now + fresh[:, None] * unit[None, :]
    return lax.fori_loop(0, size_now, column_step, jnp.zeros_like(matrix))

def lower_inverse(lower_factor):
    size_now = lower_factor.shape[0]
    positions = jnp.arange(size_now, dtype=jnp.int32)

    def row_step(row_index, inverse_now):
        unit = (positions == row_index).astype(lower_factor.dtype)
        lower_row = jnp.dot(unit, lower_factor, precision=lax.Precision.HIGHEST)
        pivot = jnp.dot(lower_row, unit, precision=lax.Precision.HIGHEST)
        fresh = (unit - jnp.dot(lower_row, inverse_now, precision=lax.Precision.HIGHEST)) / pivot
        return inverse_now + unit[:, None] * fresh[None, :]
    return lax.fori_loop(0, size_now, row_step, jnp.zeros_like(lower_factor))

def apply_hamiltonian(orbital_field, potential):
    laplacian = 3.0 * stencil_weights[0] * orbital_field
    for offset in range(1, 5):
        weight_now = stencil_weights[offset]
        for axis_number in (1, 2, 3):
            laplacian = laplacian + weight_now * (jnp.roll(orbital_field, offset, axis_number) + jnp.roll(orbital_field, -offset, axis_number))
    return -0.5 * laplacian + potential[None] * orbital_field

def reference(orbitals, potential):
    cells_total = float(NX * NY * NZ)
    current = orbitals.reshape(NORB, NX * NY * NZ)
    block_of_row = (jnp.arange(NORB) // BLK).astype(jnp.int32)
    for step_index in range(STEPS):
        start = step_index * BLK
        block_rows = current[start:start + BLK]
        gram = jnp.dot(block_rows, block_rows.T, precision=lax.Precision.HIGHEST) / cells_total
        inverse_factor = lower_inverse(cholesky_lower(gram))
        basis = jnp.dot(inverse_factor, block_rows, precision=lax.Precision.HIGHEST)
        correlation = jnp.dot(basis, current.T, precision=lax.Precision.HIGHEST) / cells_total
        projected = current - jnp.dot(correlation.T, basis, precision=lax.Precision.HIGHEST)
        current = jnp.where((block_of_row > step_index)[:, None], projected, current)
        current = jnp.concatenate([current[:start], basis, current[start + BLK:]], axis=0)
    blocks_view = current.reshape(N_BAND, BLK, NX, NY, NZ)

    def per_block(block_field):
        applied = apply_hamiltonian(block_field, potential).reshape(BLK, -1)
        rows = block_field.reshape(BLK, -1)
        block_gram = jnp.dot(rows, rows.T, precision=lax.Precision.HIGHEST) / cells_total
        theta = jnp.dot(rows, applied.T, precision=lax.Precision.HIGHEST) / cells_total
        inverse_block = lower_inverse(cholesky_lower(block_gram))
        halfway = jnp.dot(inverse_block, theta, precision=lax.Precision.HIGHEST)
        coeff = jnp.dot(inverse_block.T, halfway, precision=lax.Precision.HIGHEST)
        return applied - jnp.dot(coeff.T, rows, precision=lax.Precision.HIGHEST)
    residual = lax.map(per_block, blocks_view)
    return (current.reshape(NORB, NX, NY, NZ), residual.reshape(NORB, NX, NY, NZ))
```

```python
import jax
import jax.numpy as jnp
from jax import lax
from jax.experimental import pallas as pl
from jax.experimental.pallas import tpu as pltpu
from jax.sharding import PartitionSpec as P

stencil_weights = (-205.0 / 72.0, 8.0 / 5.0, -1.0 / 5.0, 8.0 / 315.0, -1.0 / 560.0)
BLK = 8
RING = 8
F32 = jnp.float32
VMEM = pl.BlockSpec(memory_space=pltpu.VMEM)
SMEM = pl.BlockSpec(memory_space=pltpu.SMEM)


def call(kernel, outs, scratch=(), specs=None, flops=0, bytes_moved=0):
    return pl.pallas_call(
        kernel,
        out_shape=outs,
        in_specs=specs,
        out_specs=jax.tree.map(lambda _: VMEM, outs),
        scratch_shapes=scratch,
        compiler_params=pltpu.CompilerParams(vmem_limit_bytes=32 * 1024 * 1024),
        cost_estimate=pl.CostEstimate(flops=flops, bytes_accessed=bytes_moved, transcendentals=0),
    )


def lanes():
    return lax.broadcasted_iota(jnp.int32, (8, 128), 1)


def subs():
    return lax.broadcasted_iota(jnp.int32, (8, 128), 0)


def pair_sums(first, second, chunks, symmetric):
    lane = lanes()
    result = jnp.zeros((8, 128), F32)
    for low in (0, 4):
        partners = second[low:] if symmetric else second

        def body(c, sums, low=low, partners=partners):
            left = [load(c) for load in first[low : low + 4]]
            right = [load(c) for load in partners]
            return tuple(
                s + left[n // len(partners)] * right[n % len(partners)]
                for n, s in enumerate(sums)
            )

        zero = jnp.zeros((8, 128), F32)
        sums = lax.fori_loop(0, chunks, body, (zero,) * (4 * len(partners)))
        for i in range(4):
            rows = [
                jnp.sum(s, axis=0, keepdims=True)
                for s in sums[i * len(partners) : (i + 1) * len(partners)]
            ]
            rows = [jnp.zeros((1, 128), F32)] * (8 - len(rows)) + rows
            column = jnp.sum(jnp.concatenate(rows, axis=0), axis=1, keepdims=True)
            result = jnp.where(lane == low + i, column, result)
    return result


def loader(ref, index):
    return lambda c: ref[index, pl.ds(pl.multiple_of(c * 8, 8), 8), :]


def move(tile, source, target):
    lane = lanes()
    if source != target:
        tile = pltpu.roll(tile, (target - source) % 128, 1)
    return jnp.where((lane >= target) & (lane < target + 8), tile, 0.0)


def flipped(sums):
    return jnp.transpose(jnp.concatenate([sums, jnp.zeros((120, 128), F32)], axis=0))


def completed(sums, turned, slot):
    lane, sub = lanes(), subs()
    other = turned[8 * slot : 8 * slot + 8, :]
    if slot:
        other = pltpu.roll(other, 8 * slot, 1)
    missing = (lane >= 8 * slot + 4) & (lane < 8 * slot + 8) & (sub < 4)
    return jnp.where(missing, other, sums)


def spread_lane(tile, k):
    return jnp.broadcast_to(tile[:, k : k + 1], (8, 128))


def rows_of(refs):
    return [(r, i) for r in refs for i in range(r.shape[0])]


def gram_kernel(*refs):
    *pieces, own, out = refs
    chunks = own.shape[1] // 8
    gathered = [loader(r, i) for r, i in rows_of(pieces)]
    low, high = gathered[:8], gathered[8:]
    block = [loader(own, i) for i in range(BLK)]
    total = jnp.zeros((8, 128), F32)
    tiles = (
        (low, low, True),
        (low, high, False),
        (low, block, False),
        (high, high, True),
        (high, block, False),
        (block, block, True),
    )
    for slot, (first, second, symmetric) in enumerate(tiles):
        total = total + move(pair_sums(first, second, chunks, symmetric), 0, 8 * slot)
    for n in range(out.shape[0]):
        out[n] = total


def combine_kernel(cells_total, band_ref, sums_ref, *refs):
    *pieces, own, out, splat = refs
    band = band_ref[0]
    lane, sub = lanes(), subs()
    sums = jnp.sum(sums_ref[...], axis=0) / cells_total
    turned = flipped(sums)
    w0 = (
        move(completed(sums, turned, 0), 0, 0)
        + move(turned[8:16, :], 0, 8)
        + move(turned[16:24, :], 0, 16)
    )
    w1 = (
        move(sums, 8, 0)
        + move(completed(sums, turned, 3), 24, 8)
        + move(turned[32:40, :], 0, 16)
    )
    w2 = (
        move(sums, 16, 0)
        + move(sums, 32, 8)
        + move(completed(sums, turned, 5), 40, 16)
        + jnp.where(lane == 40 + sub, 1.0, 0.0)
    )
    later = band >= 2
    second = band == 1

    def taken(position):
        place = position & 7
        return later | (second & (place >= 2) & (place <= 5))

    row_in = taken(sub)
    lane_in = (lane >= 16) | taken(lane)
    kept = row_in & lane_in
    w0 = jnp.where(lane < 24, jnp.where(kept, w0, jnp.where(lane == sub, 1.0, 0.0)), 0.0)
    w1 = jnp.where(lane < 24, jnp.where(kept, w1, jnp.where(lane == 8 + sub, 1.0, 0.0)), 0.0)
    w0 = w0 + jnp.where(lane == 24 + sub, 1.0, 0.0)
    w1 = w1 + jnp.where(lane == 32 + sub, 1.0, 0.0)
    w2 = jnp.where(lane_in, w2, 0.0)
    tiles = [w0, w1, w2]
    for k in range(16):
        v, s = divmod(k, 8)
        row = tiles[v][s : s + 1, :]
        row = row / jnp.broadcast_to(row[:, k : k + 1], (1, 128))
        row = jnp.broadcast_to(row, (8, 128))
        for u in range(v, 3):
            column = spread_lane(tiles[u], k)
            if u == v:
                column = jnp.where(sub > s, column, 0.0)
            tiles[u] = tiles[u] - column * row
    plain = tiles[2]
    scaled = plain
    for k in range(8):
        row = scaled[k : k + 1, :]
        row = row / jnp.broadcast_to(row[:, 16 + k : 17 + k], (1, 128))
        column = jnp.where(sub > k, spread_lane(scaled, 16 + k), 0.0)
        scaled = scaled - column * jnp.broadcast_to(row, (8, 128))
    pivots = jnp.sum(jnp.where(lane == 16 + sub, scaled, 0.0), axis=1, keepdims=True)
    scaled = scaled / jnp.sqrt(jnp.broadcast_to(pivots, (8, 128)))
    weights = jnp.where(later, plain, scaled)
    for c in range(24):
        splat[c] = spread_lane(weights, 24 + c)
    rows = rows_of(pieces) + [(own, i) for i in range(BLK)]

    def body(c, carry):
        part = pl.ds(pl.multiple_of(c * 16, 16), 16)
        inputs = [r[i, part, :] for r, i in rows]
        for i in range(BLK):
            total = splat[0, pl.ds(i, 1), :] * inputs[0]
            for n in range(1, 24):
                total = total + splat[n, pl.ds(i, 1), :] * inputs[n]
            out[i, part, :] = total
        return carry

    lax.fori_loop(0, own.shape[1] // 16, body, 0)


def inner_kernel(f_ref, v_ref, out, gram):
    def body(i, carry):
        layers = [f_ref[i, x] for x in range(4)]
        for x in range(4):
            here = layers[x]
            total = 3.0 * stencil_weights[0] * here
            for offset in range(1, 5):
                beside = pltpu.roll(here, offset, 0) + pltpu.roll(here, 64 - offset, 0)
                beside = beside + pltpu.roll(here, offset, 1) + pltpu.roll(here, 128 - offset, 1)
                if x + offset < 4:
                    beside = beside + layers[x + offset]
                if x - offset >= 0:
                    beside = beside + layers[x - offset]
                total = total + stencil_weights[offset] * beside
            out[i, x] = -0.5 * total + v_ref[x] * here
        return carry

    lax.fori_loop(0, BLK, body, 0)

    def row(i):
        return lambda c: f_ref[i, c // 8, pl.ds(pl.multiple_of((c % 8) * 8, 8), 8), :]

    rows = [row(i) for i in range(BLK)]
    gram[...] = pair_sums(rows, rows, 32, True)


def edge_kernel(f_ref, inner_ref, left_ref, right_ref, gram_ref, out, sums):
    def body(i, carry):
        for x in range(4):
            total = None
            for offset in range(1, 5):
                if x + offset >= 4:
                    term = stencil_weights[offset] * right_ref[i, x + offset - 4]
                    total = term if total is None else total + term
                if x - offset < 0:
                    term = stencil_weights[offset] * left_ref[i, x - offset + 4]
                    total = term if total is None else total + term
            out[i, x] = inner_ref[i, x] - 0.5 * total
        return carry

    lax.fori_loop(0, BLK, body, 0)

    def row(ref, i):
        return lambda c: ref[i, c // 8, pl.ds(pl.multiple_of((c % 8) * 8, 8), 8), :]

    theta = pair_sums(
        [row(out, i) for i in range(BLK)], [row(f_ref, i) for i in range(BLK)], 32, False
    )
    total = gram_ref[...] + move(theta, 0, 8)
    for n in range(sums.shape[0]):
        sums[n] = total


def residual_kernel(cells_total, sums_ref, f_ref, h_ref, out, splat):
    lane, sub = lanes(), subs()
    sums = jnp.sum(sums_ref[...], axis=0) / cells_total
    work = completed(sums, flipped(sums), 0)
    for k in range(8):
        row = work[k : k + 1, :]
        row = jnp.broadcast_to(row / jnp.broadcast_to(row[:, k : k + 1], (1, 128)), (8, 128))
        work = jnp.where(sub == k, row, work - spread_lane(work, k) * row)
    for j in range(8):
        splat[j] = spread_lane(work, 8 + j)

    def body(c, carry):
        part = pl.ds(pl.multiple_of(c * 16, 16), 16)
        inputs = [f_ref[i, part, :] for i in range(BLK)]
        for j in range(BLK):
            total = h_ref[j, part, :]
            for i in range(BLK):
                total = total - splat[j, pl.ds(i, 1), :] * inputs[i]
            out[j, part, :] = total
        return carry

    lax.fori_loop(0, f_ref.shape[1] // 16, body, 0)


def domain_parts(copies):
    return lax.all_to_all(copies, "domain", 0, 0)


def ring_shift(block, step):
    pairs = [(z * RING + y, z * RING + (y + step) % RING) for z in range(2) for y in range(RING)]
    return lax.ppermute(block, "band", pairs)


def local(orbitals, potential):
    blocks, slab_width, rows_y, rows_z = orbitals.shape
    domain = lax.axis_size("domain")
    cells_total = float(slab_width * rows_y * rows_z * domain)
    band = lax.axis_index("band")
    flat = (blocks, slab_width * rows_y, rows_z)
    own = orbitals.reshape(flat)
    quarters = [own[2 * k : 2 * k + 2] for k in range(4)]
    piece = jnp.where(band < 2, quarters[0], 0.0)
    for k in (1, 3, 2):
        piece = piece + lax.ppermute(quarters[k], "band", [(0, 2 * k), (1, 2 * k + 1)])
    crossed = lax.ppermute(piece, "band", [(y, y + RING) for y in range(RING)])
    piece = jnp.where(band < RING, piece, crossed)
    pieces = [piece]
    up = down = piece
    for _ in range(3):
        up, down = ring_shift(up, 1), ring_shift(down, -1)
        pieces += [up, down]
    pieces += [ring_shift(up[:1], 1), ring_shift(down[1:], -1)]

    big = flat[0] * flat[1] * flat[2]
    sums = call(
        gram_kernel,
        jax.ShapeDtypeStruct((domain, 8, 128), F32),
        specs=[VMEM] * 10,
        flops=40 * big,
        bytes_moved=12 * big,
    )(*pieces, own)
    sums = domain_parts(sums)
    basis = call(
        lambda *refs: combine_kernel(cells_total, *refs),
        jax.ShapeDtypeStruct(flat, F32),
        scratch=[pltpu.VMEM((24, 8, 128), F32)],
        specs=[SMEM] + [VMEM] * 11,
        flops=48 * big,
        bytes_moved=16 * big,
    )(band.reshape(1).astype(jnp.int32), sums, *pieces, own)
    field = basis.reshape(orbitals.shape)
    count = domain
    left = lax.ppermute(field, "domain", [(i, (i + 1) % count) for i in range(count)])
    right = lax.ppermute(field, "domain", [((i + 1) % count, i) for i in range(count)])
    inner, gram = call(
        inner_kernel,
        (
            jax.ShapeDtypeStruct(orbitals.shape, F32),
            jax.ShapeDtypeStruct((8, 128), F32),
        ),
        specs=[VMEM] * 2,
        flops=60 * big,
        bytes_moved=8 * big,
    )(field, potential)
    applied, sums = call(
        edge_kernel,
        (
            jax.ShapeDtypeStruct(orbitals.shape, F32),
            jax.ShapeDtypeStruct((domain, 8, 128), F32),
        ),
        specs=[VMEM] * 5,
        flops=40 * big,
        bytes_moved=20 * big,
    )(field, inner, left, right, gram)
    sums = domain_parts(sums)
    residual = call(
        lambda *refs: residual_kernel(cells_total, *refs),
        jax.ShapeDtypeStruct(flat, F32),
        scratch=[pltpu.VMEM((8, 8, 128), F32)],
        specs=[VMEM] * 3,
        flops=16 * big,
        bytes_moved=12 * big,
    )(sums, basis, applied.reshape(flat))
    return (field, residual.reshape(orbitals.shape))


def solution(mesh):
    return jax.shard_map(
        local,
        mesh=mesh,
        in_specs=(P("band", "domain", None, None), P("domain", None, None)),
        out_specs=(P("band", "domain", None, None), P("band", "domain", None, None)),
        check_vma=False,
    )
```

```python
import jax
import jax.numpy as jnp
from jax import lax
from jax.experimental import pallas as pl
from jax.experimental.pallas import tpu as pltpu
from jax.sharding import PartitionSpec as P

stencil_weights = (-205.0 / 72.0, 8.0 / 5.0, -1.0 / 5.0, 8.0 / 315.0, -1.0 / 560.0)
BLK = 8
RING = 8
F32 = jnp.float32
VMEM = pl.BlockSpec(memory_space=pltpu.VMEM)
SMEM = pl.BlockSpec(memory_space=pltpu.SMEM)


def call(kernel, outs, scratch=(), specs=None, flops=0, bytes_moved=0):
    return pl.pallas_call(
        kernel,
        out_shape=outs,
        in_specs=specs,
        out_specs=jax.tree.map(lambda _: VMEM, outs),
        scratch_shapes=scratch,
        compiler_params=pltpu.CompilerParams(vmem_limit_bytes=32 * 1024 * 1024),
        cost_estimate=pl.CostEstimate(flops=flops, bytes_accessed=bytes_moved, transcendentals=0),
    )


def lanes():
    return lax.broadcasted_iota(jnp.int32, (8, 128), 1)


def subs():
    return lax.broadcasted_iota(jnp.int32, (8, 128), 0)


def pair_sums(jobs, load, chunks):
    lane = lanes()
    result = jnp.zeros((8, 128), F32)
    zero_row = jnp.zeros((1, 128), F32)
    for pairs in jobs:
        used = sorted({n for pair in pairs for n in pair})

        def body(c, sums, pairs=pairs, used=used):
            for step in range(4):
                rows = {n: load[n](4 * c + step) for n in used}
                sums = tuple(s + rows[q] * rows[r] for s, (q, r) in zip(sums, pairs))
            return sums

        zero = jnp.zeros((8, 128), F32)
        sums = lax.fori_loop(0, chunks // 4, body, (zero,) * len(pairs))
        columns = {}
        for s, (q, r) in zip(sums, pairs):
            rows = columns.setdefault(32 * (r // 8) + q, [zero_row] * 8)
            rows[r % 8] = jnp.sum(s, axis=0, keepdims=True)
        for place, rows in columns.items():
            column = jnp.sum(jnp.concatenate(rows, axis=0), axis=1, keepdims=True)
            result = result + jnp.where(lane == place, column, 0.0)
    return result


def loader(ref, index):
    return lambda c: ref[index, pl.ds(pl.multiple_of(c * 8, 8), 8), :]


def move(tile, source, target):
    lane = lanes()
    if source != target:
        tile = pltpu.roll(tile, (target - source) % 128, 1)
    return jnp.where((lane >= target) & (lane < target + 8), tile, 0.0)


def spread_lane(tile, k):
    return jnp.broadcast_to(tile[:, k : k + 1], (8, 128))


def rows_of(refs):
    return [(r, i) for r in refs for i in range(r.shape[0])]


def unpacked(sums):
    lane = lanes()
    parts = [sums] + [pltpu.roll(sums, 128 - 32 * n, 1) for n in (1, 2)]
    return [jnp.where(lane < 32, part, 0.0) for part in parts]


def tall(tiles):
    return jnp.concatenate(tiles + [jnp.zeros((128 - 8 * len(tiles), 128), F32)], axis=0)


OWN = list(range(16, 24))
IMAGE = list(range(24, 32))


def split(pairs, size=36):
    if not pairs:
        return []
    count = -(-len(pairs) // size)
    size = -(-len(pairs) // count)
    return [pairs[n : n + size] for n in range(0, len(pairs), size)]


def stage_kernel(parts, fresh, imaged, last, *refs):
    out = refs[-1]
    pieces, refs = refs[:parts], refs[parts:-1]
    own, image, before = (refs[0], refs[1], refs[2:]) if imaged else (refs[0], None, refs[1:])
    chunks = own.shape[1] // 8
    load = {n: loader(r, i) for n, (r, i) in enumerate(rows_of(pieces))}
    load |= {n: loader(own, n - 16) for n in OWN}
    if imaged:
        load |= {n: loader(image, n - 24) for n in IMAGE}
    jobs = split([(q, r) for q in OWN for r in fresh])
    jobs += split([(q, r) for q in fresh for r in range(q + 1)])
    jobs += split([(q, r) for q in IMAGE for r in imaged])
    total = pair_sums(jobs, load, chunks)
    for part in before[: len(before) - last]:
        total = total + part[...]
    if last:
        for n in range(3):
            total = total + move(before[-1][...], 32 * n + 24, 96 + 8 * n)
        for n in range(out.shape[0]):
            out[n] = total
    else:
        out[...] = total


def combine_kernel(cells_total, band_ref, sums_ref, *refs):
    *pieces, own, out, weights_ref, gram_ref, shared, splat = refs
    band = band_ref[0]
    lane, sub = lanes(), subs()
    sums = jnp.sum(sums_ref[...], axis=0) / cells_total
    for n in range(shared.shape[0]):
        shared[n] = sums
    tiles = unpacked(sums)
    turned = jnp.transpose(tall(tiles))
    w0, w1, w2 = (
        jnp.where(lane < 24, tile + jnp.where(lane == sub + 8 * n, 0.0, turned[8 * n : 8 * n + 8]), 0.0)
        for n, tile in enumerate(tiles)
    )
    later = band >= 2
    second = band == 1

    def taken(position):
        place = position & 7
        return later | (second & (place >= 2) & (place <= 5))

    row_in = taken(sub)
    lane_in = (lane >= 16) | taken(lane)
    kept = row_in & lane_in
    w0 = jnp.where(kept, w0, jnp.where(lane == sub, 1.0, 0.0))
    w1 = jnp.where(kept, w1, jnp.where(lane == 8 + sub, 1.0, 0.0))
    w0 = w0 + jnp.where(lane == 24 + sub, 1.0, 0.0)
    w1 = w1 + jnp.where(lane == 32 + sub, 1.0, 0.0)
    w2 = jnp.where(lane_in, w2, 0.0) + jnp.where(lane == 40 + sub, 1.0, 0.0)
    tiles = [w0, w1, w2]
    for k in range(16):
        v, s = divmod(k, 8)
        row = tiles[v][s : s + 1, :]
        row = row / jnp.broadcast_to(row[:, k : k + 1], (1, 128))
        row = jnp.broadcast_to(row, (8, 128))
        for u in range(v, 3):
            column = spread_lane(tiles[u], k)
            if u == v:
                column = jnp.where(sub > s, column, 0.0)
            tiles[u] = tiles[u] - column * row
    plain = tiles[2]
    scaled = plain
    for k in range(8):
        row = scaled[k : k + 1, :]
        row = row / jnp.broadcast_to(row[:, 16 + k : 17 + k], (1, 128))
        column = jnp.where(sub > k, spread_lane(scaled, 16 + k), 0.0)
        scaled = scaled - column * jnp.broadcast_to(row, (8, 128))
    pivots = jnp.sum(jnp.where(lane == 16 + sub, scaled, 0.0), axis=1, keepdims=True)
    scaled = scaled / jnp.sqrt(jnp.broadcast_to(pivots, (8, 128)))
    weights = jnp.where(later, plain, scaled)
    weights_ref[...] = weights
    gram_ref[...] = jnp.where(later, move(plain, 16, 0), jnp.where(lane == sub, 1.0, 0.0))
    for c in range(24):
        splat[c] = spread_lane(weights, 24 + c)
    rows = rows_of(pieces) + [(own, i) for i in range(BLK)]

    def body(c, carry):
        part = pl.ds(pl.multiple_of(c * 16, 16), 16)
        inputs = [r[i, part, :] for r, i in rows]
        for i in range(BLK):
            total = splat[0, pl.ds(i, 1), :] * inputs[0]
            for n in range(1, 24):
                total = total + splat[n, pl.ds(i, 1), :] * inputs[n]
            out[i, part, :] = total
        return carry

    lax.fori_loop(0, own.shape[1] // 16, body, 0)


def inner_kernel(f_ref, v_ref, out, *sums):
    def body(i, carry):
        layers = [f_ref[i, x] for x in range(4)]
        for x in range(4):
            here = layers[x]
            total = 3.0 * stencil_weights[0] * here
            for offset in range(1, 5):
                beside = pltpu.roll(here, offset, 0) + pltpu.roll(here, 64 - offset, 0)
                beside = beside + pltpu.roll(here, offset, 1) + pltpu.roll(here, 128 - offset, 1)
                if x + offset < 4:
                    beside = beside + layers[x + offset]
                if x - offset >= 0:
                    beside = beside + layers[x - offset]
                total = total + stencil_weights[offset] * beside
            out[i, x] = -0.5 * total + v_ref[x] * here
        return carry

    lax.fori_loop(0, BLK, body, 0)
    if sums:

        def row(i):
            return lambda c: f_ref[i, c // 8, pl.ds(pl.multiple_of((c % 8) * 8, 8), 8), :]

        load = {n: row(n - 16) for n in OWN}
        sums[0][...] = pair_sums([[(q, r) for q in OWN for r in range(16, q + 1)]], load, 32)


def edged(inner, x, left, right):
    total = None
    for offset in range(1, 5):
        if x + offset >= 4:
            term = stencil_weights[offset] * right(x + offset - 4)
            total = term if total is None else total + term
        if x - offset < 0:
            term = stencil_weights[offset] * left(x - offset + 4)
            total = term if total is None else total + term
    return inner - 0.5 * total


def image_kernel(own, inner, left, right, out, sums):
    def body(i, carry):
        for x in range(4):
            part = pl.ds(64 * x, 64)
            out[i, part, :] = edged(
                inner[i, part, :],
                x,
                lambda n: left[i, pl.ds(64 * n, 64), :],
                lambda n: right[i, pl.ds(64 * n, 64), :],
            )
        return carry

    lax.fori_loop(0, BLK, body, 0)
    load = {n: loader(own, n - 16) for n in OWN}
    load |= {n: loader(out, n - 24) for n in IMAGE}
    jobs = split([(q, r) for q in IMAGE for r in OWN], 32)
    sums[...] = pair_sums(jobs, load, own.shape[1] // 8)


def dot(left, right, turn_left=False, turn_right=False):
    dims = (((0 if turn_left else 1,), (1 if turn_right else 0,)), ((), ()))
    return lax.dot_general(
        left, right, dims, precision=lax.Precision.HIGHEST, preferred_element_type=F32
    )


def places(y, home=None):
    row = lax.broadcasted_iota(jnp.int32, (128, 128), 0)
    lane = lax.broadcasted_iota(jnp.int32, (128, 128), 1)
    distance = (row + 2) >> 2
    distance = jnp.where(((row + 2) & 2) == 0, -distance, distance)
    piece = (y + distance) & 7
    target = (piece & 1) * 8 + (piece >> 1) * 2 + (row & 1)
    if home is None:
        target = jnp.where(row < 16, target, row)
    else:
        target = jnp.where((piece & 1) == home, -1, target)
        target = jnp.where(row < 16, target, row - 16 + 8 * home)
    return jnp.where((lane == target) & (row < 24), 1.0, 0.0)


def coeff_kernel(band_ref, weights_ref, gram_ref, own_ref, shared_ref, out):
    lane, sub = lanes(), subs()
    wide = lax.broadcasted_iota(jnp.int32, (128, 128), 1)
    row = lax.broadcasted_iota(jnp.int32, (128, 128), 0)
    place = places(band_ref[0] & 7)
    weights = jnp.where(lane < 24, pltpu.roll(weights_ref[...], 104, 1), 0.0)
    weights = dot(weights, place)

    def image_columns(matrix, place, source, target):
        columns = dot(place, matrix, turn_left=True)
        columns = pltpu.roll(columns, (target - source) % 128, 1)
        return jnp.where((wide >= target) & (wide < target + 8), columns, 0.0)

    def visiting(n):
        packed = shared_ref[n]
        home = tall([move(packed, 32 * k + 24, 0) for k in range(3)])
        away = tall([move(packed, 96 + 8 * k, 0) for k in range(3)])
        matrix = jnp.where(band_ref[0] < RING, home, away)
        return image_columns(matrix, places(n, n), 0, 8 * n)

    block0, block1 = visiting(0), visiting(1)
    block = image_columns(tall(unpacked(own_ref[...])), place, 24, 16)
    half = dot(weights, block0 + block1 + block)
    half = half + dot(weights, jnp.where(row < 16, block, 0.0), turn_right=True)
    theta = dot(half, tall([weights]), turn_right=True)
    work = gram_ref[...] + move(theta, 0, 8)
    for k in range(8):
        line = work[k : k + 1, :]
        line = jnp.broadcast_to(line / jnp.broadcast_to(line[:, k : k + 1], (1, 128)), (8, 128))
        work = jnp.where(sub == k, line, work - spread_lane(work, k) * line)
    for j in range(8):
        out[j] = spread_lane(work, 8 + j)


def residual_kernel(f_ref, inner_ref, left_ref, right_ref, splat, out):
    def body(c, carry):
        def part(x):
            return pl.ds(pl.multiple_of(64 * x + 8 * c, 8), 8)

        for x in range(4):
            inputs = [f_ref[i, part(x), :] for i in range(BLK)]
            for j in range(BLK):
                total = edged(
                    inner_ref[j, part(x), :],
                    x,
                    lambda n: left_ref[j, part(n), :],
                    lambda n: right_ref[j, part(n), :],
                )
                for i in range(BLK):
                    total = total - splat[j, pl.ds(i, 1), :] * inputs[i]
                out[j, part(x), :] = total
        return carry

    lax.fori_loop(0, 8, body, 0)


def domain_parts(copies):
    return lax.all_to_all(copies, "domain", 0, 0)


def ring_shift(block, step):
    pairs = [(z * RING + y, z * RING + (y + step) % RING) for z in range(2) for y in range(RING)]
    return lax.ppermute(block, "band", pairs)


def neighbours(block):
    count = lax.axis_size("domain")
    left = lax.ppermute(block, "domain", [(i, (i + 1) % count) for i in range(count)])
    right = lax.ppermute(block, "domain", [((i + 1) % count, i) for i in range(count)])
    return left, right


def local(orbitals, potential):
    blocks, slab_width, rows_y, rows_z = orbitals.shape
    domain, bands = lax.axis_size("domain"), lax.axis_size("band")
    cells_total = float(slab_width * rows_y * rows_z * domain)
    band = lax.axis_index("band")
    band_word = band.reshape(1).astype(jnp.int32)
    flat = (blocks, slab_width * rows_y, rows_z)
    big = flat[0] * flat[1] * flat[2]
    slab = jax.ShapeDtypeStruct(flat, F32)
    field = jax.ShapeDtypeStruct(orbitals.shape, F32)
    tile = jax.ShapeDtypeStruct((8, 128), F32)

    def inner_part(block, *sums):
        return call(
            inner_kernel,
            (field, *sums),
            specs=[VMEM] * 2,
            flops=60 * big,
            bytes_moved=8 * big,
        )(block, potential)

    own = orbitals.reshape(flat)
    quarters = [own[2 * k : 2 * k + 2] for k in range(4)]
    arrived = [
        lax.ppermute(quarters[k], "band", [(0, 2 * k), (1, 2 * k + 1)]) for k in (1, 3, 2)
    ]
    inner, sums = inner_part(orbitals, tile)
    arrived, inner, sums = lax.optimization_barrier((arrived, inner, sums))
    piece = jnp.where(band < 2, quarters[0], 0.0)
    for part in arrived:
        piece = piece + part
    left, right = neighbours(own)
    crossed = lax.ppermute(piece, "band", [(y, y + RING) for y in range(RING)])
    piece = jnp.where(band < RING, piece, crossed)

    def stage(fresh, imaged, pieces, *sums, guest=None):
        sources = (*pieces, own, *((image,) if imaged else ()), *sums)
        sources += () if guest is None else (guest,)
        return call(
            lambda *refs: stage_kernel(len(pieces), fresh, imaged, guest is not None, *refs),
            tile if guest is None else jax.ShapeDtypeStruct((domain, 8, 128), F32),
            specs=[VMEM] * len(sources),
            flops=20 * big,
            bytes_moved=10 * big,
        )(*sources)

    pieces = [piece]
    up, down = ring_shift(piece, 1), ring_shift(piece, -1)
    pieces += [up, down]
    up, down = ring_shift(up, 1), ring_shift(down, -1)
    sums = stage(range(6), (), pieces, sums)
    down, sums = lax.optimization_barrier((down, sums))
    pieces += [up, down]
    up, down = ring_shift(up, 1), ring_shift(down, -1)
    sums = stage(range(6, 10), (), pieces, sums)
    image, image_sums = call(
        image_kernel, (slab, tile), specs=[VMEM] * 4, flops=50 * big, bytes_moved=20 * big
    )(own, inner.reshape(flat), left, right)
    down, sums, image, image_sums = lax.optimization_barrier((down, sums, image, image_sums))
    pieces += [up, down]
    up, down = ring_shift(up[:1], 1), ring_shift(down[1:], -1)
    sums = stage(range(10, 14), range(14), pieces, sums, image_sums)
    guest = lax.ppermute(sums, "band", [(0, RING), (1, RING + 1)])
    pieces += [up, down]
    sums = stage(range(14, 16), range(14, 16), pieces, sums, guest=guest)
    sums = domain_parts(sums)
    basis, weights, gram, shared = call(
        lambda *refs: combine_kernel(cells_total, *refs),
        (slab, tile, tile, jax.ShapeDtypeStruct((RING, 8, 128), F32)),
        scratch=[pltpu.VMEM((24, 8, 128), F32)],
        specs=[SMEM] + [VMEM] * 11,
        flops=48 * big,
        bytes_moved=16 * big,
    )(band_word, sums, *pieces, own)
    left, right = neighbours(basis)
    own_sums = shared[0]
    rings = [list(range(RING)), list(range(RING, bands))]
    shared = lax.all_to_all(shared, "band", 0, 0, axis_index_groups=rings)
    inner = inner_part(basis.reshape(orbitals.shape))[0].reshape(flat)
    splat = call(
        coeff_kernel, jax.ShapeDtypeStruct((8, 8, 128), F32), specs=[SMEM] + [VMEM] * 4
    )(band_word, weights, gram, own_sums, shared)
    residual = call(
        residual_kernel, slab, specs=[VMEM] * 5, flops=30 * big, bytes_moved=20 * big
    )(basis, inner, left, right, splat)
    return (basis.reshape(orbitals.shape), residual.reshape(orbitals.shape))


def solution(mesh):
    return jax.shard_map(
        local,
        mesh=mesh,
        in_specs=(P("band", "domain", None, None), P("domain", None, None)),
        out_specs=(P("band", "domain", None, None), P("band", "domain", None, None)),
        check_vma=False,
    )
```

```python
import jax
import jax.numpy as jnp
from jax import lax
from jax.experimental import pallas as pl
from jax.experimental.pallas import tpu as pltpu
from jax.sharding import PartitionSpec as P

stencil_weights = (-205.0 / 72.0, 8.0 / 5.0, -1.0 / 5.0, 8.0 / 315.0, -1.0 / 560.0)
BLK = 8
RING = 8
F32 = jnp.float32
VMEM = pl.BlockSpec(memory_space=pltpu.VMEM)
SMEM = pl.BlockSpec(memory_space=pltpu.SMEM)


def call(kernel, outs, scratch=(), specs=None, flops=0, bytes_moved=0):
    return pl.pallas_call(
        kernel,
        out_shape=outs,
        in_specs=specs,
        out_specs=jax.tree.map(lambda _: VMEM, outs),
        scratch_shapes=scratch,
        compiler_params=pltpu.CompilerParams(vmem_limit_bytes=32 * 1024 * 1024),
        cost_estimate=pl.CostEstimate(flops=flops, bytes_accessed=bytes_moved, transcendentals=0),
    )


def lanes():
    return lax.broadcasted_iota(jnp.int32, (8, 128), 1)


def subs():
    return lax.broadcasted_iota(jnp.int32, (8, 128), 0)


def pair_sums(jobs, load, chunks):
    lane = lanes()
    result = jnp.zeros((8, 128), F32)
    zero_row = jnp.zeros((1, 128), F32)
    for pairs in jobs:
        used = sorted({n for pair in pairs for n in pair})

        def body(c, sums, pairs=pairs, used=used):
            for step in range(4):
                rows = {n: load[n](4 * c + step) for n in used}
                sums = tuple(s + rows[q] * rows[r] for s, (q, r) in zip(sums, pairs))
            return sums

        zero = jnp.zeros((8, 128), F32)
        sums = lax.fori_loop(0, chunks // 4, body, (zero,) * len(pairs))
        columns = {}
        for s, (q, r) in zip(sums, pairs):
            rows = columns.setdefault(32 * (r // 8) + q, [zero_row] * 8)
            rows[r % 8] = jnp.sum(s, axis=0, keepdims=True)
        for place, rows in columns.items():
            column = jnp.sum(jnp.concatenate(rows, axis=0), axis=1, keepdims=True)
            result = result + jnp.where(lane == place, column, 0.0)
    return result


def loader(ref, index):
    return lambda c: ref[index, pl.ds(pl.multiple_of(c * 8, 8), 8), :]


def move(tile, source, target):
    lane = lanes()
    if source != target:
        tile = pltpu.roll(tile, (target - source) % 128, 1)
    return jnp.where((lane >= target) & (lane < target + 8), tile, 0.0)


def spread_lane(tile, k):
    return jnp.broadcast_to(tile[:, k : k + 1], (8, 128))


def rows_of(refs):
    return [(r, i) for r in refs for i in range(r.shape[0])]


def unpacked(sums):
    lane = lanes()
    parts = [sums] + [pltpu.roll(sums, 128 - 32 * n, 1) for n in (1, 2)]
    return [jnp.where(lane < 32, part, 0.0) for part in parts]


def tall(tiles):
    return jnp.concatenate(tiles + [jnp.zeros((128 - 8 * len(tiles), 128), F32)], axis=0)


OWN = list(range(16, 24))
IMAGE = list(range(24, 32))


def split(pairs, size=36):
    if not pairs:
        return []
    count = -(-len(pairs) // size)
    size = -(-len(pairs) // count)
    return [pairs[n : n + size] for n in range(0, len(pairs), size)]


def stage_kernel(parts, fresh, imaged, last, *refs):
    out = refs[-1]
    pieces, refs = refs[:parts], refs[parts:-1]
    own, image, before = (refs[0], refs[1], refs[2:]) if imaged else (refs[0], None, refs[1:])
    chunks = own.shape[1] // 8
    load = {n: loader(r, i) for n, (r, i) in enumerate(rows_of(pieces))}
    load |= {n: loader(own, n - 16) for n in OWN}
    if imaged:
        load |= {n: loader(image, n - 24) for n in IMAGE}
    jobs = split([(q, r) for q in OWN for r in fresh])
    jobs += split([(q, r) for q in fresh for r in range(q + 1)])
    jobs += split([(q, r) for q in IMAGE for r in imaged])
    total = pair_sums(jobs, load, chunks)
    for part in before:
        total = total + part[...]
    if last:
        for n in range(out.shape[0]):
            out[n] = total
    else:
        out[...] = total


def total_kernel(cells_total, parts_ref, out):
    out[...] = jnp.sum(parts_ref[...], axis=0) / cells_total


def combine_kernel(band_ref, sums_ref, *refs):
    *pieces, own, out, weights_ref, gram_ref, splat = refs
    band = band_ref[0]
    lane, sub = lanes(), subs()
    tiles = unpacked(sums_ref[...])
    turned = jnp.transpose(tall(tiles))
    w0, w1, w2 = (
        jnp.where(lane < 24, tile + jnp.where(lane == sub + 8 * n, 0.0, turned[8 * n : 8 * n + 8]), 0.0)
        for n, tile in enumerate(tiles)
    )
    later = band >= 2
    second = band == 1

    def taken(position):
        place = position & 7
        return later | (second & (place >= 2) & (place <= 5))

    row_in = taken(sub)
    lane_in = (lane >= 16) | taken(lane)
    kept = row_in & lane_in
    w0 = jnp.where(kept, w0, jnp.where(lane == sub, 1.0, 0.0))
    w1 = jnp.where(kept, w1, jnp.where(lane == 8 + sub, 1.0, 0.0))
    w0 = w0 + jnp.where(lane == 24 + sub, 1.0, 0.0)
    w1 = w1 + jnp.where(lane == 32 + sub, 1.0, 0.0)
    w2 = jnp.where(lane_in, w2, 0.0) + jnp.where(lane == 40 + sub, 1.0, 0.0)
    tiles = [w0, w1, w2]
    for k in range(16):
        v, s = divmod(k, 8)
        row = tiles[v][s : s + 1, :]
        row = row / jnp.broadcast_to(row[:, k : k + 1], (1, 128))
        row = jnp.broadcast_to(row, (8, 128))
        for u in range(v, 3):
            column = spread_lane(tiles[u], k)
            if u == v:
                column = jnp.where(sub > s, column, 0.0)
            tiles[u] = tiles[u] - column * row
    plain = tiles[2]
    scaled = plain
    for k in range(8):
        row = scaled[k : k + 1, :]
        row = row / jnp.broadcast_to(row[:, 16 + k : 17 + k], (1, 128))
        column = jnp.where(sub > k, spread_lane(scaled, 16 + k), 0.0)
        scaled = scaled - column * jnp.broadcast_to(row, (8, 128))
    pivots = jnp.sum(jnp.where(lane == 16 + sub, scaled, 0.0), axis=1, keepdims=True)
    scaled = scaled / jnp.sqrt(jnp.broadcast_to(pivots, (8, 128)))
    weights = jnp.where(later, plain, scaled)
    weights_ref[...] = weights
    gram_ref[...] = jnp.where(later, move(plain, 16, 0), jnp.where(lane == sub, 1.0, 0.0))
    for c in range(24):
        splat[c] = spread_lane(weights, 24 + c)
    rows = rows_of(pieces) + [(own, i) for i in range(BLK)]

    def body(c, carry):
        part = pl.ds(pl.multiple_of(c * 16, 16), 16)
        inputs = [r[i, part, :] for r, i in rows]
        for i in range(BLK):
            total = splat[0, pl.ds(i, 1), :] * inputs[0]
            for n in range(1, 24):
                total = total + splat[n, pl.ds(i, 1), :] * inputs[n]
            out[i, part, :] = total
        return carry

    lax.fori_loop(0, own.shape[1] // 16, body, 0)


def inner_kernel(f_ref, v_ref, out, *sums):
    def body(i, carry):
        layers = [f_ref[i, x] for x in range(4)]
        for x in range(4):
            here = layers[x]
            total = 3.0 * stencil_weights[0] * here
            for offset in range(1, 5):
                beside = pltpu.roll(here, offset, 0) + pltpu.roll(here, 64 - offset, 0)
                beside = beside + pltpu.roll(here, offset, 1) + pltpu.roll(here, 128 - offset, 1)
                if x + offset < 4:
                    beside = beside + layers[x + offset]
                if x - offset >= 0:
                    beside = beside + layers[x - offset]
                total = total + stencil_weights[offset] * beside
            out[i, x] = -0.5 * total + v_ref[x] * here
        return carry

    lax.fori_loop(0, BLK, body, 0)
    if sums:

        def row(i):
            return lambda c: f_ref[i, c // 8, pl.ds(pl.multiple_of((c % 8) * 8, 8), 8), :]

        load = {n: row(n - 16) for n in OWN}
        sums[0][...] = pair_sums([[(q, r) for q in OWN for r in range(16, q + 1)]], load, 32)


def edged(inner, x, left, right):
    total = None
    for offset in range(1, 5):
        if x + offset >= 4:
            term = stencil_weights[offset] * right(x + offset - 4)
            total = term if total is None else total + term
        if x - offset < 0:
            term = stencil_weights[offset] * left(x - offset + 4)
            total = term if total is None else total + term
    return inner - 0.5 * total


def image_kernel(own, inner, left, right, out, sums):
    def body(i, carry):
        for x in range(4):
            part = pl.ds(64 * x, 64)
            out[i, part, :] = edged(
                inner[i, part, :],
                x,
                lambda n: left[i, pl.ds(64 * n, 64), :],
                lambda n: right[i, pl.ds(64 * n, 64), :],
            )
        return carry

    lax.fori_loop(0, BLK, body, 0)
    load = {n: loader(own, n - 16) for n in OWN}
    load |= {n: loader(out, n - 24) for n in IMAGE}
    jobs = split([(q, r) for q in IMAGE for r in OWN], 32)
    sums[...] = pair_sums(jobs, load, own.shape[1] // 8)


def dot(left, right, turn_left=False, turn_right=False):
    dims = (((0 if turn_left else 1,), (1 if turn_right else 0,)), ((), ()))
    return lax.dot_general(
        left, right, dims, precision=lax.Precision.HIGHEST, preferred_element_type=F32
    )


def places(y, home=None):
    row = lax.broadcasted_iota(jnp.int32, (128, 128), 0)
    lane = lax.broadcasted_iota(jnp.int32, (128, 128), 1)
    distance = (row + 2) >> 2
    distance = jnp.where(((row + 2) & 2) == 0, -distance, distance)
    piece = (y + distance) & 7
    target = (piece & 1) * 8 + (piece >> 1) * 2 + (row & 1)
    if home is None:
        target = jnp.where(row < 16, target, row)
    else:
        target = jnp.where((piece & 1) == home, -1, target)
        target = jnp.where(row < 16, target, row - 16 + 8 * home)
    return jnp.where((lane == target) & (row < 24), 1.0, 0.0)


def coeff_kernel(band_ref, weights_ref, gram_ref, own_ref, shared_ref, out):
    lane, sub = lanes(), subs()
    wide = lax.broadcasted_iota(jnp.int32, (128, 128), 1)
    row = lax.broadcasted_iota(jnp.int32, (128, 128), 0)
    place = places(band_ref[0] & 7)
    weights = jnp.where(lane < 24, pltpu.roll(weights_ref[...], 104, 1), 0.0)
    weights = dot(weights, place)

    def image_columns(matrix, place, source, target):
        columns = dot(place, matrix, turn_left=True)
        columns = pltpu.roll(columns, (target - source) % 128, 1)
        return jnp.where((wide >= target) & (wide < target + 8), columns, 0.0)

    def visiting(n):
        return image_columns(tall(unpacked(shared_ref[n])), places(n, n), 24, 8 * n)

    block0, block1 = visiting(0), visiting(1)
    block = image_columns(tall(unpacked(own_ref[...])), place, 24, 16)
    half = dot(weights, block0 + block1 + block)
    half = half + dot(weights, jnp.where(row < 16, block, 0.0), turn_right=True)
    theta = dot(half, tall([weights]), turn_right=True)
    work = gram_ref[...] + move(theta, 0, 8)
    for k in range(8):
        line = work[k : k + 1, :]
        line = jnp.broadcast_to(line / jnp.broadcast_to(line[:, k : k + 1], (1, 128)), (8, 128))
        work = jnp.where(sub == k, line, work - spread_lane(work, k) * line)
    for j in range(8):
        out[j] = spread_lane(work, 8 + j)


def residual_kernel(f_ref, inner_ref, left_ref, right_ref, splat, out):
    def body(c, carry):
        def part(x):
            return pl.ds(pl.multiple_of(64 * x + 8 * c, 8), 8)

        for x in range(4):
            inputs = [f_ref[i, part(x), :] for i in range(BLK)]
            for j in range(BLK):
                total = edged(
                    inner_ref[j, part(x), :],
                    x,
                    lambda n: left_ref[j, part(n), :],
                    lambda n: right_ref[j, part(n), :],
                )
                for i in range(BLK):
                    total = total - splat[j, pl.ds(i, 1), :] * inputs[i]
                out[j, part(x), :] = total
        return carry

    lax.fori_loop(0, 8, body, 0)


def domain_parts(copies):
    return lax.all_to_all(copies, "domain", 0, 0)


def ring_shift(block, step):
    pairs = [(z * RING + y, z * RING + (y + step) % RING) for z in range(2) for y in range(RING)]
    return lax.ppermute(block, "band", pairs)


def neighbours(block):
    count = lax.axis_size("domain")
    left = lax.ppermute(block, "domain", [(i, (i + 1) % count) for i in range(count)])
    right = lax.ppermute(block, "domain", [((i + 1) % count, i) for i in range(count)])
    return left, right


def local(orbitals, potential):
    blocks, slab_width, rows_y, rows_z = orbitals.shape
    domain, bands = lax.axis_size("domain"), lax.axis_size("band")
    cells_total = float(slab_width * rows_y * rows_z * domain)
    band = lax.axis_index("band")
    band_word = band.reshape(1).astype(jnp.int32)
    flat = (blocks, slab_width * rows_y, rows_z)
    big = flat[0] * flat[1] * flat[2]
    slab = jax.ShapeDtypeStruct(flat, F32)
    field = jax.ShapeDtypeStruct(orbitals.shape, F32)
    tile = jax.ShapeDtypeStruct((8, 128), F32)

    def inner_part(block, *sums):
        return call(
            inner_kernel,
            (field, *sums),
            specs=[VMEM] * 2,
            flops=60 * big,
            bytes_moved=8 * big,
        )(block, potential)

    own = orbitals.reshape(flat)
    quarters = [own[2 * k : 2 * k + 2] for k in range(4)]
    arrived = [
        lax.ppermute(quarters[k], "band", [(0, 2 * k), (1, 2 * k + 1)]) for k in (1, 3, 2)
    ]
    inner, sums = inner_part(orbitals, tile)
    arrived, inner, sums = lax.optimization_barrier((arrived, inner, sums))
    piece = jnp.where(band < 2, quarters[0], 0.0)
    for part in arrived:
        piece = piece + part
    left, right = neighbours(own)
    crossed = lax.ppermute(piece, "band", [(y, y + RING) for y in range(RING)])
    piece = jnp.where(band < RING, piece, crossed)

    def stage(fresh, imaged, pieces, *sums, last=False):
        sources = (*pieces, own, *((image,) if imaged else ()), *sums)
        return call(
            lambda *refs: stage_kernel(len(pieces), fresh, imaged, last, *refs),
            jax.ShapeDtypeStruct((domain, 8, 128), F32) if last else tile,
            specs=[VMEM] * len(sources),
            flops=20 * big,
            bytes_moved=10 * big,
        )(*sources)

    pieces = [piece]
    up, down = ring_shift(piece, 1), ring_shift(piece, -1)
    pieces += [up, down]
    up, down = ring_shift(up, 1), ring_shift(down, -1)
    sums = stage(range(6), (), pieces, sums)
    down, sums = lax.optimization_barrier((down, sums))
    pieces += [up, down]
    up, down = ring_shift(up, 1), ring_shift(down, -1)
    sums = stage(range(6, 10), (), pieces, sums)
    image, image_sums = call(
        image_kernel, (slab, tile), specs=[VMEM] * 4, flops=50 * big, bytes_moved=20 * big
    )(own, inner.reshape(flat), left, right)
    down, sums, image, image_sums = lax.optimization_barrier((down, sums, image, image_sums))
    pieces += [up, down]
    up, down = ring_shift(up[:1], 1), ring_shift(down[1:], -1)
    sums = stage(range(10, 14), range(14), pieces, sums, image_sums)
    pieces += [up, down]
    sums = stage(range(14, 16), range(14, 16), pieces, sums, last=True)
    sums = call(
        lambda *refs: total_kernel(cells_total, *refs),
        tile,
        specs=[VMEM],
        flops=40 * 1024,
        bytes_moved=160 * 1024,
    )(domain_parts(sums))
    guest = lax.ppermute(sums, "band", [(0, RING), (1, RING + 1)])
    basis, weights, gram = call(
        combine_kernel,
        (slab, tile, tile),
        scratch=[pltpu.VMEM((24, 8, 128), F32)],
        specs=[SMEM] + [VMEM] * 11,
        flops=48 * big,
        bytes_moved=16 * big,
    )(band_word, sums, *pieces, own)
    basis, guest = lax.optimization_barrier((basis, guest))
    left, right = neighbours(basis)
    shared = jnp.where((band == RING) | (band == RING + 1), guest, sums)
    shared = jnp.broadcast_to(shared, (RING, 8, 128))
    rings = [list(range(RING)), list(range(RING, bands))]
    shared = lax.all_to_all(shared, "band", 0, 0, axis_index_groups=rings)
    inner = inner_part(basis.reshape(orbitals.shape))[0].reshape(flat)
    splat = call(
        coeff_kernel, jax.ShapeDtypeStruct((8, 8, 128), F32), specs=[SMEM] + [VMEM] * 4
    )(band_word, weights, gram, sums, shared)
    residual = call(
        residual_kernel, slab, specs=[VMEM] * 5, flops=30 * big, bytes_moved=20 * big
    )(basis, inner, left, right, splat)
    return (basis.reshape(orbitals.shape), residual.reshape(orbitals.shape))


def solution(mesh):
    return jax.shard_map(
        local,
        mesh=mesh,
        in_specs=(P("band", "domain", None, None), P("domain", None, None)),
        out_specs=(P("band", "domain", None, None), P("band", "domain", None, None)),
        check_vma=False,
    )
```

```python
import jax
import jax.numpy as jnp
from jax import lax
from jax.experimental import pallas as pl
from jax.experimental.pallas import tpu as pltpu
from jax.sharding import PartitionSpec as P

stencil_weights = (-205.0 / 72.0, 8.0 / 5.0, -1.0 / 5.0, 8.0 / 315.0, -1.0 / 560.0)
BLK = 8
RING = 8
F32 = jnp.float32
VMEM = pl.BlockSpec(memory_space=pltpu.VMEM)
SMEM = pl.BlockSpec(memory_space=pltpu.SMEM)


def call(kernel, outs, scratch=(), specs=None, flops=0, bytes_moved=0):
    return pl.pallas_call(
        kernel,
        out_shape=outs,
        in_specs=specs,
        out_specs=jax.tree.map(lambda _: VMEM, outs),
        scratch_shapes=scratch,
        compiler_params=pltpu.CompilerParams(vmem_limit_bytes=32 * 1024 * 1024),
        cost_estimate=pl.CostEstimate(flops=flops, bytes_accessed=bytes_moved, transcendentals=0),
    )


def lanes():
    return lax.broadcasted_iota(jnp.int32, (8, 128), 1)


def subs():
    return lax.broadcasted_iota(jnp.int32, (8, 128), 0)


def pair_sums(jobs, load, chunks):
    lane = lanes()
    result = jnp.zeros((8, 128), F32)
    zero_row = jnp.zeros((1, 128), F32)
    for pairs in jobs:
        used = sorted({n for pair in pairs for n in pair})

        def body(c, sums, pairs=pairs, used=used):
            for step in range(4):
                rows = {n: load[n](4 * c + step) for n in used}
                sums = tuple(s + rows[q] * rows[r] for s, (q, r) in zip(sums, pairs))
            return sums

        zero = jnp.zeros((8, 128), F32)
        sums = lax.fori_loop(0, chunks // 4, body, (zero,) * len(pairs))
        columns = {}
        for s, (q, r) in zip(sums, pairs):
            rows = columns.setdefault(32 * (r // 8) + q, [zero_row] * 8)
            rows[r % 8] = jnp.sum(s, axis=0, keepdims=True)
        for place, rows in columns.items():
            column = jnp.sum(jnp.concatenate(rows, axis=0), axis=1, keepdims=True)
            result = result + jnp.where(lane == place, column, 0.0)
    return result


def loader(ref, index):
    return lambda c: ref[index, pl.ds(pl.multiple_of(c * 8, 8), 8), :]


def move(tile, source, target):
    lane = lanes()
    if source != target:
        tile = pltpu.roll(tile, (target - source) % 128, 1)
    return jnp.where((lane >= target) & (lane < target + 8), tile, 0.0)


def spread_lane(tile, k):
    return jnp.broadcast_to(tile[:, k : k + 1], (8, 128))


def rows_of(refs):
    return [(r, i) for r in refs for i in range(r.shape[0])]


def unpacked(sums):
    lane = lanes()
    parts = [sums] + [pltpu.roll(sums, 128 - 32 * n, 1) for n in (1, 2)]
    return [jnp.where(lane < 32, part, 0.0) for part in parts]


def tall(tiles):
    return jnp.concatenate(tiles + [jnp.zeros((128 - 8 * len(tiles), 128), F32)], axis=0)


OWN = list(range(16, 24))
IMAGE = list(range(24, 32))


def split(pairs, size=36):
    if not pairs:
        return []
    count = -(-len(pairs) // size)
    size = -(-len(pairs) // count)
    return [pairs[n : n + size] for n in range(0, len(pairs), size)]


def stage_kernel(parts, fresh, imaged, last, *refs):
    out = refs[-1]
    pieces, refs = refs[:parts], refs[parts:-1]
    own, image, before = (refs[0], refs[1], refs[2:]) if imaged else (refs[0], None, refs[1:])
    chunks = own.shape[1] // 8
    load = {n: loader(r, i) for n, (r, i) in enumerate(rows_of(pieces))}
    load |= {n: loader(own, n - 16) for n in OWN}
    if imaged:
        load |= {n: loader(image, n - 24) for n in IMAGE}
    jobs = split([(q, r) for q in OWN for r in fresh])
    jobs += split([(q, r) for q in fresh for r in range(q + 1)])
    jobs += split([(q, r) for q in IMAGE for r in imaged])
    total = pair_sums(jobs, load, chunks)
    for part in before:
        total = total + part[...]
    if last:
        for n in range(out.shape[0]):
            out[n] = total
    else:
        out[...] = total


def total_kernel(cells_total, parts_ref, out):
    out[...] = jnp.sum(parts_ref[...], axis=0) / cells_total


def combine_kernel(band_ref, sums_ref, *refs):
    *pieces, own, out, weights_ref, gram_ref, splat = refs
    band = band_ref[0]
    lane, sub = lanes(), subs()
    tiles = unpacked(sums_ref[...])
    turned = jnp.transpose(tall(tiles))
    w0, w1, w2 = (
        jnp.where(lane < 24, tile + jnp.where(lane == sub + 8 * n, 0.0, turned[8 * n : 8 * n + 8]), 0.0)
        for n, tile in enumerate(tiles)
    )
    later = band >= 2
    second = band == 1

    def taken(position):
        place = position & 7
        return later | (second & (place >= 2) & (place <= 5))

    row_in = taken(sub)
    lane_in = (lane >= 16) | taken(lane)
    kept = row_in & lane_in
    w0 = jnp.where(kept, w0, jnp.where(lane == sub, 1.0, 0.0))
    w1 = jnp.where(kept, w1, jnp.where(lane == 8 + sub, 1.0, 0.0))
    w0 = w0 + jnp.where(lane == 24 + sub, 1.0, 0.0)
    w1 = w1 + jnp.where(lane == 32 + sub, 1.0, 0.0)
    w2 = jnp.where(lane_in, w2, 0.0) + jnp.where(lane == 40 + sub, 1.0, 0.0)
    tiles = [w0, w1, w2]
    for k in range(16):
        v, s = divmod(k, 8)
        row = tiles[v][s : s + 1, :]
        row = row / jnp.broadcast_to(row[:, k : k + 1], (1, 128))
        row = jnp.broadcast_to(row, (8, 128))
        for u in range(v, 3):
            column = spread_lane(tiles[u], k)
            if u == v:
                column = jnp.where(sub > s, column, 0.0)
            tiles[u] = tiles[u] - column * row
    plain = tiles[2]
    scaled = plain
    for k in range(8):
        row = scaled[k : k + 1, :]
        row = row / jnp.broadcast_to(row[:, 16 + k : 17 + k], (1, 128))
        column = jnp.where(sub > k, spread_lane(scaled, 16 + k), 0.0)
        scaled = scaled - column * jnp.broadcast_to(row, (8, 128))
    pivots = jnp.sum(jnp.where(lane == 16 + sub, scaled, 0.0), axis=1, keepdims=True)
    scaled = scaled / jnp.sqrt(jnp.broadcast_to(pivots, (8, 128)))
    weights = jnp.where(later, plain, scaled)
    weights_ref[...] = weights
    gram_ref[...] = jnp.where(later, move(plain, 16, 0), jnp.where(lane == sub, 1.0, 0.0))
    for c in range(24):
        splat[c] = spread_lane(weights, 24 + c)
    rows = rows_of(pieces) + [(own, i) for i in range(BLK)]

    def body(c, carry):
        part = pl.ds(pl.multiple_of(c * 16, 16), 16)
        inputs = [r[i, part, :] for r, i in rows]
        for i in range(BLK):
            total = splat[0, pl.ds(i, 1), :] * inputs[0]
            for n in range(1, 24):
                total = total + splat[n, pl.ds(i, 1), :] * inputs[n]
            out[i, part, :] = total
        return carry

    lax.fori_loop(0, own.shape[1] // 16, body, 0)


def inner_kernel(f_ref, v_ref, out, *sums):
    def body(i, carry):
        layers = [f_ref[i, x] for x in range(4)]
        for x in range(4):
            here = layers[x]
            total = 3.0 * stencil_weights[0] * here
            for offset in range(1, 5):
                beside = pltpu.roll(here, offset, 0) + pltpu.roll(here, 64 - offset, 0)
                beside = beside + pltpu.roll(here, offset, 1) + pltpu.roll(here, 128 - offset, 1)
                if x + offset < 4:
                    beside = beside + layers[x + offset]
                if x - offset >= 0:
                    beside = beside + layers[x - offset]
                total = total + stencil_weights[offset] * beside
            out[i, x] = -0.5 * total + v_ref[x] * here
        return carry

    lax.fori_loop(0, BLK, body, 0)
    if sums:

        def row(i):
            return lambda c: f_ref[i, c // 8, pl.ds(pl.multiple_of((c % 8) * 8, 8), 8), :]

        load = {n: row(n - 16) for n in OWN}
        sums[0][...] = pair_sums([[(q, r) for q in OWN for r in range(16, q + 1)]], load, 32)


def edged(inner, x, left, right):
    total = None
    for offset in range(1, 5):
        if x + offset >= 4:
            term = stencil_weights[offset] * right(x + offset - 4)
            total = term if total is None else total + term
        if x - offset < 0:
            term = stencil_weights[offset] * left(x - offset + 4)
            total = term if total is None else total + term
    return inner - 0.5 * total


def image_kernel(own, inner, left, right, out, sums):
    def body(i, carry):
        for x in range(4):
            part = pl.ds(64 * x, 64)
            out[i, part, :] = edged(
                inner[i, part, :],
                x,
                lambda n: left[i, pl.ds(64 * n, 64), :],
                lambda n: right[i, pl.ds(64 * n, 64), :],
            )
        return carry

    lax.fori_loop(0, BLK, body, 0)
    load = {n: loader(own, n - 16) for n in OWN}
    load |= {n: loader(out, n - 24) for n in IMAGE}
    jobs = split([(q, r) for q in IMAGE for r in OWN], 32)
    sums[...] = pair_sums(jobs, load, own.shape[1] // 8)


def dot(left, right, turn_left=False, turn_right=False):
    dims = (((0 if turn_left else 1,), (1 if turn_right else 0,)), ((), ()))
    return lax.dot_general(
        left, right, dims, precision=lax.Precision.HIGHEST, preferred_element_type=F32
    )


def places(y, home=None):
    row = lax.broadcasted_iota(jnp.int32, (128, 128), 0)
    lane = lax.broadcasted_iota(jnp.int32, (128, 128), 1)
    distance = (row + 2) >> 2
    distance = jnp.where(((row + 2) & 2) == 0, -distance, distance)
    piece = (y + distance) & 7
    target = (piece & 1) * 8 + (piece >> 1) * 2 + (row & 1)
    if home is None:
        target = jnp.where(row < 16, target, row)
    else:
        target = jnp.where((piece & 1) == home, -1, target)
        target = jnp.where(row < 16, target, row - 16 + 8 * home)
    return jnp.where((lane == target) & (row < 24), 1.0, 0.0)


def coeff_kernel(band_ref, weights_ref, gram_ref, own_ref, shared_ref, out):
    lane, sub = lanes(), subs()
    wide = lax.broadcasted_iota(jnp.int32, (128, 128), 1)
    row = lax.broadcasted_iota(jnp.int32, (128, 128), 0)
    place = places(band_ref[0] & 7)
    weights = jnp.where(lane < 24, pltpu.roll(weights_ref[...], 104, 1), 0.0)
    weights = dot(weights, place)

    def image_columns(matrix, place, source, target):
        columns = dot(place, matrix, turn_left=True)
        columns = pltpu.roll(columns, (target - source) % 128, 1)
        return jnp.where((wide >= target) & (wide < target + 8), columns, 0.0)

    def visiting(n):
        return image_columns(tall(unpacked(shared_ref[n])), places(n, n), 24, 8 * n)

    block0, block1 = visiting(0), visiting(1)
    block = image_columns(tall(unpacked(own_ref[...])), place, 24, 16)
    half = dot(weights, block0 + block1 + block)
    half = half + dot(weights, jnp.where(row < 16, block, 0.0), turn_right=True)
    theta = dot(half, tall([weights]), turn_right=True)
    work = gram_ref[...] + move(theta, 0, 8)
    for k in range(8):
        line = work[k : k + 1, :]
        line = jnp.broadcast_to(line / jnp.broadcast_to(line[:, k : k + 1], (1, 128)), (8, 128))
        work = jnp.where(sub == k, line, work - spread_lane(work, k) * line)
    for j in range(8):
        out[j] = spread_lane(work, 8 + j)


def residual_kernel(f_ref, inner_ref, left_ref, right_ref, splat, out):
    def body(c, carry):
        def part(x):
            return pl.ds(pl.multiple_of(64 * x + 8 * c, 8), 8)

        for x in range(4):
            inputs = [f_ref[i, part(x), :] for i in range(BLK)]
            for j in range(BLK):
                total = edged(
                    inner_ref[j, part(x), :],
                    x,
                    lambda n: left_ref[j, part(n), :],
                    lambda n: right_ref[j, part(n), :],
                )
                for i in range(BLK):
                    total = total - splat[j, pl.ds(i, 1), :] * inputs[i]
                out[j, part(x), :] = total
        return carry

    lax.fori_loop(0, 8, body, 0)


def domain_parts(copies):
    return lax.all_to_all(copies, "domain", 0, 0)


def ring_shift(block, step):
    pairs = [(z * RING + y, z * RING + (y + step) % RING) for z in range(2) for y in range(RING)]
    return lax.ppermute(block, "band", pairs)


def neighbours(block):
    count = lax.axis_size("domain")
    left = lax.ppermute(block, "domain", [(i, (i + 1) % count) for i in range(count)])
    right = lax.ppermute(block, "domain", [((i + 1) % count, i) for i in range(count)])
    return left, right


def local(orbitals, potential):
    blocks, slab_width, rows_y, rows_z = orbitals.shape
    domain, bands = lax.axis_size("domain"), lax.axis_size("band")
    cells_total = float(slab_width * rows_y * rows_z * domain)
    band = lax.axis_index("band")
    band_word = band.reshape(1).astype(jnp.int32)
    flat = (blocks, slab_width * rows_y, rows_z)
    big = flat[0] * flat[1] * flat[2]
    slab = jax.ShapeDtypeStruct(flat, F32)
    field = jax.ShapeDtypeStruct(orbitals.shape, F32)
    tile = jax.ShapeDtypeStruct((8, 128), F32)

    def inner_part(block, *sums):
        return call(
            inner_kernel,
            (field, *sums),
            specs=[VMEM] * 2,
            flops=60 * big,
            bytes_moved=8 * big,
        )(block, potential)

    own = orbitals.reshape(flat)
    quarters = [own[2 * k : 2 * k + 2] for k in range(4)]
    arrived = [
        lax.ppermute(quarters[k], "band", [(0, 2 * k), (1, 2 * k + 1)]) for k in (1, 3, 2)
    ]
    inner, sums = inner_part(orbitals, tile)
    arrived, inner, sums = lax.optimization_barrier((arrived, inner, sums))
    piece = jnp.where(band < 2, quarters[0], 0.0)
    for part in arrived:
        piece = piece + part
    left, right = neighbours(own)
    crossed = lax.ppermute(piece, "band", [(y, y + RING) for y in range(RING)])
    piece = jnp.where(band < RING, piece, crossed)

    def stage(fresh, imaged, pieces, *sums, last=False):
        sources = (*pieces, own, *((image,) if imaged else ()), *sums)
        return call(
            lambda *refs: stage_kernel(len(pieces), fresh, imaged, last, *refs),
            jax.ShapeDtypeStruct((domain, 8, 128), F32) if last else tile,
            specs=[VMEM] * len(sources),
            flops=20 * big,
            bytes_moved=10 * big,
        )(*sources)

    pieces = [piece]
    up, down = ring_shift(piece, 1), ring_shift(piece, -1)
    pieces += [up, down]
    up, down = ring_shift(up, 1), ring_shift(down, -1)
    sums = stage(range(6), (), pieces, sums)
    down, sums = lax.optimization_barrier((down, sums))
    pieces += [up, down]
    up, down = ring_shift(up, 1), ring_shift(down, -1)
    sums = stage(range(6, 10), (), pieces, sums)
    image, image_sums = call(
        image_kernel, (slab, tile), specs=[VMEM] * 4, flops=50 * big, bytes_moved=20 * big
    )(own, inner.reshape(flat), left, right)
    down, sums, image, image_sums = lax.optimization_barrier((down, sums, image, image_sums))
    pieces += [up, down]
    up, down = ring_shift(up[:1], 1), ring_shift(down[1:], -1)
    sums = stage(range(10, 14), range(14), pieces, sums, image_sums)
    pieces += [up, down]
    sums = stage(range(14, 16), range(14, 16), pieces, sums, last=True)
    sums = call(
        lambda *refs: total_kernel(cells_total, *refs),
        tile,
        specs=[VMEM],
        flops=40 * 1024,
        bytes_moved=160 * 1024,
    )(domain_parts(sums))
    basis, weights, gram = call(
        combine_kernel,
        (slab, tile, tile),
        scratch=[pltpu.VMEM((24, 8, 128), F32)],
        specs=[SMEM] + [VMEM] * 11,
        flops=48 * big,
        bytes_moved=16 * big,
    )(band_word, sums, *pieces, own)
    left, right = neighbours(basis)
    sums, weights = lax.optimization_barrier((sums, weights))
    guest = lax.ppermute(sums, "band", [(0, RING), (1, RING + 1)])
    shared = jnp.where((band == RING) | (band == RING + 1), guest, sums)
    shared = jnp.broadcast_to(shared, (RING, 8, 128))
    rings = [list(range(RING)), list(range(RING, bands))]
    shared = lax.all_to_all(shared, "band", 0, 0, axis_index_groups=rings)
    inner = inner_part(basis.reshape(orbitals.shape))[0].reshape(flat)
    splat = call(
        coeff_kernel, jax.ShapeDtypeStruct((8, 8, 128), F32), specs=[SMEM] + [VMEM] * 4
    )(band_word, weights, gram, sums, shared)
    residual = call(
        residual_kernel, slab, specs=[VMEM] * 5, flops=30 * big, bytes_moved=20 * big
    )(basis, inner, left, right, splat)
    return (basis.reshape(orbitals.shape), residual.reshape(orbitals.shape))


def solution(mesh):
    return jax.shard_map(
        local,
        mesh=mesh,
        in_specs=(P("band", "domain", None, None), P("domain", None, None)),
        out_specs=(P("band", "domain", None, None), P("band", "domain", None, None)),
        check_vma=False,
    )
```

```python
import jax
import jax.numpy as jnp
from jax import lax
from jax.experimental import pallas as pl
from jax.experimental.pallas import tpu as pltpu
from jax.sharding import PartitionSpec as P

stencil_weights = (-205.0 / 72.0, 8.0 / 5.0, -1.0 / 5.0, 8.0 / 315.0, -1.0 / 560.0)
BLK = 8
RING = 8
F32 = jnp.float32
VMEM = pl.BlockSpec(memory_space=pltpu.VMEM)
SMEM = pl.BlockSpec(memory_space=pltpu.SMEM)


def call(kernel, outs, scratch=(), specs=None, flops=0, bytes_moved=0):
    return pl.pallas_call(
        kernel,
        out_shape=outs,
        in_specs=specs,
        out_specs=jax.tree.map(lambda _: VMEM, outs),
        scratch_shapes=scratch,
        compiler_params=pltpu.CompilerParams(vmem_limit_bytes=32 * 1024 * 1024),
        cost_estimate=pl.CostEstimate(flops=flops, bytes_accessed=bytes_moved, transcendentals=0),
    )


def lanes():
    return lax.broadcasted_iota(jnp.int32, (8, 128), 1)


def subs():
    return lax.broadcasted_iota(jnp.int32, (8, 128), 0)


def pair_sums(jobs, load, chunks):
    lane = lanes()
    result = jnp.zeros((8, 128), F32)
    zero_row = jnp.zeros((1, 128), F32)
    for pairs in jobs:
        used = sorted({n for pair in pairs for n in pair})

        def body(c, sums, pairs=pairs, used=used):
            for step in range(4):
                rows = {n: load[n](4 * c + step) for n in used}
                sums = tuple(s + rows[q] * rows[r] for s, (q, r) in zip(sums, pairs))
            return sums

        zero = jnp.zeros((8, 128), F32)
        sums = lax.fori_loop(0, chunks // 4, body, (zero,) * len(pairs))
        columns = {}
        for s, (q, r) in zip(sums, pairs):
            rows = columns.setdefault(32 * (r // 8) + q, [zero_row] * 8)
            rows[r % 8] = jnp.sum(s, axis=0, keepdims=True)
        for place, rows in columns.items():
            column = jnp.sum(jnp.concatenate(rows, axis=0), axis=1, keepdims=True)
            result = result + jnp.where(lane == place, column, 0.0)
    return result


def loader(ref, index):
    return lambda c: ref[index, pl.ds(pl.multiple_of(c * 8, 8), 8), :]


def move(tile, source, target):
    lane = lanes()
    if source != target:
        tile = pltpu.roll(tile, (target - source) % 128, 1)
    return jnp.where((lane >= target) & (lane < target + 8), tile, 0.0)


def spread_lane(tile, k):
    return jnp.broadcast_to(tile[:, k : k + 1], (8, 128))


def rows_of(refs):
    return [(r, i) for r in refs for i in range(r.shape[0])]


def unpacked(sums):
    lane = lanes()
    parts = [sums] + [pltpu.roll(sums, 128 - 32 * n, 1) for n in (1, 2)]
    return [jnp.where(lane < 32, part, 0.0) for part in parts]


def tall(tiles):
    return jnp.concatenate(tiles + [jnp.zeros((128 - 8 * len(tiles), 128), F32)], axis=0)


OWN = list(range(16, 24))
IMAGE = list(range(24, 32))


def split(pairs, size=36):
    if not pairs:
        return []
    count = -(-len(pairs) // size)
    size = -(-len(pairs) // count)
    return [pairs[n : n + size] for n in range(0, len(pairs), size)]


def stage_kernel(parts, fresh, imaged, last, *refs):
    out = refs[-1]
    pieces, refs = refs[:parts], refs[parts:-1]
    own, image, before = (refs[0], refs[1], refs[2:]) if imaged else (refs[0], None, refs[1:])
    chunks = own.shape[1] // 8
    load = {n: loader(r, i) for n, (r, i) in enumerate(rows_of(pieces))}
    load |= {n: loader(own, n - 16) for n in OWN}
    if imaged:
        load |= {n: loader(image, n - 24) for n in IMAGE}
    jobs = split([(q, r) for q in OWN for r in fresh])
    jobs += split([(q, r) for q in fresh for r in range(q + 1)])
    jobs += split([(q, r) for q in IMAGE for r in imaged])
    total = pair_sums(jobs, load, chunks)
    for part in before:
        total = total + part[...]
    if last:
        for n in range(out.shape[0]):
            out[n] = total
    else:
        out[...] = total


def total_kernel(cells_total, parts_ref, out):
    out[...] = jnp.sum(parts_ref[...], axis=0) / cells_total


def combine_kernel(band_ref, sums_ref, *refs):
    *pieces, own, out, weights_ref, gram_ref, splat = refs
    band = band_ref[0]
    lane, sub = lanes(), subs()
    tiles = unpacked(sums_ref[...])
    turned = jnp.transpose(tall(tiles))
    w0, w1, w2 = (
        jnp.where(lane < 24, tile + jnp.where(lane == sub + 8 * n, 0.0, turned[8 * n : 8 * n + 8]), 0.0)
        for n, tile in enumerate(tiles)
    )
    later = band >= 2
    second = band == 1

    def taken(position):
        place = position & 7
        return later | (second & (place >= 2) & (place <= 5))

    row_in = taken(sub)
    lane_in = (lane >= 16) | taken(lane)
    kept = row_in & lane_in
    w0 = jnp.where(kept, w0, jnp.where(lane == sub, 1.0, 0.0))
    w1 = jnp.where(kept, w1, jnp.where(lane == 8 + sub, 1.0, 0.0))
    w0 = w0 + jnp.where(lane == 24 + sub, 1.0, 0.0)
    w1 = w1 + jnp.where(lane == 32 + sub, 1.0, 0.0)
    w2 = jnp.where(lane_in, w2, 0.0) + jnp.where(lane == 40 + sub, 1.0, 0.0)
    tiles = [w0, w1, w2]
    for k in range(16):
        v, s = divmod(k, 8)
        row = tiles[v][s : s + 1, :]
        row = row / jnp.broadcast_to(row[:, k : k + 1], (1, 128))
        row = jnp.broadcast_to(row, (8, 128))
        for u in range(v, 3):
            column = spread_lane(tiles[u], k)
            if u == v:
                column = jnp.where(sub > s, column, 0.0)
            tiles[u] = tiles[u] - column * row
    plain = tiles[2]
    scaled = plain
    for k in range(8):
        row = scaled[k : k + 1, :]
        row = row / jnp.broadcast_to(row[:, 16 + k : 17 + k], (1, 128))
        column = jnp.where(sub > k, spread_lane(scaled, 16 + k), 0.0)
        scaled = scaled - column * jnp.broadcast_to(row, (8, 128))
    pivots = jnp.sum(jnp.where(lane == 16 + sub, scaled, 0.0), axis=1, keepdims=True)
    scaled = scaled / jnp.sqrt(jnp.broadcast_to(pivots, (8, 128)))
    weights = jnp.where(later, plain, scaled)
    weights_ref[...] = weights
    gram_ref[...] = jnp.where(later, move(plain, 16, 0), jnp.where(lane == sub, 1.0, 0.0))
    for c in range(24):
        splat[c] = spread_lane(weights, 24 + c)
    rows = rows_of(pieces) + [(own, i) for i in range(BLK)]

    def body(c, carry):
        part = pl.ds(pl.multiple_of(c * 16, 16), 16)
        inputs = [r[i, part, :] for r, i in rows]
        for i in range(BLK):
            total = splat[0, pl.ds(i, 1), :] * inputs[0]
            for n in range(1, 24):
                total = total + splat[n, pl.ds(i, 1), :] * inputs[n]
            out[i, part, :] = total
        return carry

    lax.fori_loop(0, own.shape[1] // 16, body, 0)


def inner_kernel(f_ref, v_ref, out, *sums):
    def body(i, carry):
        layers = [f_ref[i, x] for x in range(4)]
        for x in range(4):
            here = layers[x]
            total = 3.0 * stencil_weights[0] * here
            for offset in range(1, 5):
                beside = pltpu.roll(here, offset, 0) + pltpu.roll(here, 64 - offset, 0)
                beside = beside + pltpu.roll(here, offset, 1) + pltpu.roll(here, 128 - offset, 1)
                if x + offset < 4:
                    beside = beside + layers[x + offset]
                if x - offset >= 0:
                    beside = beside + layers[x - offset]
                total = total + stencil_weights[offset] * beside
            out[i, x] = -0.5 * total + v_ref[x] * here
        return carry

    lax.fori_loop(0, BLK, body, 0)
    if sums:

        def row(i):
            return lambda c: f_ref[i, c // 8, pl.ds(pl.multiple_of((c % 8) * 8, 8), 8), :]

        load = {n: row(n - 16) for n in OWN}
        sums[0][...] = pair_sums([[(q, r) for q in OWN for r in range(16, q + 1)]], load, 32)


def edged(inner, x, left, right):
    total = None
    for offset in range(1, 5):
        if x + offset >= 4:
            term = stencil_weights[offset] * right(x + offset - 4)
            total = term if total is None else total + term
        if x - offset < 0:
            term = stencil_weights[offset] * left(x - offset + 4)
            total = term if total is None else total + term
    return inner - 0.5 * total


def image_kernel(own, inner, left, right, out, sums):
    def body(i, carry):
        for x in range(4):
            part = pl.ds(64 * x, 64)
            out[i, part, :] = edged(
                inner[i, part, :],
                x,
                lambda n: left[i, pl.ds(64 * n, 64), :],
                lambda n: right[i, pl.ds(64 * n, 64), :],
            )
        return carry

    lax.fori_loop(0, BLK, body, 0)
    load = {n: loader(own, n - 16) for n in OWN}
    load |= {n: loader(out, n - 24) for n in IMAGE}
    jobs = split([(q, r) for q in IMAGE for r in OWN], 32)
    sums[...] = pair_sums(jobs, load, own.shape[1] // 8)


def dot(left, right, turn_left=False, turn_right=False):
    dims = (((0 if turn_left else 1,), (1 if turn_right else 0,)), ((), ()))
    return lax.dot_general(
        left, right, dims, precision=lax.Precision.HIGHEST, preferred_element_type=F32
    )


def places(y, home=None):
    row = lax.broadcasted_iota(jnp.int32, (128, 128), 0)
    lane = lax.broadcasted_iota(jnp.int32, (128, 128), 1)
    distance = (row + 2) >> 2
    distance = jnp.where(((row + 2) & 2) == 0, -distance, distance)
    piece = (y + distance) & 7
    target = (piece & 1) * 8 + (piece >> 1) * 2 + (row & 1)
    if home is None:
        target = jnp.where(row < 16, target, row)
    else:
        target = jnp.where((piece & 1) == home, -1, target)
        target = jnp.where(row < 16, target, row - 16 + 8 * home)
    return jnp.where((lane == target) & (row < 24), 1.0, 0.0)


def coeff_kernel(band_ref, weights_ref, gram_ref, own_ref, near_ref, far_ref, out):
    lane, sub = lanes(), subs()
    wide = lax.broadcasted_iota(jnp.int32, (128, 128), 1)
    row = lax.broadcasted_iota(jnp.int32, (128, 128), 0)
    place = places(band_ref[0] & 7)
    weights = jnp.where(lane < 24, pltpu.roll(weights_ref[...], 104, 1), 0.0)
    weights = dot(weights, place)

    def image_columns(matrix, place, source, target):
        columns = dot(place, matrix, turn_left=True)
        columns = pltpu.roll(columns, (target - source) % 128, 1)
        return jnp.where((wide >= target) & (wide < target + 8), columns, 0.0)

    def visiting(n):
        packed = jnp.where(band_ref[0] < RING, near_ref[n], far_ref[n])
        return image_columns(tall(unpacked(packed)), places(n, n), 24, 8 * n)

    block0, block1 = visiting(0), visiting(1)
    block = image_columns(tall(unpacked(own_ref[...])), place, 24, 16)
    half = dot(weights, block0 + block1 + block)
    half = half + dot(weights, jnp.where(row < 16, block, 0.0), turn_right=True)
    theta = dot(half, tall([weights]), turn_right=True)
    work = gram_ref[...] + move(theta, 0, 8)
    for k in range(8):
        line = work[k : k + 1, :]
        line = jnp.broadcast_to(line / jnp.broadcast_to(line[:, k : k + 1], (1, 128)), (8, 128))
        work = jnp.where(sub == k, line, work - spread_lane(work, k) * line)
    for j in range(8):
        out[j] = spread_lane(work, 8 + j)


def residual_kernel(f_ref, inner_ref, left_ref, right_ref, splat, out):
    def body(c, carry):
        def part(x):
            return pl.ds(pl.multiple_of(64 * x + 8 * c, 8), 8)

        for x in range(4):
            inputs = [f_ref[i, part(x), :] for i in range(BLK)]
            for j in range(BLK):
                total = edged(
                    inner_ref[j, part(x), :],
                    x,
                    lambda n: left_ref[j, part(n), :],
                    lambda n: right_ref[j, part(n), :],
                )
                for i in range(BLK):
                    total = total - splat[j, pl.ds(i, 1), :] * inputs[i]
                out[j, part(x), :] = total
        return carry

    lax.fori_loop(0, 8, body, 0)


def domain_parts(copies):
    return lax.all_to_all(copies, "domain", 0, 0)


def ring_shift(block, step):
    pairs = [(z * RING + y, z * RING + (y + step) % RING) for z in range(2) for y in range(RING)]
    return lax.ppermute(block, "band", pairs)


def neighbours(block):
    count = lax.axis_size("domain")
    left = lax.ppermute(block, "domain", [(i, (i + 1) % count) for i in range(count)])
    right = lax.ppermute(block, "domain", [((i + 1) % count, i) for i in range(count)])
    return left, right


def local(orbitals, potential):
    blocks, slab_width, rows_y, rows_z = orbitals.shape
    domain, bands = lax.axis_size("domain"), lax.axis_size("band")
    cells_total = float(slab_width * rows_y * rows_z * domain)
    band = lax.axis_index("band")
    band_word = band.reshape(1).astype(jnp.int32)
    flat = (blocks, slab_width * rows_y, rows_z)
    big = flat[0] * flat[1] * flat[2]
    slab = jax.ShapeDtypeStruct(flat, F32)
    field = jax.ShapeDtypeStruct(orbitals.shape, F32)
    tile = jax.ShapeDtypeStruct((8, 128), F32)

    def inner_part(block, *sums):
        return call(
            inner_kernel,
            (field, *sums),
            specs=[VMEM] * 2,
            flops=60 * big,
            bytes_moved=8 * big,
        )(block, potential)

    own = orbitals.reshape(flat)
    quarters = [own[2 * k : 2 * k + 2] for k in range(4)]
    arrived = [
        lax.ppermute(quarters[k], "band", [(0, 2 * k), (1, 2 * k + 1)]) for k in (1, 3, 2)
    ]
    inner, sums = inner_part(orbitals, tile)
    arrived, inner, sums = lax.optimization_barrier((arrived, inner, sums))
    piece = jnp.where(band < 2, quarters[0], 0.0)
    for part in arrived:
        piece = piece + part
    left, right = neighbours(own)
    crossed = lax.ppermute(piece, "band", [(y, y + RING) for y in range(RING)])
    piece = jnp.where(band < RING, piece, crossed)

    def stage(fresh, imaged, pieces, *sums, last=False):
        sources = (*pieces, own, *((image,) if imaged else ()), *sums)
        return call(
            lambda *refs: stage_kernel(len(pieces), fresh, imaged, last, *refs),
            jax.ShapeDtypeStruct((domain, 8, 128), F32) if last else tile,
            specs=[VMEM] * len(sources),
            flops=20 * big,
            bytes_moved=10 * big,
        )(*sources)

    pieces = [piece]
    up, down = ring_shift(piece, 1), ring_shift(piece, -1)
    pieces += [up, down]
    up, down = ring_shift(up, 1), ring_shift(down, -1)
    sums = stage(range(6), (), pieces, sums)
    down, sums = lax.optimization_barrier((down, sums))
    pieces += [up, down]
    up, down = ring_shift(up, 1), ring_shift(down, -1)
    sums = stage(range(6, 10), (), pieces, sums)
    image, image_sums = call(
        image_kernel, (slab, tile), specs=[VMEM] * 4, flops=50 * big, bytes_moved=20 * big
    )(own, inner.reshape(flat), left, right)
    down, sums, image, image_sums = lax.optimization_barrier((down, sums, image, image_sums))
    pieces += [up, down]
    up, down = ring_shift(up[:1], 1), ring_shift(down[1:], -1)
    sums = stage(range(10, 14), range(14), pieces, sums, image_sums)
    pieces += [up, down]
    sums = stage(range(14, 16), range(14, 16), pieces, sums, last=True)
    sums = call(
        lambda *refs: total_kernel(cells_total, *refs),
        tile,
        specs=[VMEM],
        flops=40 * 1024,
        bytes_moved=160 * 1024,
    )(domain_parts(sums))
    basis, weights, gram = call(
        combine_kernel,
        (slab, tile, tile),
        scratch=[pltpu.VMEM((24, 8, 128), F32)],
        specs=[SMEM] + [VMEM] * 11,
        flops=48 * big,
        bytes_moved=16 * big,
    )(band_word, sums, *pieces, own)
    left, right = neighbours(basis)
    inner = inner_part(basis.reshape(orbitals.shape))[0].reshape(flat)
    rings = [list(range(RING)), list(range(RING, bands))]
    shared, inner = lax.optimization_barrier((sums, inner))
    near = jnp.broadcast_to(shared, (RING, 8, 128))
    near = lax.all_to_all(near, "band", 0, 0, axis_index_groups=rings)
    far = lax.ppermute(near[:2], "band", [(y, y + RING) for y in range(RING)])
    splat = call(
        coeff_kernel, jax.ShapeDtypeStruct((8, 8, 128), F32), specs=[SMEM] + [VMEM] * 5
    )(band_word, weights, gram, sums, near, far)
    residual = call(
        residual_kernel, slab, specs=[VMEM] * 5, flops=30 * big, bytes_moved=20 * big
    )(basis, inner, left, right, splat)
    return (basis.reshape(orbitals.shape), residual.reshape(orbitals.shape))


def solution(mesh):
    return jax.shard_map(
        local,
        mesh=mesh,
        in_specs=(P("band", "domain", None, None), P("domain", None, None)),
        out_specs=(P("band", "domain", None, None), P("band", "domain", None, None)),
        check_vma=False,
    )
```

```python
import jax
import jax.numpy as jnp
from jax import lax
from jax.experimental import pallas as pl
from jax.experimental.pallas import tpu as pltpu
from jax.sharding import PartitionSpec as P

stencil_weights = (-205.0 / 72.0, 8.0 / 5.0, -1.0 / 5.0, 8.0 / 315.0, -1.0 / 560.0)
BLK = 8
RING = 8
F32 = jnp.float32
VMEM = pl.BlockSpec(memory_space=pltpu.VMEM)
SMEM = pl.BlockSpec(memory_space=pltpu.SMEM)


def call(kernel, outs, scratch=(), specs=None, flops=0, bytes_moved=0):
    return pl.pallas_call(
        kernel,
        out_shape=outs,
        in_specs=specs,
        out_specs=jax.tree.map(lambda _: VMEM, outs),
        scratch_shapes=scratch,
        compiler_params=pltpu.CompilerParams(vmem_limit_bytes=32 * 1024 * 1024),
        cost_estimate=pl.CostEstimate(flops=flops, bytes_accessed=bytes_moved, transcendentals=0),
    )


def lanes():
    return lax.broadcasted_iota(jnp.int32, (8, 128), 1)


def subs():
    return lax.broadcasted_iota(jnp.int32, (8, 128), 0)


def pair_sums(jobs, load, chunks):
    lane = lanes()
    result = jnp.zeros((8, 128), F32)
    zero_row = jnp.zeros((1, 128), F32)
    for pairs in jobs:
        used = sorted({n for pair in pairs for n in pair})

        def body(c, sums, pairs=pairs, used=used):
            for step in range(4):
                rows = {n: load[n](4 * c + step) for n in used}
                sums = tuple(s + rows[q] * rows[r] for s, (q, r) in zip(sums, pairs))
            return sums

        zero = jnp.zeros((8, 128), F32)
        sums = lax.fori_loop(0, chunks // 4, body, (zero,) * len(pairs))
        columns = {}
        for s, (q, r) in zip(sums, pairs):
            rows = columns.setdefault(32 * (r // 8) + q, [zero_row] * 8)
            rows[r % 8] = jnp.sum(s, axis=0, keepdims=True)
        for place, rows in columns.items():
            column = jnp.sum(jnp.concatenate(rows, axis=0), axis=1, keepdims=True)
            result = result + jnp.where(lane == place, column, 0.0)
    return result


def loader(ref, index):
    return lambda c: ref[index, pl.ds(pl.multiple_of(c * 8, 8), 8), :]


def move(tile, source, target):
    lane = lanes()
    if source != target:
        tile = pltpu.roll(tile, (target - source) % 128, 1)
    return jnp.where((lane >= target) & (lane < target + 8), tile, 0.0)


def spread_lane(tile, k):
    return jnp.broadcast_to(tile[:, k : k + 1], (8, 128))


def rows_of(refs):
    return [(r, i) for r in refs for i in range(r.shape[0])]


def unpacked(sums):
    lane = lanes()
    parts = [sums] + [pltpu.roll(sums, 128 - 32 * n, 1) for n in (1, 2)]
    return [jnp.where(lane < 32, part, 0.0) for part in parts]


def tall(tiles):
    return jnp.concatenate(tiles + [jnp.zeros((128 - 8 * len(tiles), 128), F32)], axis=0)


OWN = list(range(16, 24))
IMAGE = list(range(24, 32))


def split(pairs, size=36):
    if not pairs:
        return []
    count = -(-len(pairs) // size)
    size = -(-len(pairs) // count)
    return [pairs[n : n + size] for n in range(0, len(pairs), size)]


def stage_kernel(parts, fresh, imaged, last, *refs):
    out = refs[-1]
    pieces, refs = refs[:parts], refs[parts:-1]
    own, image, before = (refs[0], refs[1], refs[2:]) if imaged else (refs[0], None, refs[1:])
    chunks = own.shape[1] // 8
    load = {n: loader(r, i) for n, (r, i) in enumerate(rows_of(pieces))}
    load |= {n: loader(own, n - 16) for n in OWN}
    if imaged:
        load |= {n: loader(image, n - 24) for n in IMAGE}
    jobs = split([(q, r) for q in OWN for r in fresh])
    jobs += split([(q, r) for q in fresh for r in range(q + 1)])
    jobs += split([(q, r) for q in IMAGE for r in imaged])
    total = pair_sums(jobs, load, chunks)
    for part in before:
        total = total + part[...]
    if last:
        for n in range(out.shape[0]):
            out[n] = total
    else:
        out[...] = total


def total_kernel(cells_total, parts_ref, out):
    out[...] = jnp.sum(parts_ref[...], axis=0) / cells_total


def combine_kernel(band_ref, sums_ref, *refs):
    *pieces, own, out, weights_ref, gram_ref, splat = refs
    band = band_ref[0]
    lane, sub = lanes(), subs()
    tiles = unpacked(sums_ref[...])
    turned = jnp.transpose(tall(tiles))
    w0, w1, w2 = (
        jnp.where(lane < 24, tile + jnp.where(lane == sub + 8 * n, 0.0, turned[8 * n : 8 * n + 8]), 0.0)
        for n, tile in enumerate(tiles)
    )
    later = band >= 2
    second = band == 1

    def taken(position):
        place = position & 7
        return later | (second & (place >= 2) & (place <= 5))

    row_in = taken(sub)
    lane_in = (lane >= 16) | taken(lane)
    kept = row_in & lane_in
    w0 = jnp.where(kept, w0, jnp.where(lane == sub, 1.0, 0.0))
    w1 = jnp.where(kept, w1, jnp.where(lane == 8 + sub, 1.0, 0.0))
    w0 = w0 + jnp.where(lane == 24 + sub, 1.0, 0.0)
    w1 = w1 + jnp.where(lane == 32 + sub, 1.0, 0.0)
    w2 = jnp.where(lane_in, w2, 0.0) + jnp.where(lane == 40 + sub, 1.0, 0.0)
    tiles = [w0, w1, w2]
    for k in range(16):
        v, s = divmod(k, 8)
        row = tiles[v][s : s + 1, :]
        row = row / jnp.broadcast_to(row[:, k : k + 1], (1, 128))
        row = jnp.broadcast_to(row, (8, 128))
        for u in range(v, 3):
            column = spread_lane(tiles[u], k)
            if u == v:
                column = jnp.where(sub > s, column, 0.0)
            tiles[u] = tiles[u] - column * row
    plain = tiles[2]
    scaled = plain
    for k in range(8):
        row = scaled[k : k + 1, :]
        row = row / jnp.broadcast_to(row[:, 16 + k : 17 + k], (1, 128))
        column = jnp.where(sub > k, spread_lane(scaled, 16 + k), 0.0)
        scaled = scaled - column * jnp.broadcast_to(row, (8, 128))
    pivots = jnp.sum(jnp.where(lane == 16 + sub, scaled, 0.0), axis=1, keepdims=True)
    scaled = scaled / jnp.sqrt(jnp.broadcast_to(pivots, (8, 128)))
    weights = jnp.where(later, plain, scaled)
    weights_ref[...] = weights
    gram_ref[...] = jnp.where(later, move(plain, 16, 0), jnp.where(lane == sub, 1.0, 0.0))
    for c in range(24):
        splat[c] = spread_lane(weights, 24 + c)
    rows = rows_of(pieces) + [(own, i) for i in range(BLK)]

    def body(c, carry):
        part = pl.ds(pl.multiple_of(c * 16, 16), 16)
        inputs = [r[i, part, :] for r, i in rows]
        for i in range(BLK):
            total = splat[0, pl.ds(i, 1), :] * inputs[0]
            for n in range(1, 24):
                total = total + splat[n, pl.ds(i, 1), :] * inputs[n]
            out[i, part, :] = total
        return carry

    lax.fori_loop(0, own.shape[1] // 16, body, 0)


def inner_kernel(f_ref, v_ref, out, *sums):
    def body(i, carry):
        layers = [f_ref[i, x] for x in range(4)]
        for x in range(4):
            here = layers[x]
            total = 3.0 * stencil_weights[0] * here
            for offset in range(1, 5):
                beside = pltpu.roll(here, offset, 0) + pltpu.roll(here, 64 - offset, 0)
                beside = beside + pltpu.roll(here, offset, 1) + pltpu.roll(here, 128 - offset, 1)
                if x + offset < 4:
                    beside = beside + layers[x + offset]
                if x - offset >= 0:
                    beside = beside + layers[x - offset]
                total = total + stencil_weights[offset] * beside
            out[i, x] = -0.5 * total + v_ref[x] * here
        return carry

    lax.fori_loop(0, BLK, body, 0)
    if sums:

        def row(i):
            return lambda c: f_ref[i, c // 8, pl.ds(pl.multiple_of((c % 8) * 8, 8), 8), :]

        load = {n: row(n - 16) for n in OWN}
        sums[0][...] = pair_sums([[(q, r) for q in OWN for r in range(16, q + 1)]], load, 32)


def edged(inner, x, left, right):
    total = None
    for offset in range(1, 5):
        if x + offset >= 4:
            term = stencil_weights[offset] * right(x + offset - 4)
            total = term if total is None else total + term
        if x - offset < 0:
            term = stencil_weights[offset] * left(x - offset + 4)
            total = term if total is None else total + term
    return inner - 0.5 * total


def image_kernel(own, inner, left, right, out, sums):
    def body(i, carry):
        for x in range(4):
            part = pl.ds(64 * x, 64)
            out[i, part, :] = edged(
                inner[i, part, :],
                x,
                lambda n: left[i, pl.ds(64 * n, 64), :],
                lambda n: right[i, pl.ds(64 * n, 64), :],
            )
        return carry

    lax.fori_loop(0, BLK, body, 0)
    load = {n: loader(own, n - 16) for n in OWN}
    load |= {n: loader(out, n - 24) for n in IMAGE}
    jobs = split([(q, r) for q in IMAGE for r in OWN], 32)
    sums[...] = pair_sums(jobs, load, own.shape[1] // 8)


def dot(left, right, turn_left=False, turn_right=False):
    dims = (((0 if turn_left else 1,), (1 if turn_right else 0,)), ((), ()))
    return lax.dot_general(
        left, right, dims, precision=lax.Precision.HIGHEST, preferred_element_type=F32
    )


def places(y, home=None):
    row = lax.broadcasted_iota(jnp.int32, (128, 128), 0)
    lane = lax.broadcasted_iota(jnp.int32, (128, 128), 1)
    distance = (row + 2) >> 2
    distance = jnp.where(((row + 2) & 2) == 0, -distance, distance)
    piece = (y + distance) & 7
    target = (piece & 1) * 8 + (piece >> 1) * 2 + (row & 1)
    if home is None:
        target = jnp.where(row < 16, target, row)
    else:
        target = jnp.where((piece & 1) == home, -1, target)
        target = jnp.where(row < 16, target, row - 16 + 8 * home)
    return jnp.where((lane == target) & (row < 24), 1.0, 0.0)


def coeff_kernel(band_ref, weights_ref, gram_ref, own_ref, near_ref, far_ref, out):
    lane, sub = lanes(), subs()
    wide = lax.broadcasted_iota(jnp.int32, (128, 128), 1)
    row = lax.broadcasted_iota(jnp.int32, (128, 128), 0)
    place = places(band_ref[0] & 7)
    weights = jnp.where(lane < 24, pltpu.roll(weights_ref[...], 104, 1), 0.0)
    weights = dot(weights, place)

    def image_columns(matrix, place, source, target):
        columns = dot(place, matrix, turn_left=True)
        columns = pltpu.roll(columns, (target - source) % 128, 1)
        return jnp.where((wide >= target) & (wide < target + 8), columns, 0.0)

    def visiting(n):
        packed = jnp.where(band_ref[0] < RING, near_ref[n], far_ref[n])
        return image_columns(tall(unpacked(packed)), places(n, n), 24, 8 * n)

    block0, block1 = visiting(0), visiting(1)
    block = image_columns(tall(unpacked(own_ref[...])), place, 24, 16)
    half = dot(weights, block0 + block1 + block)
    half = half + dot(weights, jnp.where(row < 16, block, 0.0), turn_right=True)
    theta = dot(half, tall([weights]), turn_right=True)
    work = gram_ref[...] + move(theta, 0, 8)
    for k in range(8):
        line = work[k : k + 1, :]
        line = jnp.broadcast_to(line / jnp.broadcast_to(line[:, k : k + 1], (1, 128)), (8, 128))
        work = jnp.where(sub == k, line, work - spread_lane(work, k) * line)
    for j in range(8):
        out[j] = spread_lane(work, 8 + j)


def residual_kernel(f_ref, inner_ref, left_ref, right_ref, splat, out):
    def body(c, carry):
        def part(x):
            return pl.ds(pl.multiple_of(64 * x + 8 * c, 8), 8)

        for x in range(4):
            inputs = [f_ref[i, part(x), :] for i in range(BLK)]
            for j in range(BLK):
                total = edged(
                    inner_ref[j, part(x), :],
                    x,
                    lambda n: left_ref[j, part(n), :],
                    lambda n: right_ref[j, part(n), :],
                )
                for i in range(BLK):
                    total = total - splat[j, pl.ds(i, 1), :] * inputs[i]
                out[j, part(x), :] = total
        return carry

    lax.fori_loop(0, 8, body, 0)


def domain_parts(copies):
    return lax.all_to_all(copies, "domain", 0, 0)


def ring_shift(block, step, rings=(0, 1)):
    pairs = [(z * RING + y, z * RING + (y + step) % RING) for z in rings for y in range(RING)]
    return lax.ppermute(block, "band", pairs)


def neighbours(block):
    count = lax.axis_size("domain")
    left = lax.ppermute(block, "domain", [(i, (i + 1) % count) for i in range(count)])
    right = lax.ppermute(block, "domain", [((i + 1) % count, i) for i in range(count)])
    return left, right


def local(orbitals, potential):
    blocks, slab_width, rows_y, rows_z = orbitals.shape
    domain, bands = lax.axis_size("domain"), lax.axis_size("band")
    cells_total = float(slab_width * rows_y * rows_z * domain)
    band = lax.axis_index("band")
    band_word = band.reshape(1).astype(jnp.int32)
    flat = (blocks, slab_width * rows_y, rows_z)
    big = flat[0] * flat[1] * flat[2]
    slab = jax.ShapeDtypeStruct(flat, F32)
    field = jax.ShapeDtypeStruct(orbitals.shape, F32)
    tile = jax.ShapeDtypeStruct((8, 128), F32)

    def inner_part(block, *sums):
        return call(
            inner_kernel,
            (field, *sums),
            specs=[VMEM] * 2,
            flops=60 * big,
            bytes_moved=8 * big,
        )(block, potential)

    own = orbitals.reshape(flat)
    quarters = [own[2 * k : 2 * k + 2] for k in range(4)]
    arrived = [
        lax.ppermute(quarters[k], "band", [(0, 2 * k), (1, 2 * k + 1)]) for k in (1, 3, 2)
    ]
    inner, sums = inner_part(orbitals, tile)
    arrived, inner, sums = lax.optimization_barrier((arrived, inner, sums))
    piece = jnp.where(band < 2, quarters[0], 0.0)
    for part in arrived:
        piece = piece + part
    left, right = neighbours(own)
    near = band < RING
    crossed = lax.ppermute(piece, "band", [(y, y + RING) for y in range(RING)])
    first = [ring_shift(piece, 1, (0,)), ring_shift(piece, -1, (0,))]
    second = [ring_shift(crossed, 1, (1,)), ring_shift(crossed, -1, (1,))]
    up, down = (jnp.where(near, a, b) for a, b in zip(first, second))
    piece = jnp.where(near, piece, crossed)

    def stage(fresh, imaged, pieces, *sums, last=False):
        sources = (*pieces, own, *((image,) if imaged else ()), *sums)
        return call(
            lambda *refs: stage_kernel(len(pieces), fresh, imaged, last, *refs),
            jax.ShapeDtypeStruct((domain, 8, 128), F32) if last else tile,
            specs=[VMEM] * len(sources),
            flops=20 * big,
            bytes_moved=10 * big,
        )(*sources)

    pieces = [piece, up, down]
    up, down = ring_shift(up, 1), ring_shift(down, -1)
    sums = stage(range(6), (), pieces, sums)
    down, sums = lax.optimization_barrier((down, sums))
    pieces += [up, down]
    up, down = ring_shift(up, 1), ring_shift(down, -1)
    sums = stage(range(6, 10), (), pieces, sums)
    image, image_sums = call(
        image_kernel, (slab, tile), specs=[VMEM] * 4, flops=50 * big, bytes_moved=20 * big
    )(own, inner.reshape(flat), left, right)
    down, sums, image, image_sums = lax.optimization_barrier((down, sums, image, image_sums))
    pieces += [up, down]
    up, down = ring_shift(up[:1], 1), ring_shift(down[1:], -1)
    sums = stage(range(10, 14), range(14), pieces, sums, image_sums)
    pieces += [up, down]
    sums = stage(range(14, 16), range(14, 16), pieces, sums, last=True)
    sums = call(
        lambda *refs: total_kernel(cells_total, *refs),
        tile,
        specs=[VMEM],
        flops=40 * 1024,
        bytes_moved=160 * 1024,
    )(domain_parts(sums))
    basis, weights, gram = call(
        combine_kernel,
        (slab, tile, tile),
        scratch=[pltpu.VMEM((24, 8, 128), F32)],
        specs=[SMEM] + [VMEM] * 11,
        flops=48 * big,
        bytes_moved=16 * big,
    )(band_word, sums, *pieces, own)
    left, right = neighbours(basis)
    inner = inner_part(basis.reshape(orbitals.shape))[0].reshape(flat)
    shared, inner = lax.optimization_barrier((sums, inner))
    other = lax.ppermute(shared, "band", [(0, 1), (1, 0)])
    shared = jnp.stack([jnp.where(band == 0, shared, other), jnp.where(band == 0, other, shared)])
    shared = jnp.where(band < 2, shared, 0.0)
    shared = shared + lax.ppermute(shared, "band", [(0, 4), (1, 5)])
    shared = shared + lax.ppermute(shared, "band", [(0, 2), (1, 3), (4, 6), (5, 7)])
    far = lax.ppermute(shared, "band", [(y, y + RING) for y in range(RING)])
    splat = call(
        coeff_kernel, jax.ShapeDtypeStruct((8, 8, 128), F32), specs=[SMEM] + [VMEM] * 5
    )(band_word, weights, gram, sums, shared, far)
    residual = call(
        residual_kernel, slab, specs=[VMEM] * 5, flops=30 * big, bytes_moved=20 * big
    )(basis, inner, left, right, splat)
    return (basis.reshape(orbitals.shape), residual.reshape(orbitals.shape))


def solution(mesh):
    return jax.shard_map(
        local,
        mesh=mesh,
        in_specs=(P("band", "domain", None, None), P("domain", None, None)),
        out_specs=(P("band", "domain", None, None), P("band", "domain", None, None)),
        check_vma=False,
    )
```

```python
import jax
import jax.numpy as jnp
from jax import lax
from jax.experimental import pallas as pl
from jax.experimental.pallas import tpu as pltpu
from jax.sharding import PartitionSpec as P

stencil_weights = (-205.0 / 72.0, 8.0 / 5.0, -1.0 / 5.0, 8.0 / 315.0, -1.0 / 560.0)
BLK = 8
RING = 8
F32 = jnp.float32
VMEM = pl.BlockSpec(memory_space=pltpu.VMEM)
SMEM = pl.BlockSpec(memory_space=pltpu.SMEM)


def call(kernel, outs, scratch=(), specs=None, flops=0, bytes_moved=0):
    return pl.pallas_call(
        kernel,
        out_shape=outs,
        in_specs=specs,
        out_specs=jax.tree.map(lambda _: VMEM, outs),
        scratch_shapes=scratch,
        compiler_params=pltpu.CompilerParams(vmem_limit_bytes=32 * 1024 * 1024),
        cost_estimate=pl.CostEstimate(flops=flops, bytes_accessed=bytes_moved, transcendentals=0),
    )


def lanes():
    return lax.broadcasted_iota(jnp.int32, (8, 128), 1)


def subs():
    return lax.broadcasted_iota(jnp.int32, (8, 128), 0)


def pair_sums(jobs, load, chunks):
    lane = lanes()
    result = jnp.zeros((8, 128), F32)
    zero_row = jnp.zeros((1, 128), F32)
    for pairs in jobs:
        used = sorted({n for pair in pairs for n in pair})

        def body(c, sums, pairs=pairs, used=used):
            for step in range(4):
                rows = {n: load[n](4 * c + step) for n in used}
                sums = tuple(s + rows[q] * rows[r] for s, (q, r) in zip(sums, pairs))
            return sums

        zero = jnp.zeros((8, 128), F32)
        sums = lax.fori_loop(0, chunks // 4, body, (zero,) * len(pairs))
        columns = {}
        for s, (q, r) in zip(sums, pairs):
            rows = columns.setdefault(32 * (r // 8) + q, [zero_row] * 8)
            rows[r % 8] = jnp.sum(s, axis=0, keepdims=True)
        for place, rows in columns.items():
            column = jnp.sum(jnp.concatenate(rows, axis=0), axis=1, keepdims=True)
            result = result + jnp.where(lane == place, column, 0.0)
    return result


def loader(ref, index):
    return lambda c: ref[index, pl.ds(pl.multiple_of(c * 8, 8), 8), :]


def move(tile, source, target):
    lane = lanes()
    if source != target:
        tile = pltpu.roll(tile, (target - source) % 128, 1)
    return jnp.where((lane >= target) & (lane < target + 8), tile, 0.0)


def spread_lane(tile, k):
    return jnp.broadcast_to(tile[:, k : k + 1], (8, 128))


def rows_of(refs):
    return [(r, i) for r in refs for i in range(r.shape[0])]


def unpacked(sums):
    lane = lanes()
    parts = [sums] + [pltpu.roll(sums, 128 - 32 * n, 1) for n in (1, 2)]
    return [jnp.where(lane < 32, part, 0.0) for part in parts]


def tall(tiles):
    return jnp.concatenate(tiles + [jnp.zeros((128 - 8 * len(tiles), 128), F32)], axis=0)


OWN = list(range(16, 24))
IMAGE = list(range(24, 32))


def split(pairs, size=36):
    if not pairs:
        return []
    count = -(-len(pairs) // size)
    size = -(-len(pairs) // count)
    return [pairs[n : n + size] for n in range(0, len(pairs), size)]


def stage_kernel(parts, fresh, imaged, last, *refs):
    out = refs[-1]
    pieces, refs = refs[:parts], refs[parts:-1]
    own, image, before = (refs[0], refs[1], refs[2:]) if imaged else (refs[0], None, refs[1:])
    chunks = own.shape[1] // 8
    load = {n: loader(r, i) for n, (r, i) in enumerate(rows_of(pieces))}
    load |= {n: loader(own, n - 16) for n in OWN}
    if imaged:
        load |= {n: loader(image, n - 24) for n in IMAGE}
    jobs = split([(q, r) for q in OWN for r in fresh])
    jobs += split([(q, r) for q in fresh for r in range(q + 1)])
    jobs += split([(q, r) for q in IMAGE for r in imaged])
    total = pair_sums(jobs, load, chunks)
    for part in before:
        total = total + part[...]
    if last:
        for n in range(out.shape[0]):
            out[n] = total
    else:
        out[...] = total


def total_kernel(cells_total, parts_ref, out):
    out[...] = jnp.sum(parts_ref[...], axis=0) / cells_total


def combine_kernel(band_ref, sums_ref, *refs):
    *pieces, own, out, weights_ref, gram_ref, splat = refs
    band = band_ref[0]
    lane, sub = lanes(), subs()
    tiles = unpacked(sums_ref[...])
    turned = jnp.transpose(tall(tiles))
    w0, w1, w2 = (
        jnp.where(lane < 24, tile + jnp.where(lane == sub + 8 * n, 0.0, turned[8 * n : 8 * n + 8]), 0.0)
        for n, tile in enumerate(tiles)
    )
    later = band >= 2
    second = band == 1

    def taken(position):
        place = position & 7
        return later | (second & (place >= 2) & (place <= 5))

    row_in = taken(sub)
    lane_in = (lane >= 16) | taken(lane)
    kept = row_in & lane_in
    w0 = jnp.where(kept, w0, jnp.where(lane == sub, 1.0, 0.0))
    w1 = jnp.where(kept, w1, jnp.where(lane == 8 + sub, 1.0, 0.0))
    w0 = w0 + jnp.where(lane == 24 + sub, 1.0, 0.0)
    w1 = w1 + jnp.where(lane == 32 + sub, 1.0, 0.0)
    w2 = jnp.where(lane_in, w2, 0.0) + jnp.where(lane == 40 + sub, 1.0, 0.0)
    tiles = [w0, w1, w2]
    for k in range(16):
        v, s = divmod(k, 8)
        row = tiles[v][s : s + 1, :]
        row = row / jnp.broadcast_to(row[:, k : k + 1], (1, 128))
        row = jnp.broadcast_to(row, (8, 128))
        for u in range(v, 3):
            column = spread_lane(tiles[u], k)
            if u == v:
                column = jnp.where(sub > s, column, 0.0)
            tiles[u] = tiles[u] - column * row
    plain = tiles[2]
    scaled = plain
    for k in range(8):
        row = scaled[k : k + 1, :]
        row = row / jnp.broadcast_to(row[:, 16 + k : 17 + k], (1, 128))
        column = jnp.where(sub > k, spread_lane(scaled, 16 + k), 0.0)
        scaled = scaled - column * jnp.broadcast_to(row, (8, 128))
    pivots = jnp.sum(jnp.where(lane == 16 + sub, scaled, 0.0), axis=1, keepdims=True)
    scaled = scaled / jnp.sqrt(jnp.broadcast_to(pivots, (8, 128)))
    weights = jnp.where(later, plain, scaled)
    weights_ref[...] = weights
    gram_ref[...] = jnp.where(later, move(plain, 16, 0), jnp.where(lane == sub, 1.0, 0.0))
    for c in range(24):
        splat[c] = spread_lane(weights, 24 + c)
    rows = rows_of(pieces) + [(own, i) for i in range(BLK)]

    def body(c, carry):
        part = pl.ds(pl.multiple_of(c * 16, 16), 16)
        inputs = [r[i, part, :] for r, i in rows]
        for i in range(BLK):
            total = splat[0, pl.ds(i, 1), :] * inputs[0]
            for n in range(1, 24):
                total = total + splat[n, pl.ds(i, 1), :] * inputs[n]
            out[i, part, :] = total
        return carry

    lax.fori_loop(0, own.shape[1] // 16, body, 0)


def inner_kernel(f_ref, v_ref, out, *sums):
    def body(i, carry):
        layers = [f_ref[i, x] for x in range(4)]
        for x in range(4):
            here = layers[x]
            total = 3.0 * stencil_weights[0] * here
            for offset in range(1, 5):
                beside = pltpu.roll(here, offset, 0) + pltpu.roll(here, 64 - offset, 0)
                beside = beside + pltpu.roll(here, offset, 1) + pltpu.roll(here, 128 - offset, 1)
                if x + offset < 4:
                    beside = beside + layers[x + offset]
                if x - offset >= 0:
                    beside = beside + layers[x - offset]
                total = total + stencil_weights[offset] * beside
            out[i, x] = -0.5 * total + v_ref[x] * here
        return carry

    lax.fori_loop(0, BLK, body, 0)
    if sums:

        def row(i):
            return lambda c: f_ref[i, c // 8, pl.ds(pl.multiple_of((c % 8) * 8, 8), 8), :]

        load = {n: row(n - 16) for n in OWN}
        sums[0][...] = pair_sums([[(q, r) for q in OWN for r in range(16, q + 1)]], load, 32)


def edged(inner, x, left, right):
    total = None
    for offset in range(1, 5):
        if x + offset >= 4:
            term = stencil_weights[offset] * right(x + offset - 4)
            total = term if total is None else total + term
        if x - offset < 0:
            term = stencil_weights[offset] * left(x - offset + 4)
            total = term if total is None else total + term
    return inner - 0.5 * total


def image_kernel(own, inner, left, right, out, sums):
    def body(i, carry):
        for x in range(4):
            part = pl.ds(64 * x, 64)
            out[i, part, :] = edged(
                inner[i, part, :],
                x,
                lambda n: left[i, pl.ds(64 * n, 64), :],
                lambda n: right[i, pl.ds(64 * n, 64), :],
            )
        return carry

    lax.fori_loop(0, BLK, body, 0)
    load = {n: loader(own, n - 16) for n in OWN}
    load |= {n: loader(out, n - 24) for n in IMAGE}
    jobs = split([(q, r) for q in IMAGE for r in OWN], 32)
    sums[...] = pair_sums(jobs, load, own.shape[1] // 8)


def dot(left, right, turn_left=False, turn_right=False):
    dims = (((0 if turn_left else 1,), (1 if turn_right else 0,)), ((), ()))
    return lax.dot_general(
        left, right, dims, precision=lax.Precision.HIGHEST, preferred_element_type=F32
    )


def places(y, home=None):
    row = lax.broadcasted_iota(jnp.int32, (128, 128), 0)
    lane = lax.broadcasted_iota(jnp.int32, (128, 128), 1)
    distance = (row + 2) >> 2
    distance = jnp.where(((row + 2) & 2) == 0, -distance, distance)
    piece = (y + distance) & 7
    target = (piece & 1) * 8 + (piece >> 1) * 2 + (row & 1)
    if home is None:
        target = jnp.where(row < 16, target, row)
    else:
        target = jnp.where((piece & 1) == home, -1, target)
        target = jnp.where(row < 16, target, row - 16 + 8 * home)
    return jnp.where((lane == target) & (row < 24), 1.0, 0.0)


def coeff_kernel(band_ref, weights_ref, gram_ref, own_ref, near_ref, far_ref, out):
    lane, sub = lanes(), subs()
    wide = lax.broadcasted_iota(jnp.int32, (128, 128), 1)
    row = lax.broadcasted_iota(jnp.int32, (128, 128), 0)
    place = places(band_ref[0] & 7)
    weights = jnp.where(lane < 24, pltpu.roll(weights_ref[...], 104, 1), 0.0)
    weights = dot(weights, place)

    def image_columns(matrix, place, source, target):
        columns = dot(place, matrix, turn_left=True)
        columns = pltpu.roll(columns, (target - source) % 128, 1)
        return jnp.where((wide >= target) & (wide < target + 8), columns, 0.0)

    def visiting(n):
        packed = jnp.where(band_ref[0] < RING, near_ref[n], far_ref[n])
        return image_columns(tall(unpacked(packed)), places(n, n), 24, 8 * n)

    block0, block1 = visiting(0), visiting(1)
    block = image_columns(tall(unpacked(own_ref[...])), place, 24, 16)
    half = dot(weights, block0 + block1 + block)
    half = half + dot(weights, jnp.where(row < 16, block, 0.0), turn_right=True)
    theta = dot(half, tall([weights]), turn_right=True)
    work = gram_ref[...] + move(theta, 0, 8)
    for k in range(8):
        line = work[k : k + 1, :]
        line = jnp.broadcast_to(line / jnp.broadcast_to(line[:, k : k + 1], (1, 128)), (8, 128))
        work = jnp.where(sub == k, line, work - spread_lane(work, k) * line)
    for j in range(8):
        out[j] = spread_lane(work, 8 + j)


def residual_kernel(f_ref, inner_ref, left_ref, right_ref, splat, out):
    def body(c, carry):
        def part(x):
            return pl.ds(pl.multiple_of(64 * x + 8 * c, 8), 8)

        for x in range(4):
            inputs = [f_ref[i, part(x), :] for i in range(BLK)]
            for j in range(BLK):
                total = edged(
                    inner_ref[j, part(x), :],
                    x,
                    lambda n: left_ref[j, part(n), :],
                    lambda n: right_ref[j, part(n), :],
                )
                for i in range(BLK):
                    total = total - splat[j, pl.ds(i, 1), :] * inputs[i]
                out[j, part(x), :] = total
        return carry

    lax.fori_loop(0, 8, body, 0)


def domain_parts(copies):
    return lax.all_to_all(copies, "domain", 0, 0)


def ring_shift(block, step):
    pairs = [(z * RING + y, z * RING + (y + step) % RING) for z in range(2) for y in range(RING)]
    return lax.ppermute(block, "band", pairs)


def neighbours(block):
    count = lax.axis_size("domain")
    left = lax.ppermute(block, "domain", [(i, (i + 1) % count) for i in range(count)])
    right = lax.ppermute(block, "domain", [((i + 1) % count, i) for i in range(count)])
    return left, right


def local(orbitals, potential):
    blocks, slab_width, rows_y, rows_z = orbitals.shape
    domain = lax.axis_size("domain")
    cells_total = float(slab_width * rows_y * rows_z * domain)
    band = lax.axis_index("band")
    band_word = band.reshape(1).astype(jnp.int32)
    flat = (blocks, slab_width * rows_y, rows_z)
    big = flat[0] * flat[1] * flat[2]
    slab = jax.ShapeDtypeStruct(flat, F32)
    field = jax.ShapeDtypeStruct(orbitals.shape, F32)
    tile = jax.ShapeDtypeStruct((8, 128), F32)

    def inner_part(block, *sums):
        return call(
            inner_kernel,
            (field, *sums),
            specs=[VMEM] * 2,
            flops=60 * big,
            bytes_moved=8 * big,
        )(block, potential)

    own = orbitals.reshape(flat)
    quarters = [own[2 * k : 2 * k + 2] for k in range(4)]
    arrived = [
        lax.ppermute(quarters[k], "band", [(0, 2 * k), (1, 2 * k + 1)]) for k in (1, 3, 2)
    ]
    inner, sums = inner_part(orbitals, tile)
    arrived, inner, sums = lax.optimization_barrier((arrived, inner, sums))
    piece = jnp.where(band < 2, quarters[0], 0.0)
    for part in arrived:
        piece = piece + part
    left, right = neighbours(own)
    crossed = lax.ppermute(piece, "band", [(y, y + RING) for y in range(RING)])
    piece = jnp.where(band < RING, piece, crossed)

    def stage(fresh, imaged, pieces, *sums, last=False):
        sources = (*pieces, own, *((image,) if imaged else ()), *sums)
        return call(
            lambda *refs: stage_kernel(len(pieces), fresh, imaged, last, *refs),
            jax.ShapeDtypeStruct((domain, 8, 128), F32) if last else tile,
            specs=[VMEM] * len(sources),
            flops=20 * big,
            bytes_moved=10 * big,
        )(*sources)

    pieces = [piece]
    up, down = ring_shift(piece, 1), ring_shift(piece, -1)
    pieces += [up, down]
    up, down = ring_shift(up, 1), ring_shift(down, -1)
    sums = stage(range(6), (), pieces, sums)
    down, sums = lax.optimization_barrier((down, sums))
    pieces += [up, down]
    up, down = ring_shift(up, 1), ring_shift(down, -1)
    sums = stage(range(6, 10), (), pieces, sums)
    image, image_sums = call(
        image_kernel, (slab, tile), specs=[VMEM] * 4, flops=50 * big, bytes_moved=20 * big
    )(own, inner.reshape(flat), left, right)
    down, sums, image, image_sums = lax.optimization_barrier((down, sums, image, image_sums))
    pieces += [up, down]
    up, down = ring_shift(up[:1], 1), ring_shift(down[1:], -1)
    sums = stage(range(10, 14), range(14), pieces, sums, image_sums)
    pieces += [up, down]
    sums = stage(range(14, 16), range(14, 16), pieces, sums, last=True)
    sums = call(
        lambda *refs: total_kernel(cells_total, *refs),
        tile,
        specs=[VMEM],
        flops=40 * 1024,
        bytes_moved=160 * 1024,
    )(domain_parts(sums))
    basis, weights, gram = call(
        combine_kernel,
        (slab, tile, tile),
        scratch=[pltpu.VMEM((24, 8, 128), F32)],
        specs=[SMEM] + [VMEM] * 11,
        flops=48 * big,
        bytes_moved=16 * big,
    )(band_word, sums, *pieces, own)
    left, right = neighbours(basis)
    inner = inner_part(basis.reshape(orbitals.shape))[0].reshape(flat)
    shared, inner = lax.optimization_barrier((sums, inner))
    other = lax.ppermute(shared, "band", [(0, 1), (1, 0)])
    shared = jnp.stack([jnp.where(band == 0, shared, other), jnp.where(band == 0, other, shared)])
    shared = jnp.where(band < 2, shared, 0.0)
    shared = shared + lax.ppermute(shared, "band", [(0, 4), (1, 5)])
    shared = shared + lax.ppermute(shared, "band", [(0, 2), (1, 3), (4, 6), (5, 7)])
    far = lax.ppermute(shared, "band", [(y, y + RING) for y in range(RING)])
    splat = call(
        coeff_kernel, jax.ShapeDtypeStruct((8, 8, 128), F32), specs=[SMEM] + [VMEM] * 5
    )(band_word, weights, gram, sums, shared, far)
    residual = call(
        residual_kernel, slab, specs=[VMEM] * 5, flops=30 * big, bytes_moved=20 * big
    )(basis, inner, left, right, splat)
    return (basis.reshape(orbitals.shape), residual.reshape(orbitals.shape))


def solution(mesh):
    return jax.shard_map(
        local,
        mesh=mesh,
        in_specs=(P("band", "domain", None, None), P("domain", None, None)),
        out_specs=(P("band", "domain", None, None), P("band", "domain", None, None)),
        check_vma=False,
    )
```

```python
import jax
import jax.numpy as jnp
from jax import lax
from jax.experimental import pallas as pl
from jax.experimental.pallas import tpu as pltpu
from jax.sharding import PartitionSpec as P

stencil_weights = (-205.0 / 72.0, 8.0 / 5.0, -1.0 / 5.0, 8.0 / 315.0, -1.0 / 560.0)
BLK = 8
RING = 8
F32 = jnp.float32
VMEM = pl.BlockSpec(memory_space=pltpu.VMEM)
SMEM = pl.BlockSpec(memory_space=pltpu.SMEM)


def call(kernel, outs, scratch=(), specs=None, flops=0, bytes_moved=0):
    return pl.pallas_call(
        kernel,
        out_shape=outs,
        in_specs=specs,
        out_specs=jax.tree.map(lambda _: VMEM, outs),
        scratch_shapes=scratch,
        compiler_params=pltpu.CompilerParams(vmem_limit_bytes=32 * 1024 * 1024),
        cost_estimate=pl.CostEstimate(flops=flops, bytes_accessed=bytes_moved, transcendentals=0),
    )


def lanes():
    return lax.broadcasted_iota(jnp.int32, (8, 128), 1)


def subs():
    return lax.broadcasted_iota(jnp.int32, (8, 128), 0)


def pair_sums(jobs, load, chunks):
    lane = lanes()
    result = jnp.zeros((8, 128), F32)
    zero_row = jnp.zeros((1, 128), F32)
    for pairs in jobs:
        used = sorted({n for pair in pairs for n in pair})

        def body(c, sums, pairs=pairs, used=used):
            for step in range(4):
                rows = {n: load[n](4 * c + step) for n in used}
                sums = tuple(s + rows[q] * rows[r] for s, (q, r) in zip(sums, pairs))
            return sums

        zero = jnp.zeros((8, 128), F32)
        sums = lax.fori_loop(0, chunks // 4, body, (zero,) * len(pairs))
        columns = {}
        for s, (q, r) in zip(sums, pairs):
            rows = columns.setdefault(32 * (r // 8) + q, [zero_row] * 8)
            rows[r % 8] = jnp.sum(s, axis=0, keepdims=True)
        for place, rows in columns.items():
            column = jnp.sum(jnp.concatenate(rows, axis=0), axis=1, keepdims=True)
            result = result + jnp.where(lane == place, column, 0.0)
    return result


def loader(ref, index):
    return lambda c: ref[index, pl.ds(pl.multiple_of(c * 8, 8), 8), :]


def move(tile, source, target):
    lane = lanes()
    if source != target:
        tile = pltpu.roll(tile, (target - source) % 128, 1)
    return jnp.where((lane >= target) & (lane < target + 8), tile, 0.0)


def spread_lane(tile, k):
    return jnp.broadcast_to(tile[:, k : k + 1], (8, 128))


def rows_of(refs):
    return [(r, i) for r in refs for i in range(r.shape[0])]


def unpacked(sums):
    lane = lanes()
    parts = [sums] + [pltpu.roll(sums, 128 - 32 * n, 1) for n in (1, 2)]
    return [jnp.where(lane < 32, part, 0.0) for part in parts]


def tall(tiles):
    return jnp.concatenate(tiles + [jnp.zeros((128 - 8 * len(tiles), 128), F32)], axis=0)


OWN = list(range(16, 24))
IMAGE = list(range(24, 32))


def split(pairs, size=36):
    if not pairs:
        return []
    count = -(-len(pairs) // size)
    size = -(-len(pairs) // count)
    return [pairs[n : n + size] for n in range(0, len(pairs), size)]


def stage_kernel(parts, fresh, imaged, last, *refs):
    out = refs[-1]
    pieces, refs = refs[:parts], refs[parts:-1]
    own, image, before = (refs[0], refs[1], refs[2:]) if imaged else (refs[0], None, refs[1:])
    chunks = own.shape[1] // 8
    load = {n: loader(r, i) for n, (r, i) in enumerate(rows_of(pieces))}
    load |= {n: loader(own, n - 16) for n in OWN}
    if imaged:
        load |= {n: loader(image, n - 24) for n in IMAGE}
    jobs = split([(q, r) for q in OWN for r in fresh])
    jobs += split([(q, r) for q in fresh for r in range(q + 1)])
    jobs += split([(q, r) for q in IMAGE for r in imaged])
    total = pair_sums(jobs, load, chunks)
    for part in before:
        total = total + part[...]
    if last:
        for n in range(out.shape[0]):
            out[n] = total
    else:
        out[...] = total


def total_kernel(cells_total, parts_ref, out):
    out[...] = jnp.sum(parts_ref[...], axis=0) / cells_total


def combine_kernel(band_ref, sums_ref, *refs):
    *pieces, own, out, weights_ref, gram_ref, splat = refs
    band = band_ref[0]
    lane, sub = lanes(), subs()
    tiles = unpacked(sums_ref[...])
    turned = jnp.transpose(tall(tiles))
    w0, w1, w2 = (
        jnp.where(lane < 24, tile + jnp.where(lane == sub + 8 * n, 0.0, turned[8 * n : 8 * n + 8]), 0.0)
        for n, tile in enumerate(tiles)
    )
    later = band >= 2
    second = band == 1

    def taken(position):
        place = position & 7
        return later | (second & (place >= 2) & (place <= 5))

    row_in = taken(sub)
    lane_in = (lane >= 16) | taken(lane)
    kept = row_in & lane_in
    w0 = jnp.where(kept, w0, jnp.where(lane == sub, 1.0, 0.0))
    w1 = jnp.where(kept, w1, jnp.where(lane == 8 + sub, 1.0, 0.0))
    w0 = w0 + jnp.where(lane == 24 + sub, 1.0, 0.0)
    w1 = w1 + jnp.where(lane == 32 + sub, 1.0, 0.0)
    w2 = jnp.where(lane_in, w2, 0.0) + jnp.where(lane == 40 + sub, 1.0, 0.0)
    tiles = [w0, w1, w2]
    for k in range(16):
        v, s = divmod(k, 8)
        row = tiles[v][s : s + 1, :]
        row = row / jnp.broadcast_to(row[:, k : k + 1], (1, 128))
        row = jnp.broadcast_to(row, (8, 128))
        for u in range(v, 3):
            column = spread_lane(tiles[u], k)
            if u == v:
                column = jnp.where(sub > s, column, 0.0)
            tiles[u] = tiles[u] - column * row
    plain = tiles[2]
    scaled = plain
    for k in range(8):
        row = scaled[k : k + 1, :]
        row = row / jnp.broadcast_to(row[:, 16 + k : 17 + k], (1, 128))
        column = jnp.where(sub > k, spread_lane(scaled, 16 + k), 0.0)
        scaled = scaled - column * jnp.broadcast_to(row, (8, 128))
    pivots = jnp.sum(jnp.where(lane == 16 + sub, scaled, 0.0), axis=1, keepdims=True)
    scaled = scaled / jnp.sqrt(jnp.broadcast_to(pivots, (8, 128)))
    weights = jnp.where(later, plain, scaled)
    weights_ref[...] = weights
    gram_ref[...] = jnp.where(later, move(plain, 16, 0), jnp.where(lane == sub, 1.0, 0.0))
    for c in range(24):
        splat[c] = spread_lane(weights, 24 + c)
    rows = rows_of(pieces) + [(own, i) for i in range(BLK)]

    def body(c, carry):
        part = pl.ds(pl.multiple_of(c * 16, 16), 16)
        inputs = [r[i, part, :] for r, i in rows]
        for i in range(BLK):
            total = splat[0, pl.ds(i, 1), :] * inputs[0]
            for n in range(1, 24):
                total = total + splat[n, pl.ds(i, 1), :] * inputs[n]
            out[i, part, :] = total
        return carry

    lax.fori_loop(0, own.shape[1] // 16, body, 0)


def inner_kernel(f_ref, v_ref, out, *sums):
    def body(i, carry):
        layers = [f_ref[i, x] for x in range(4)]
        for x in range(4):
            here = layers[x]
            total = 3.0 * stencil_weights[0] * here
            for offset in range(1, 5):
                beside = pltpu.roll(here, offset, 0) + pltpu.roll(here, 64 - offset, 0)
                beside = beside + pltpu.roll(here, offset, 1) + pltpu.roll(here, 128 - offset, 1)
                if x + offset < 4:
                    beside = beside + layers[x + offset]
                if x - offset >= 0:
                    beside = beside + layers[x - offset]
                total = total + stencil_weights[offset] * beside
            out[i, x] = -0.5 * total + v_ref[x] * here
        return carry

    lax.fori_loop(0, BLK, body, 0)
    if sums:

        def row(i):
            return lambda c: f_ref[i, c // 8, pl.ds(pl.multiple_of((c % 8) * 8, 8), 8), :]

        load = {n: row(n - 16) for n in OWN}
        sums[0][...] = pair_sums([[(q, r) for q in OWN for r in range(16, q + 1)]], load, 32)


def edged(inner, x, left, right):
    total = None
    for offset in range(1, 5):
        if x + offset >= 4:
            term = stencil_weights[offset] * right(x + offset - 4)
            total = term if total is None else total + term
        if x - offset < 0:
            term = stencil_weights[offset] * left(x - offset + 4)
            total = term if total is None else total + term
    return inner - 0.5 * total


def image_kernel(own, inner, left, right, out, sums):
    def body(i, carry):
        for x in range(4):
            part = pl.ds(64 * x, 64)
            out[i, part, :] = edged(
                inner[i, part, :],
                x,
                lambda n: left[i, pl.ds(64 * n, 64), :],
                lambda n: right[i, pl.ds(64 * n, 64), :],
            )
        return carry

    lax.fori_loop(0, BLK, body, 0)
    load = {n: loader(own, n - 16) for n in OWN}
    load |= {n: loader(out, n - 24) for n in IMAGE}
    jobs = split([(q, r) for q in IMAGE for r in OWN], 32)
    sums[...] = pair_sums(jobs, load, own.shape[1] // 8)


def dot(left, right, turn_left=False, turn_right=False):
    dims = (((0 if turn_left else 1,), (1 if turn_right else 0,)), ((), ()))
    return lax.dot_general(
        left, right, dims, precision=lax.Precision.HIGHEST, preferred_element_type=F32
    )


def places(y, home=None):
    row = lax.broadcasted_iota(jnp.int32, (128, 128), 0)
    lane = lax.broadcasted_iota(jnp.int32, (128, 128), 1)
    distance = (row + 2) >> 2
    distance = jnp.where(((row + 2) & 2) == 0, -distance, distance)
    piece = (y + distance) & 7
    target = (piece & 1) * 8 + (piece >> 1) * 2 + (row & 1)
    if home is None:
        target = jnp.where(row < 16, target, row)
    else:
        target = jnp.where((piece & 1) == home, -1, target)
        target = jnp.where(row < 16, target, row - 16 + 8 * home)
    return jnp.where((lane == target) & (row < 24), 1.0, 0.0)


def coeff_kernel(band_ref, weights_ref, gram_ref, own_ref, near_ref, far_ref, out):
    lane, sub = lanes(), subs()
    wide = lax.broadcasted_iota(jnp.int32, (128, 128), 1)
    row = lax.broadcasted_iota(jnp.int32, (128, 128), 0)
    place = places(band_ref[0] & 7)
    weights = jnp.where(lane < 24, pltpu.roll(weights_ref[...], 104, 1), 0.0)
    weights = dot(weights, place)

    def image_columns(matrix, place, source, target):
        columns = dot(place, matrix, turn_left=True)
        columns = pltpu.roll(columns, (target - source) % 128, 1)
        return jnp.where((wide >= target) & (wide < target + 8), columns, 0.0)

    def visiting(n):
        packed = jnp.where(band_ref[0] < RING, near_ref[n], far_ref[n])
        return image_columns(tall(unpacked(packed)), places(n, n), 24, 8 * n)

    block0, block1 = visiting(0), visiting(1)
    block = image_columns(tall(unpacked(own_ref[...])), place, 24, 16)
    half = dot(weights, block0 + block1 + block)
    half = half + dot(weights, jnp.where(row < 16, block, 0.0), turn_right=True)
    theta = dot(half, tall([weights]), turn_right=True)
    work = gram_ref[...] + move(theta, 0, 8)
    for k in range(8):
        line = work[k : k + 1, :]
        line = jnp.broadcast_to(line / jnp.broadcast_to(line[:, k : k + 1], (1, 128)), (8, 128))
        work = jnp.where(sub == k, line, work - spread_lane(work, k) * line)
    for j in range(8):
        out[j] = spread_lane(work, 8 + j)


def residual_kernel(f_ref, inner_ref, left_ref, right_ref, splat, out):
    def body(c, carry):
        def part(x):
            return pl.ds(pl.multiple_of(64 * x + 8 * c, 8), 8)

        for x in range(4):
            inputs = [f_ref[i, part(x), :] for i in range(BLK)]
            for j in range(BLK):
                total = edged(
                    inner_ref[j, part(x), :],
                    x,
                    lambda n: left_ref[j, part(n), :],
                    lambda n: right_ref[j, part(n), :],
                )
                for i in range(BLK):
                    total = total - splat[j, pl.ds(i, 1), :] * inputs[i]
                out[j, part(x), :] = total
        return carry

    lax.fori_loop(0, 8, body, 0)


def domain_parts(copies):
    return lax.all_to_all(copies, "domain", 0, 0)


def ring_shift(block, step):
    pairs = [(z * RING + y, z * RING + (y + step) % RING) for z in range(2) for y in range(RING)]
    return lax.ppermute(block, "band", pairs)


def neighbours(block):
    count = lax.axis_size("domain")
    left = lax.ppermute(block, "domain", [(i, (i + 1) % count) for i in range(count)])
    right = lax.ppermute(block, "domain", [((i + 1) % count, i) for i in range(count)])
    return left, right


def local(orbitals, potential):
    blocks, slab_width, rows_y, rows_z = orbitals.shape
    domain = lax.axis_size("domain")
    cells_total = float(slab_width * rows_y * rows_z * domain)
    band = lax.axis_index("band")
    band_word = band.reshape(1).astype(jnp.int32)
    flat = (blocks, slab_width * rows_y, rows_z)
    big = flat[0] * flat[1] * flat[2]
    slab = jax.ShapeDtypeStruct(flat, F32)
    field = jax.ShapeDtypeStruct(orbitals.shape, F32)
    tile = jax.ShapeDtypeStruct((8, 128), F32)

    def inner_part(block, *sums):
        return call(
            inner_kernel,
            (field, *sums),
            specs=[VMEM] * 2,
            flops=60 * big,
            bytes_moved=8 * big,
        )(block, potential)

    own = orbitals.reshape(flat)
    quarters = [own[2 * k : 2 * k + 2] for k in range(4)]
    arrived = [
        lax.ppermute(quarters[k], "band", [(0, 2 * k), (1, 2 * k + 1)]) for k in (1, 3, 2)
    ]
    inner, sums = inner_part(orbitals, tile)
    arrived, inner, sums = lax.optimization_barrier((arrived, inner, sums))
    piece = jnp.where(band < 2, quarters[0], 0.0)
    for part in arrived:
        piece = piece + part
    left, right = neighbours(own)
    crossed = lax.ppermute(piece, "band", [(y, y + RING) for y in range(RING)])
    piece = jnp.where(band < RING, piece, crossed)

    def stage(fresh, imaged, pieces, *sums, last=False):
        sources = (*pieces, own, *((image,) if imaged else ()), *sums)
        return call(
            lambda *refs: stage_kernel(len(pieces), fresh, imaged, last, *refs),
            jax.ShapeDtypeStruct((domain, 8, 128), F32) if last else tile,
            specs=[VMEM] * len(sources),
            flops=20 * big,
            bytes_moved=10 * big,
        )(*sources)

    pieces = [piece]
    up, down = ring_shift(piece, 1), ring_shift(piece, -1)
    pieces += [up, down]
    up, down = ring_shift(up, 1), ring_shift(down, -1)
    sums = stage(range(6), (), pieces, sums)
    down, sums = lax.optimization_barrier((down, sums))
    pieces += [up, down]
    up, down = ring_shift(up, 1), ring_shift(down, -1)
    sums = stage(range(6, 10), (), pieces, sums)
    down, sums, left, right = lax.optimization_barrier((down, sums, left, right))
    pieces += [up, down]
    up, down = ring_shift(up[:1], 1), ring_shift(down[1:], -1)
    image, image_sums = call(
        image_kernel, (slab, tile), specs=[VMEM] * 4, flops=50 * big, bytes_moved=20 * big
    )(own, inner.reshape(flat), left, right)
    sums = stage(range(10, 14), range(14), pieces, sums, image_sums)
    pieces += [up, down]
    sums = stage(range(14, 16), range(14, 16), pieces, sums, last=True)
    sums = call(
        lambda *refs: total_kernel(cells_total, *refs),
        tile,
        specs=[VMEM],
        flops=40 * 1024,
        bytes_moved=160 * 1024,
    )(domain_parts(sums))
    basis, weights, gram = call(
        combine_kernel,
        (slab, tile, tile),
        scratch=[pltpu.VMEM((24, 8, 128), F32)],
        specs=[SMEM] + [VMEM] * 11,
        flops=48 * big,
        bytes_moved=16 * big,
    )(band_word, sums, *pieces, own)
    left, right = neighbours(basis)
    inner = inner_part(basis.reshape(orbitals.shape))[0].reshape(flat)
    shared, inner = lax.optimization_barrier((sums, inner))
    other = lax.ppermute(shared, "band", [(0, 1), (1, 0)])
    shared = jnp.stack([jnp.where(band == 0, shared, other), jnp.where(band == 0, other, shared)])
    shared = jnp.where(band < 2, shared, 0.0)
    shared = shared + lax.ppermute(shared, "band", [(0, 4), (1, 5)])
    shared = shared + lax.ppermute(shared, "band", [(0, 2), (1, 3), (4, 6), (5, 7)])
    far = lax.ppermute(shared, "band", [(y, y + RING) for y in range(RING)])
    splat = call(
        coeff_kernel, jax.ShapeDtypeStruct((8, 8, 128), F32), specs=[SMEM] + [VMEM] * 5
    )(band_word, weights, gram, sums, shared, far)
    residual = call(
        residual_kernel, slab, specs=[VMEM] * 5, flops=30 * big, bytes_moved=20 * big
    )(basis, inner, left, right, splat)
    return (basis.reshape(orbitals.shape), residual.reshape(orbitals.shape))


def solution(mesh):
    return jax.shard_map(
        local,
        mesh=mesh,
        in_specs=(P("band", "domain", None, None), P("domain", None, None)),
        out_specs=(P("band", "domain", None, None), P("band", "domain", None, None)),
        check_vma=False,
    )
```

```python
import jax
import jax.numpy as jnp
from jax import lax
from jax.experimental import pallas as pl
from jax.experimental.pallas import tpu as pltpu
from jax.sharding import PartitionSpec as P

stencil_weights = (-205.0 / 72.0, 8.0 / 5.0, -1.0 / 5.0, 8.0 / 315.0, -1.0 / 560.0)
BLK = 8
RING = 8
F32 = jnp.float32
VMEM = pl.BlockSpec(memory_space=pltpu.VMEM)
SMEM = pl.BlockSpec(memory_space=pltpu.SMEM)


def call(kernel, outs, scratch=(), specs=None, flops=0, bytes_moved=0):
    return pl.pallas_call(
        kernel,
        out_shape=outs,
        in_specs=specs,
        out_specs=jax.tree.map(lambda _: VMEM, outs),
        scratch_shapes=scratch,
        compiler_params=pltpu.CompilerParams(vmem_limit_bytes=32 * 1024 * 1024),
        cost_estimate=pl.CostEstimate(flops=flops, bytes_accessed=bytes_moved, transcendentals=0),
    )


def lanes():
    return lax.broadcasted_iota(jnp.int32, (8, 128), 1)


def subs():
    return lax.broadcasted_iota(jnp.int32, (8, 128), 0)


def pair_sums(jobs, load, chunks):
    lane = lanes()
    result = jnp.zeros((8, 128), F32)
    zero_row = jnp.zeros((1, 128), F32)
    for pairs in jobs:
        used = sorted({n for pair in pairs for n in pair})

        def body(c, sums, pairs=pairs, used=used):
            for step in range(4):
                rows = {n: load[n](4 * c + step) for n in used}
                sums = tuple(s + rows[q] * rows[r] for s, (q, r) in zip(sums, pairs))
            return sums

        zero = jnp.zeros((8, 128), F32)
        sums = lax.fori_loop(0, chunks // 4, body, (zero,) * len(pairs))
        columns = {}
        for s, (q, r) in zip(sums, pairs):
            rows = columns.setdefault(32 * (r // 8) + q, [zero_row] * 8)
            rows[r % 8] = jnp.sum(s, axis=0, keepdims=True)
        for place, rows in columns.items():
            column = jnp.sum(jnp.concatenate(rows, axis=0), axis=1, keepdims=True)
            result = result + jnp.where(lane == place, column, 0.0)
    return result


def loader(ref, index):
    return lambda c: ref[index, pl.ds(pl.multiple_of(c * 8, 8), 8), :]


def move(tile, source, target):
    lane = lanes()
    if source != target:
        tile = pltpu.roll(tile, (target - source) % 128, 1)
    return jnp.where((lane >= target) & (lane < target + 8), tile, 0.0)


def spread_lane(tile, k):
    return jnp.broadcast_to(tile[:, k : k + 1], (8, 128))


def rows_of(refs):
    return [(r, i) for r in refs for i in range(r.shape[0])]


def unpacked(sums):
    lane = lanes()
    parts = [sums] + [pltpu.roll(sums, 128 - 32 * n, 1) for n in (1, 2)]
    return [jnp.where(lane < 32, part, 0.0) for part in parts]


def tall(tiles):
    return jnp.concatenate(tiles + [jnp.zeros((128 - 8 * len(tiles), 128), F32)], axis=0)


OWN = list(range(16, 24))
IMAGE = list(range(24, 32))


def split(pairs, size=36):
    if not pairs:
        return []
    count = -(-len(pairs) // size)
    size = -(-len(pairs) // count)
    return [pairs[n : n + size] for n in range(0, len(pairs), size)]


def stage_kernel(parts, fresh, imaged, last, *refs):
    out = refs[-1]
    pieces, refs = refs[:parts], refs[parts:-1]
    own, image, before = (refs[0], refs[1], refs[2:]) if imaged else (refs[0], None, refs[1:])
    chunks = own.shape[1] // 8
    load = {n: loader(r, i) for n, (r, i) in enumerate(rows_of(pieces))}
    load |= {n: loader(own, n - 16) for n in OWN}
    if imaged:
        load |= {n: loader(image, n - 24) for n in IMAGE}
    jobs = split([(q, r) for q in OWN for r in fresh])
    jobs += split([(q, r) for q in fresh for r in range(q + 1)])
    jobs += split([(q, r) for q in IMAGE for r in imaged])
    total = pair_sums(jobs, load, chunks)
    for part in before:
        total = total + part[...]
    if last:
        for n in range(out.shape[0]):
            out[n] = total
    else:
        out[...] = total


def total_kernel(cells_total, parts_ref, out):
    out[...] = jnp.sum(parts_ref[...], axis=0) / cells_total


def combine_kernel(band_ref, sums_ref, *refs):
    *pieces, own, out, weights_ref, gram_ref, splat = refs
    band = band_ref[0]
    lane, sub = lanes(), subs()
    tiles = unpacked(sums_ref[...])
    turned = jnp.transpose(tall(tiles))
    w0, w1, w2 = (
        jnp.where(lane < 24, tile + jnp.where(lane == sub + 8 * n, 0.0, turned[8 * n : 8 * n + 8]), 0.0)
        for n, tile in enumerate(tiles)
    )
    later = band >= 2
    second = band == 1

    def taken(position):
        place = position & 7
        return later | (second & (place >= 2) & (place <= 5))

    row_in = taken(sub)
    lane_in = (lane >= 16) | taken(lane)
    kept = row_in & lane_in
    w0 = jnp.where(kept, w0, jnp.where(lane == sub, 1.0, 0.0))
    w1 = jnp.where(kept, w1, jnp.where(lane == 8 + sub, 1.0, 0.0))
    w0 = w0 + jnp.where(lane == 24 + sub, 1.0, 0.0)
    w1 = w1 + jnp.where(lane == 32 + sub, 1.0, 0.0)
    w2 = jnp.where(lane_in, w2, 0.0) + jnp.where(lane == 40 + sub, 1.0, 0.0)
    tiles = [w0, w1, w2]
    for k in range(16):
        v, s = divmod(k, 8)
        row = tiles[v][s : s + 1, :]
        row = row / jnp.broadcast_to(row[:, k : k + 1], (1, 128))
        row = jnp.broadcast_to(row, (8, 128))
        for u in range(v, 3):
            column = spread_lane(tiles[u], k)
            if u == v:
                column = jnp.where(sub > s, column, 0.0)
            tiles[u] = tiles[u] - column * row
    plain = tiles[2]
    scaled = plain
    for k in range(8):
        row = scaled[k : k + 1, :]
        row = row / jnp.broadcast_to(row[:, 16 + k : 17 + k], (1, 128))
        column = jnp.where(sub > k, spread_lane(scaled, 16 + k), 0.0)
        scaled = scaled - column * jnp.broadcast_to(row, (8, 128))
    pivots = jnp.sum(jnp.where(lane == 16 + sub, scaled, 0.0), axis=1, keepdims=True)
    scaled = scaled / jnp.sqrt(jnp.broadcast_to(pivots, (8, 128)))
    weights = jnp.where(later, plain, scaled)
    weights_ref[...] = weights
    gram_ref[...] = jnp.where(later, move(plain, 16, 0), jnp.where(lane == sub, 1.0, 0.0))
    for c in range(24):
        splat[c] = spread_lane(weights, 24 + c)
    rows = rows_of(pieces) + [(own, i) for i in range(BLK)]

    def body(c, carry):
        part = pl.ds(pl.multiple_of(c * 16, 16), 16)
        inputs = [r[i, part, :] for r, i in rows]
        for i in range(BLK):
            total = splat[0, pl.ds(i, 1), :] * inputs[0]
            for n in range(1, 24):
                total = total + splat[n, pl.ds(i, 1), :] * inputs[n]
            out[i, part, :] = total
        return carry

    lax.fori_loop(0, own.shape[1] // 16, body, 0)


def inner_kernel(f_ref, v_ref, out, *sums):
    def body(i, carry):
        layers = [f_ref[i, x] for x in range(4)]
        for x in range(4):
            here = layers[x]
            total = 3.0 * stencil_weights[0] * here
            for offset in range(1, 5):
                beside = pltpu.roll(here, offset, 0) + pltpu.roll(here, 64 - offset, 0)
                beside = beside + pltpu.roll(here, offset, 1) + pltpu.roll(here, 128 - offset, 1)
                if x + offset < 4:
                    beside = beside + layers[x + offset]
                if x - offset >= 0:
                    beside = beside + layers[x - offset]
                total = total + stencil_weights[offset] * beside
            out[i, x] = -0.5 * total + v_ref[x] * here
        return carry

    lax.fori_loop(0, BLK, body, 0)
    if sums:

        def row(i):
            return lambda c: f_ref[i, c // 8, pl.ds(pl.multiple_of((c % 8) * 8, 8), 8), :]

        load = {n: row(n - 16) for n in OWN}
        sums[0][...] = pair_sums([[(q, r) for q in OWN for r in range(16, q + 1)]], load, 32)


def edged(inner, x, left, right):
    total = None
    for offset in range(1, 5):
        if x + offset >= 4:
            term = stencil_weights[offset] * right(x + offset - 4)
            total = term if total is None else total + term
        if x - offset < 0:
            term = stencil_weights[offset] * left(x - offset + 4)
            total = term if total is None else total + term
    return inner - 0.5 * total


def image_kernel(own, inner, left, right, out, sums):
    def body(i, carry):
        for x in range(4):
            part = pl.ds(64 * x, 64)
            out[i, part, :] = edged(
                inner[i, part, :],
                x,
                lambda n: left[i, pl.ds(64 * n, 64), :],
                lambda n: right[i, pl.ds(64 * n, 64), :],
            )
        return carry

    lax.fori_loop(0, BLK, body, 0)
    load = {n: loader(own, n - 16) for n in OWN}
    load |= {n: loader(out, n - 24) for n in IMAGE}
    jobs = split([(q, r) for q in IMAGE for r in OWN], 32)
    sums[...] = pair_sums(jobs, load, own.shape[1] // 8)


def dot(left, right, turn_left=False, turn_right=False):
    dims = (((0 if turn_left else 1,), (1 if turn_right else 0,)), ((), ()))
    return lax.dot_general(
        left, right, dims, precision=lax.Precision.HIGHEST, preferred_element_type=F32
    )


def places(y, home=None):
    row = lax.broadcasted_iota(jnp.int32, (128, 128), 0)
    lane = lax.broadcasted_iota(jnp.int32, (128, 128), 1)
    distance = (row + 2) >> 2
    distance = jnp.where(((row + 2) & 2) == 0, -distance, distance)
    piece = (y + distance) & 7
    target = (piece & 1) * 8 + (piece >> 1) * 2 + (row & 1)
    if home is None:
        target = jnp.where(row < 16, target, row)
    else:
        target = jnp.where((piece & 1) == home, -1, target)
        target = jnp.where(row < 16, target, row - 16 + 8 * home)
    return jnp.where((lane == target) & (row < 24), 1.0, 0.0)


def coeff_kernel(band_ref, weights_ref, gram_ref, own_ref, near_ref, far_ref, out):
    lane, sub = lanes(), subs()
    wide = lax.broadcasted_iota(jnp.int32, (128, 128), 1)
    row = lax.broadcasted_iota(jnp.int32, (128, 128), 0)
    place = places(band_ref[0] & 7)
    weights = jnp.where(lane < 24, pltpu.roll(weights_ref[...], 104, 1), 0.0)
    weights = dot(weights, place)

    def image_columns(matrix, place, source, target):
        columns = dot(place, matrix, turn_left=True)
        columns = pltpu.roll(columns, (target - source) % 128, 1)
        return jnp.where((wide >= target) & (wide < target + 8), columns, 0.0)

    def visiting(n):
        packed = jnp.where(band_ref[0] < RING, near_ref[n], far_ref[n])
        return image_columns(tall(unpacked(packed)), places(n, n), 24, 8 * n)

    block0, block1 = visiting(0), visiting(1)
    block = image_columns(tall(unpacked(own_ref[...])), place, 24, 16)
    half = dot(weights, block0 + block1 + block)
    half = half + dot(weights, jnp.where(row < 16, block, 0.0), turn_right=True)
    theta = dot(half, tall([weights]), turn_right=True)
    work = gram_ref[...] + move(theta, 0, 8)
    for k in range(8):
        line = work[k : k + 1, :]
        line = jnp.broadcast_to(line / jnp.broadcast_to(line[:, k : k + 1], (1, 128)), (8, 128))
        work = jnp.where(sub == k, line, work - spread_lane(work, k) * line)
    for j in range(8):
        out[j] = spread_lane(work, 8 + j)


def residual_kernel(f_ref, inner_ref, left_ref, right_ref, splat, out):
    def body(c, carry):
        def part(x):
            return pl.ds(pl.multiple_of(64 * x + 8 * c, 8), 8)

        for x in range(4):
            inputs = [f_ref[i, part(x), :] for i in range(BLK)]
            for j in range(BLK):
                total = edged(
                    inner_ref[j, part(x), :],
                    x,
                    lambda n: left_ref[j, part(n), :],
                    lambda n: right_ref[j, part(n), :],
                )
                for i in range(BLK):
                    total = total - splat[j, pl.ds(i, 1), :] * inputs[i]
                out[j, part(x), :] = total
        return carry

    lax.fori_loop(0, 8, body, 0)


def domain_parts(copies):
    return lax.all_to_all(copies, "domain", 0, 0)


def ring_shift(block, step):
    pairs = [(z * RING + y, z * RING + (y + step) % RING) for z in range(2) for y in range(RING)]
    return lax.ppermute(block, "band", pairs)


def neighbours(block):
    count = lax.axis_size("domain")
    left = lax.ppermute(block, "domain", [(i, (i + 1) % count) for i in range(count)])
    right = lax.ppermute(block, "domain", [((i + 1) % count, i) for i in range(count)])
    return left, right


def local(orbitals, potential):
    blocks, slab_width, rows_y, rows_z = orbitals.shape
    domain = lax.axis_size("domain")
    cells_total = float(slab_width * rows_y * rows_z * domain)
    band = lax.axis_index("band")
    band_word = band.reshape(1).astype(jnp.int32)
    flat = (blocks, slab_width * rows_y, rows_z)
    big = flat[0] * flat[1] * flat[2]
    slab = jax.ShapeDtypeStruct(flat, F32)
    field = jax.ShapeDtypeStruct(orbitals.shape, F32)
    tile = jax.ShapeDtypeStruct((8, 128), F32)

    def inner_part(block, *sums):
        return call(
            inner_kernel,
            (field, *sums),
            specs=[VMEM] * 2,
            flops=60 * big,
            bytes_moved=8 * big,
        )(block, potential)

    own = orbitals.reshape(flat)
    quarters = [own[2 * k : 2 * k + 2] for k in range(4)]
    arrived = [
        lax.ppermute(quarters[k], "band", [(0, place), (1, place + 1)])
        for k, place in ((2, RING + 4), (1, 2), (3, 6))
    ]
    inner, sums = inner_part(orbitals, tile)
    arrived, inner, sums = lax.optimization_barrier((arrived, inner, sums))
    piece = jnp.where(band < 2, quarters[0], 0.0)
    for part in arrived:
        piece = piece + part
    left, right = neighbours(own)
    far_first = (4, 5)
    pairs = [(y + RING, y) if y in far_first else (y, y + RING) for y in range(RING)]
    crossed = lax.ppermute(piece, "band", pairs)
    at_first = (band < RING) != (((band & 7) == 4) | ((band & 7) == 5))
    piece = jnp.where(at_first, piece, crossed)

    def stage(fresh, imaged, pieces, *sums, last=False):
        sources = (*pieces, own, *((image,) if imaged else ()), *sums)
        return call(
            lambda *refs: stage_kernel(len(pieces), fresh, imaged, last, *refs),
            jax.ShapeDtypeStruct((domain, 8, 128), F32) if last else tile,
            specs=[VMEM] * len(sources),
            flops=20 * big,
            bytes_moved=10 * big,
        )(*sources)

    pieces = [piece]
    up, down = ring_shift(piece, 1), ring_shift(piece, -1)
    pieces += [up, down]
    up, down = ring_shift(up, 1), ring_shift(down, -1)
    sums = stage(range(6), (), pieces, sums)
    down, sums = lax.optimization_barrier((down, sums))
    pieces += [up, down]
    up, down = ring_shift(up, 1), ring_shift(down, -1)
    sums = stage(range(6, 10), (), pieces, sums)
    down, sums, left, right = lax.optimization_barrier((down, sums, left, right))
    pieces += [up, down]
    up, down = ring_shift(up[:1], 1), ring_shift(down[1:], -1)
    image, image_sums = call(
        image_kernel, (slab, tile), specs=[VMEM] * 4, flops=50 * big, bytes_moved=20 * big
    )(own, inner.reshape(flat), left, right)
    sums = stage(range(10, 14), range(14), pieces, sums, image_sums)
    pieces += [up, down]
    sums = stage(range(14, 16), range(14, 16), pieces, sums, last=True)
    sums = call(
        lambda *refs: total_kernel(cells_total, *refs),
        tile,
        specs=[VMEM],
        flops=40 * 1024,
        bytes_moved=160 * 1024,
    )(domain_parts(sums))
    basis, weights, gram = call(
        combine_kernel,
        (slab, tile, tile),
        scratch=[pltpu.VMEM((24, 8, 128), F32)],
        specs=[SMEM] + [VMEM] * 11,
        flops=48 * big,
        bytes_moved=16 * big,
    )(band_word, sums, *pieces, own)
    left, right = neighbours(basis)
    inner = inner_part(basis.reshape(orbitals.shape))[0].reshape(flat)
    shared, inner = lax.optimization_barrier((sums, inner))
    other = lax.ppermute(shared, "band", [(0, 1), (1, 0)])
    shared = jnp.stack([jnp.where(band == 0, shared, other), jnp.where(band == 0, other, shared)])
    shared = jnp.where(band < 2, shared, 0.0)
    shared = shared + lax.ppermute(shared, "band", [(0, 4), (1, 5)])
    shared = shared + lax.ppermute(shared, "band", [(0, 2), (1, 3), (4, 6), (5, 7)])
    far = lax.ppermute(shared, "band", [(y, y + RING) for y in range(RING)])
    splat = call(
        coeff_kernel, jax.ShapeDtypeStruct((8, 8, 128), F32), specs=[SMEM] + [VMEM] * 5
    )(band_word, weights, gram, sums, shared, far)
    residual = call(
        residual_kernel, slab, specs=[VMEM] * 5, flops=30 * big, bytes_moved=20 * big
    )(basis, inner, left, right, splat)
    return (basis.reshape(orbitals.shape), residual.reshape(orbitals.shape))


def solution(mesh):
    return jax.shard_map(
        local,
        mesh=mesh,
        in_specs=(P("band", "domain", None, None), P("domain", None, None)),
        out_specs=(P("band", "domain", None, None), P("band", "domain", None, None)),
        check_vma=False,
    )
```

```python
import jax
import jax.numpy as jnp
from jax import lax
from jax.experimental import pallas as pl
from jax.experimental.pallas import tpu as pltpu
from jax.sharding import PartitionSpec as P

stencil_weights = (-205.0 / 72.0, 8.0 / 5.0, -1.0 / 5.0, 8.0 / 315.0, -1.0 / 560.0)
BLK = 8
RING = 8
F32 = jnp.float32
VMEM = pl.BlockSpec(memory_space=pltpu.VMEM)
SMEM = pl.BlockSpec(memory_space=pltpu.SMEM)


def call(kernel, outs, scratch=(), specs=None, flops=0, bytes_moved=0):
    return pl.pallas_call(
        kernel,
        out_shape=outs,
        in_specs=specs,
        out_specs=jax.tree.map(lambda _: VMEM, outs),
        scratch_shapes=scratch,
        compiler_params=pltpu.CompilerParams(vmem_limit_bytes=32 * 1024 * 1024),
        cost_estimate=pl.CostEstimate(flops=flops, bytes_accessed=bytes_moved, transcendentals=0),
    )


def lanes():
    return lax.broadcasted_iota(jnp.int32, (8, 128), 1)


def subs():
    return lax.broadcasted_iota(jnp.int32, (8, 128), 0)


def folded(rows):
    sub = subs()
    step = 4
    while step:
        lower = (sub & step) == 0
        merged = []
        for first, second in zip(rows[:step], rows[step:]):
            if first is not None:
                first = first + pltpu.roll(first, 8 - step, 0)
            if second is not None:
                second = second + pltpu.roll(second, step, 0)
            if first is None and second is None:
                merged.append(None)
            else:
                merged.append(
                    jnp.where(lower, 0.0 if first is None else first, 0.0 if second is None else second)
                )
        rows = merged
        step //= 2
    return rows[0]


def pair_sums(jobs, load, chunks):
    lane = lanes()
    result = jnp.zeros((8, 128), F32)
    for pairs in jobs:
        used = sorted({n for pair in pairs for n in pair})

        def body(c, sums, pairs=pairs, used=used):
            for step in range(4):
                rows = {n: load[n](4 * c + step) for n in used}
                sums = tuple(s + rows[q] * rows[r] for s, (q, r) in zip(sums, pairs))
            return sums

        zero = jnp.zeros((8, 128), F32)
        sums = lax.fori_loop(0, chunks // 4, body, (zero,) * len(pairs))
        columns = {}
        for s, (q, r) in zip(sums, pairs):
            columns.setdefault(32 * (r // 8) + q, [None] * 8)[r % 8] = s
        for place, rows in columns.items():
            column = jnp.sum(folded(rows), axis=1, keepdims=True)
            result = result + jnp.where(lane == place, column, 0.0)
    return result


def loader(ref, index):
    return lambda c: ref[index, pl.ds(pl.multiple_of(c * 8, 8), 8), :]


def move(tile, source, target):
    lane = lanes()
    if source != target:
        tile = pltpu.roll(tile, (target - source) % 128, 1)
    return jnp.where((lane >= target) & (lane < target + 8), tile, 0.0)


def spread_lane(tile, k):
    return jnp.broadcast_to(tile[:, k : k + 1], (8, 128))


def rows_of(refs):
    return [(r, i) for r in refs for i in range(r.shape[0])]


def unpacked(sums):
    lane = lanes()
    parts = [sums] + [pltpu.roll(sums, 128 - 32 * n, 1) for n in (1, 2)]
    return [jnp.where(lane < 32, part, 0.0) for part in parts]


def tall(tiles):
    return jnp.concatenate(tiles + [jnp.zeros((128 - 8 * len(tiles), 128), F32)], axis=0)


OWN = list(range(16, 24))
IMAGE = list(range(24, 32))


def split(pairs, size=36):
    if not pairs:
        return []
    count = -(-len(pairs) // size)
    size = -(-len(pairs) // count)
    return [pairs[n : n + size] for n in range(0, len(pairs), size)]


def stage_kernel(parts, fresh, imaged, last, *refs):
    out = refs[-1]
    pieces, refs = refs[:parts], refs[parts:-1]
    own, image, before = (refs[0], refs[1], refs[2:]) if imaged else (refs[0], None, refs[1:])
    chunks = own.shape[1] // 8
    load = {n: loader(r, i) for n, (r, i) in enumerate(rows_of(pieces))}
    load |= {n: loader(own, n - 16) for n in OWN}
    if imaged:
        load |= {n: loader(image, n - 24) for n in IMAGE}
    jobs = split([(q, r) for q in OWN for r in fresh])
    jobs += split([(q, r) for q in fresh for r in range(q + 1)])
    jobs += split([(q, r) for q in IMAGE for r in imaged])
    total = pair_sums(jobs, load, chunks)
    for part in before:
        total = total + part[...]
    if last:
        for n in range(out.shape[0]):
            out[n] = total
    else:
        out[...] = total


def total_kernel(cells_total, parts_ref, out):
    out[...] = jnp.sum(parts_ref[...], axis=0) / cells_total


def combine_kernel(band_ref, sums_ref, *refs):
    *pieces, own, out, weights_ref, gram_ref, splat = refs
    band = band_ref[0]
    lane, sub = lanes(), subs()
    tiles = unpacked(sums_ref[...])
    turned = jnp.transpose(tall(tiles))
    w0, w1, w2 = (
        jnp.where(lane < 24, tile + jnp.where(lane == sub + 8 * n, 0.0, turned[8 * n : 8 * n + 8]), 0.0)
        for n, tile in enumerate(tiles)
    )
    later = band >= 2
    second = band == 1

    def taken(position):
        place = position & 7
        return later | (second & (place >= 2) & (place <= 5))

    row_in = taken(sub)
    lane_in = (lane >= 16) | taken(lane)
    kept = row_in & lane_in
    w0 = jnp.where(kept, w0, jnp.where(lane == sub, 1.0, 0.0))
    w1 = jnp.where(kept, w1, jnp.where(lane == 8 + sub, 1.0, 0.0))
    w0 = w0 + jnp.where(lane == 24 + sub, 1.0, 0.0)
    w1 = w1 + jnp.where(lane == 32 + sub, 1.0, 0.0)
    w2 = jnp.where(lane_in, w2, 0.0) + jnp.where(lane == 40 + sub, 1.0, 0.0)
    tiles = [w0, w1, w2]
    for k in range(16):
        v, s = divmod(k, 8)
        row = tiles[v][s : s + 1, :]
        row = row / jnp.broadcast_to(row[:, k : k + 1], (1, 128))
        row = jnp.broadcast_to(row, (8, 128))
        for u in range(v, 3):
            column = spread_lane(tiles[u], k)
            if u == v:
                column = jnp.where(sub > s, column, 0.0)
            tiles[u] = tiles[u] - column * row
    plain = tiles[2]
    scaled = plain
    for k in range(8):
        row = scaled[k : k + 1, :]
        row = row / jnp.broadcast_to(row[:, 16 + k : 17 + k], (1, 128))
        column = jnp.where(sub > k, spread_lane(scaled, 16 + k), 0.0)
        scaled = scaled - column * jnp.broadcast_to(row, (8, 128))
    pivots = jnp.sum(jnp.where(lane == 16 + sub, scaled, 0.0), axis=1, keepdims=True)
    scaled = scaled / jnp.sqrt(jnp.broadcast_to(pivots, (8, 128)))
    weights = jnp.where(later, plain, scaled)
    weights_ref[...] = weights
    gram_ref[...] = jnp.where(later, move(plain, 16, 0), jnp.where(lane == sub, 1.0, 0.0))
    for c in range(24):
        splat[c] = spread_lane(weights, 24 + c)
    rows = rows_of(pieces) + [(own, i) for i in range(BLK)]

    def combine(places, plus_own):
        def body(c, carry):
            part = pl.ds(pl.multiple_of(c * 32, 32), 32)
            for low in (0, 4):
                if plus_own:
                    totals = [own[low + k, part, :] for k in range(4)]
                else:
                    totals = [jnp.zeros((32, 128), F32)] * 4
                for n in places:
                    r, i = rows[n]
                    cells = r[i, part, :]
                    totals = [
                        t + splat[n, pl.ds(low + k, 1), :] * cells for k, t in enumerate(totals)
                    ]
                for k in range(4):
                    out[low + k, part, :] = totals[k]
            return carry

        lax.fori_loop(0, own.shape[1] // 32, body, 0)

    pl.when(later)(lambda: combine(range(16), True))
    pl.when(second)(lambda: combine((2, 3, 4, 5, 10, 11, 12, 13, *OWN), False))
    pl.when(band == 0)(lambda: combine(OWN, False))


def inner_kernel(f_ref, v_ref, out, *sums):
    def body(i, carry):
        layers = [f_ref[i, x] for x in range(4)]
        for x in range(4):
            here = layers[x]
            total = 3.0 * stencil_weights[0] * here
            for offset in range(1, 5):
                beside = pltpu.roll(here, offset, 0) + pltpu.roll(here, 64 - offset, 0)
                beside = beside + pltpu.roll(here, offset, 1) + pltpu.roll(here, 128 - offset, 1)
                if x + offset < 4:
                    beside = beside + layers[x + offset]
                if x - offset >= 0:
                    beside = beside + layers[x - offset]
                total = total + stencil_weights[offset] * beside
            out[i, x] = -0.5 * total + v_ref[x] * here
        return carry

    lax.fori_loop(0, BLK, body, 0)
    if sums:

        def row(i):
            return lambda c: f_ref[i, c // 8, pl.ds(pl.multiple_of((c % 8) * 8, 8), 8), :]

        load = {n: row(n - 16) for n in OWN}
        sums[0][...] = pair_sums([[(q, r) for q in OWN for r in range(16, q + 1)]], load, 32)


def edged(inner, x, left, right):
    total = None
    for offset in range(1, 5):
        if x + offset >= 4:
            term = stencil_weights[offset] * right(x + offset - 4)
            total = term if total is None else total + term
        if x - offset < 0:
            term = stencil_weights[offset] * left(x - offset + 4)
            total = term if total is None else total + term
    return inner - 0.5 * total


def image_kernel(own, inner, left, right, out, sums):
    def body(i, carry):
        for x in range(4):
            part = pl.ds(64 * x, 64)
            out[i, part, :] = edged(
                inner[i, part, :],
                x,
                lambda n: left[i, pl.ds(64 * n, 64), :],
                lambda n: right[i, pl.ds(64 * n, 64), :],
            )
        return carry

    lax.fori_loop(0, BLK, body, 0)
    load = {n: loader(own, n - 16) for n in OWN}
    load |= {n: loader(out, n - 24) for n in IMAGE}
    jobs = [[(q, r) for q in IMAGE for r in OWN if r <= q - 8]]
    sums[...] = pair_sums(jobs, load, own.shape[1] // 8)


def dot(left, right, turn_left=False, turn_right=False):
    dims = (((0 if turn_left else 1,), (1 if turn_right else 0,)), ((), ()))
    return lax.dot_general(
        left, right, dims, precision=lax.Precision.HIGHEST, preferred_element_type=F32
    )


def places(y, home=None):
    row = lax.broadcasted_iota(jnp.int32, (128, 128), 0)
    lane = lax.broadcasted_iota(jnp.int32, (128, 128), 1)
    distance = (row + 2) >> 2
    distance = jnp.where(((row + 2) & 2) == 0, -distance, distance)
    piece = (y + distance) & 7
    target = (piece & 1) * 8 + (piece >> 1) * 2 + (row & 1)
    if home is None:
        target = jnp.where(row < 16, target, row)
    else:
        target = jnp.where((piece & 1) == home, -1, target)
        target = jnp.where(row < 16, target, row - 16 + 8 * home)
    return jnp.where((lane == target) & (row < 24), 1.0, 0.0)


def coeff_kernel(band_ref, weights_ref, gram_ref, own_ref, near_ref, far_ref, out):
    lane, sub = lanes(), subs()
    wide = lax.broadcasted_iota(jnp.int32, (128, 128), 1)
    row = lax.broadcasted_iota(jnp.int32, (128, 128), 0)
    place = places(band_ref[0] & 7)
    weights = jnp.where(lane < 24, pltpu.roll(weights_ref[...], 104, 1), 0.0)
    weights = dot(weights, place)

    def with_mirror(packed):
        tiles = unpacked(packed)
        mirror = jnp.transpose(tall([move(tiles[2], 24, 0)]))[0:8]
        tiles[2] = tiles[2] + move(jnp.where(lane == sub, 0.0, mirror), 0, 24)
        return tall(tiles)

    def image_columns(matrix, place, source, target):
        columns = dot(place, matrix, turn_left=True)
        columns = pltpu.roll(columns, (target - source) % 128, 1)
        return jnp.where((wide >= target) & (wide < target + 8), columns, 0.0)

    def visiting(n):
        packed = jnp.where(band_ref[0] < RING, near_ref[n], far_ref[n])
        return image_columns(with_mirror(packed), places(n, n), 24, 8 * n)

    block0, block1 = visiting(0), visiting(1)
    block = image_columns(with_mirror(own_ref[...]), place, 24, 16)
    half = dot(weights, block0 + block1 + block)
    half = half + dot(weights, jnp.where(row < 16, block, 0.0), turn_right=True)
    theta = dot(half, tall([weights]), turn_right=True)
    work = gram_ref[...] + move(theta, 0, 8)
    for k in range(8):
        line = work[k : k + 1, :]
        line = jnp.broadcast_to(line / jnp.broadcast_to(line[:, k : k + 1], (1, 128)), (8, 128))
        work = jnp.where(sub == k, line, work - spread_lane(work, k) * line)
    for j in range(8):
        out[j] = spread_lane(work, 8 + j)


def partial_kernel(f_ref, inner_ref, splat, out):
    def body(c, carry):
        part = pl.ds(pl.multiple_of(c * 32, 32), 32)
        for low in (0, 4):
            totals = [inner_ref[low + k, part, :] for k in range(4)]
            for i in range(BLK):
                cells = f_ref[i, part, :]
                totals = [
                    t - splat[low + k, pl.ds(i, 1), :] * cells for k, t in enumerate(totals)
                ]
            for k in range(4):
                out[low + k, part, :] = totals[k]
        return carry

    lax.fori_loop(0, f_ref.shape[1] // 32, body, 0)


def edge_kernel(partial_ref, left_ref, right_ref, out):
    def body(i, carry):
        for x in range(4):
            part = pl.ds(64 * x, 64)
            out[i, part, :] = edged(
                partial_ref[i, part, :],
                x,
                lambda n: left_ref[i, pl.ds(64 * n, 64), :],
                lambda n: right_ref[i, pl.ds(64 * n, 64), :],
            )
        return carry

    lax.fori_loop(0, BLK, body, 0)


def domain_parts(copies):
    return lax.all_to_all(copies, "domain", 0, 0)


def ring_shift(block, step):
    pairs = [(z * RING + y, z * RING + (y + step) % RING) for z in range(2) for y in range(RING)]
    return lax.ppermute(block, "band", pairs)


def neighbours(block):
    count = lax.axis_size("domain")
    left = lax.ppermute(block, "domain", [(i, (i + 1) % count) for i in range(count)])
    right = lax.ppermute(block, "domain", [((i + 1) % count, i) for i in range(count)])
    return left, right


def local(orbitals, potential):
    blocks, slab_width, rows_y, rows_z = orbitals.shape
    domain = lax.axis_size("domain")
    cells_total = float(slab_width * rows_y * rows_z * domain)
    band = lax.axis_index("band")
    band_word = band.reshape(1).astype(jnp.int32)
    flat = (blocks, slab_width * rows_y, rows_z)
    big = flat[0] * flat[1] * flat[2]
    slab = jax.ShapeDtypeStruct(flat, F32)
    field = jax.ShapeDtypeStruct(orbitals.shape, F32)
    tile = jax.ShapeDtypeStruct((8, 128), F32)

    def inner_part(block, *sums):
        return call(
            inner_kernel,
            (field, *sums),
            specs=[VMEM] * 2,
            flops=60 * big,
            bytes_moved=8 * big,
        )(block, potential)

    own = orbitals.reshape(flat)
    quarters = [own[2 * k : 2 * k + 2] for k in range(4)]
    arrived = [
        lax.ppermute(quarters[k], "band", [(0, 2 * k), (1, 2 * k + 1)]) for k in (1, 3, 2)
    ]
    inner, sums = inner_part(orbitals, tile)
    arrived, inner, sums = lax.optimization_barrier((arrived, inner, sums))
    piece = jnp.where(band < 2, quarters[0], 0.0)
    for part in arrived:
        piece = piece + part
    left, right = neighbours(own)
    crossed = lax.ppermute(piece, "band", [(y, y + RING) for y in range(RING)])
    piece = jnp.where(band < RING, piece, crossed)

    def stage(fresh, imaged, pieces, *sums, last=False):
        sources = (*pieces, own, *((image,) if imaged else ()), *sums)
        return call(
            lambda *refs: stage_kernel(len(pieces), fresh, imaged, last, *refs),
            jax.ShapeDtypeStruct((domain, 8, 128), F32) if last else tile,
            specs=[VMEM] * len(sources),
            flops=20 * big,
            bytes_moved=10 * big,
        )(*sources)

    pieces = [piece]
    up, down = ring_shift(piece, 1), ring_shift(piece, -1)
    pieces += [up, down]
    up, down = ring_shift(up, 1), ring_shift(down, -1)
    sums = stage(range(6), (), pieces, sums)
    down, sums = lax.optimization_barrier((down, sums))
    pieces += [up, down]
    up, down = ring_shift(up, 1), ring_shift(down, -1)
    sums = stage(range(6, 10), (), pieces, sums)
    down, sums, left, right = lax.optimization_barrier((down, sums, left, right))
    pieces += [up, down]
    up, down = ring_shift(up[:1], 1), ring_shift(down[1:], -1)
    image, image_sums = call(
        image_kernel, (slab, tile), specs=[VMEM] * 4, flops=50 * big, bytes_moved=20 * big
    )(own, inner.reshape(flat), left, right)
    sums = stage(range(10, 14), range(14), pieces, sums, image_sums)
    pieces += [up, down]
    sums = stage(range(14, 16), range(14, 16), pieces, sums, last=True)
    sums = call(
        lambda *refs: total_kernel(cells_total, *refs),
        tile,
        specs=[VMEM],
        flops=40 * 1024,
        bytes_moved=160 * 1024,
    )(domain_parts(sums))
    basis, weights, gram = call(
        combine_kernel,
        (slab, tile, tile),
        scratch=[pltpu.VMEM((24, 8, 128), F32)],
        specs=[SMEM] + [VMEM] * 11,
        flops=48 * big,
        bytes_moved=16 * big,
    )(band_word, sums, *pieces, own)
    left, right = neighbours(basis)
    inner = inner_part(basis.reshape(orbitals.shape))[0].reshape(flat)
    shared = sums
    other = lax.ppermute(shared, "band", [(0, 1), (1, 0)])
    shared = jnp.stack([jnp.where(band == 0, shared, other), jnp.where(band == 0, other, shared)])
    shared = jnp.where(band < 2, shared, 0.0)
    shared = shared + lax.ppermute(shared, "band", [(0, 4), (1, 5)])
    shared = shared + lax.ppermute(shared, "band", [(0, 2), (1, 3), (4, 6), (5, 7)])
    shared, inner = lax.optimization_barrier((shared, inner))
    far = lax.ppermute(shared, "band", [(y, y + RING) for y in range(RING)])
    splat = call(
        coeff_kernel, jax.ShapeDtypeStruct((8, 8, 128), F32), specs=[SMEM] + [VMEM] * 5
    )(band_word, weights, gram, sums, shared, far)
    partial = call(
        partial_kernel, slab, specs=[VMEM] * 3, flops=16 * big, bytes_moved=12 * big
    )(basis, inner, splat)
    residual = call(
        edge_kernel, slab, specs=[VMEM] * 3, flops=20 * big, bytes_moved=16 * big
    )(partial, left, right)
    return (basis.reshape(orbitals.shape), residual.reshape(orbitals.shape))


def solution(mesh):
    return jax.shard_map(
        local,
        mesh=mesh,
        in_specs=(P("band", "domain", None, None), P("domain", None, None)),
        out_specs=(P("band", "domain", None, None), P("band", "domain", None, None)),
        check_vma=False,
    )
```

```python
import jax
import jax.numpy as jnp
from jax import lax
from jax.experimental import pallas as pl
from jax.experimental.pallas import tpu as pltpu
from jax.sharding import PartitionSpec as P

stencil_weights = (-205.0 / 72.0, 8.0 / 5.0, -1.0 / 5.0, 8.0 / 315.0, -1.0 / 560.0)
BLK = 8
RING = 8
F32 = jnp.float32
VMEM = pl.BlockSpec(memory_space=pltpu.VMEM)
SMEM = pl.BlockSpec(memory_space=pltpu.SMEM)


def call(kernel, outs, scratch=(), specs=None, flops=0, bytes_moved=0):
    return pl.pallas_call(
        kernel,
        out_shape=outs,
        in_specs=specs,
        out_specs=jax.tree.map(lambda _: VMEM, outs),
        scratch_shapes=scratch,
        compiler_params=pltpu.CompilerParams(vmem_limit_bytes=32 * 1024 * 1024),
        cost_estimate=pl.CostEstimate(flops=flops, bytes_accessed=bytes_moved, transcendentals=0),
    )


def lanes():
    return lax.broadcasted_iota(jnp.int32, (8, 128), 1)


def subs():
    return lax.broadcasted_iota(jnp.int32, (8, 128), 0)


def folded(rows):
    sub = subs()
    step = 4
    while step:
        lower = (sub & step) == 0
        merged = []
        for first, second in zip(rows[:step], rows[step:]):
            if first is not None:
                first = first + pltpu.roll(first, 8 - step, 0)
            if second is not None:
                second = second + pltpu.roll(second, step, 0)
            if first is None and second is None:
                merged.append(None)
            else:
                merged.append(
                    jnp.where(lower, 0.0 if first is None else first, 0.0 if second is None else second)
                )
        rows = merged
        step //= 2
    return rows[0]


def pair_sums(jobs, load, chunks):
    lane = lanes()
    result = jnp.zeros((8, 128), F32)
    for pairs in jobs:
        used = sorted({n for pair in pairs for n in pair})

        def body(c, sums, pairs=pairs, used=used):
            for step in range(4):
                rows = {n: load[n](4 * c + step) for n in used}
                sums = tuple(s + rows[q] * rows[r] for s, (q, r) in zip(sums, pairs))
            return sums

        zero = jnp.zeros((8, 128), F32)
        sums = lax.fori_loop(0, chunks // 4, body, (zero,) * len(pairs))
        columns = {}
        for s, (q, r) in zip(sums, pairs):
            columns.setdefault(32 * (r // 8) + q, [None] * 8)[r % 8] = s
        for place, rows in columns.items():
            column = jnp.sum(folded(rows), axis=1, keepdims=True)
            result = result + jnp.where(lane == place, column, 0.0)
    return result


def loader(ref, index):
    return lambda c: ref[index, pl.ds(pl.multiple_of(c * 8, 8), 8), :]


def move(tile, source, target):
    lane = lanes()
    if source != target:
        tile = pltpu.roll(tile, (target - source) % 128, 1)
    return jnp.where((lane >= target) & (lane < target + 8), tile, 0.0)


def spread_lane(tile, k):
    return jnp.broadcast_to(tile[:, k : k + 1], (8, 128))


def rows_of(refs):
    return [(r, i) for r in refs for i in range(r.shape[0])]


def unpacked(sums):
    lane = lanes()
    parts = [sums] + [pltpu.roll(sums, 128 - 32 * n, 1) for n in (1, 2)]
    return [jnp.where(lane < 32, part, 0.0) for part in parts]


def tall(tiles):
    return jnp.concatenate(tiles + [jnp.zeros((128 - 8 * len(tiles), 128), F32)], axis=0)


OWN = list(range(16, 24))
IMAGE = list(range(24, 32))


def split(pairs, size=36):
    if not pairs:
        return []
    count = -(-len(pairs) // size)
    size = -(-len(pairs) // count)
    return [pairs[n : n + size] for n in range(0, len(pairs), size)]


def stage_kernel(parts, fresh, imaged, last, *refs):
    out = refs[-1]
    pieces, refs = refs[:parts], refs[parts:-1]
    own, image, before = (refs[0], refs[1], refs[2:]) if imaged else (refs[0], None, refs[1:])
    chunks = own.shape[1] // 8
    load = {n: loader(r, i) for n, (r, i) in enumerate(rows_of(pieces))}
    load |= {n: loader(own, n - 16) for n in OWN}
    if imaged:
        load |= {n: loader(image, n - 24) for n in IMAGE}
    jobs = split([(q, r) for q in OWN for r in fresh])
    jobs += split([(q, r) for q in fresh for r in range(q + 1)])
    jobs += split([(q, r) for q in IMAGE for r in imaged])
    total = pair_sums(jobs, load, chunks)
    for part in before:
        total = total + part[...]
    if last:
        for n in range(out.shape[0]):
            out[n] = total
    else:
        out[...] = total


def total_kernel(cells_total, parts_ref, out):
    out[...] = jnp.sum(parts_ref[...], axis=0) / cells_total


def combine_kernel(band_ref, sums_ref, *refs):
    *pieces, own, out, weights_ref, gram_ref, splat = refs
    band = band_ref[0]
    lane, sub = lanes(), subs()
    tiles = unpacked(sums_ref[...])
    turned = jnp.transpose(tall(tiles))
    w0, w1, w2 = (
        jnp.where(lane < 24, tile + jnp.where(lane == sub + 8 * n, 0.0, turned[8 * n : 8 * n + 8]), 0.0)
        for n, tile in enumerate(tiles)
    )
    later = band >= 2
    second = band == 1

    def taken(position):
        place = position & 7
        return later | (second & (place >= 2) & (place <= 5))

    row_in = taken(sub)
    lane_in = (lane >= 16) | taken(lane)
    kept = row_in & lane_in
    w0 = jnp.where(kept, w0, jnp.where(lane == sub, 1.0, 0.0))
    w1 = jnp.where(kept, w1, jnp.where(lane == 8 + sub, 1.0, 0.0))
    w0 = w0 + jnp.where(lane == 24 + sub, 1.0, 0.0)
    w1 = w1 + jnp.where(lane == 32 + sub, 1.0, 0.0)
    w2 = jnp.where(lane_in, w2, 0.0) + jnp.where(lane == 40 + sub, 1.0, 0.0)
    tiles = [w0, w1, w2]
    for k in range(16):
        v, s = divmod(k, 8)
        row = tiles[v][s : s + 1, :]
        row = row / jnp.broadcast_to(row[:, k : k + 1], (1, 128))
        row = jnp.broadcast_to(row, (8, 128))
        for u in range(v, 3):
            column = spread_lane(tiles[u], k)
            if u == v:
                column = jnp.where(sub > s, column, 0.0)
            tiles[u] = tiles[u] - column * row
    plain = tiles[2]
    scaled = plain
    for k in range(8):
        row = scaled[k : k + 1, :]
        row = row / jnp.broadcast_to(row[:, 16 + k : 17 + k], (1, 128))
        column = jnp.where(sub > k, spread_lane(scaled, 16 + k), 0.0)
        scaled = scaled - column * jnp.broadcast_to(row, (8, 128))
    pivots = jnp.sum(jnp.where(lane == 16 + sub, scaled, 0.0), axis=1, keepdims=True)
    scaled = scaled / jnp.sqrt(jnp.broadcast_to(pivots, (8, 128)))
    weights = jnp.where(later, plain, scaled)
    weights_ref[...] = weights
    gram_ref[...] = jnp.where(later, move(plain, 16, 0), jnp.where(lane == sub, 1.0, 0.0))
    for c in range(24):
        splat[c] = spread_lane(weights, 24 + c)
    rows = rows_of(pieces) + [(own, i) for i in range(BLK)]

    def combine(places, plus_own):
        def body(c, carry):
            part = pl.ds(pl.multiple_of(c * 32, 32), 32)
            for low in (0, 4):
                if plus_own:
                    totals = [own[low + k, part, :] for k in range(4)]
                else:
                    totals = [jnp.zeros((32, 128), F32)] * 4
                for n in places:
                    r, i = rows[n]
                    cells = r[i, part, :]
                    totals = [
                        t + splat[n, pl.ds(low + k, 1), :] * cells for k, t in enumerate(totals)
                    ]
                for k in range(4):
                    out[low + k, part, :] = totals[k]
            return carry

        lax.fori_loop(0, own.shape[1] // 32, body, 0)

    pl.when(later)(lambda: combine(range(16), True))
    pl.when(second)(lambda: combine((2, 3, 4, 5, 10, 11, 12, 13, *OWN), False))
    pl.when(band == 0)(lambda: combine(OWN, False))


def inner_kernel(f_ref, v_ref, out, *sums):
    def body(i, carry):
        layers = [f_ref[i, x] for x in range(4)]
        for x in range(4):
            here = layers[x]
            total = 3.0 * stencil_weights[0] * here
            for offset in range(1, 5):
                beside = pltpu.roll(here, offset, 0) + pltpu.roll(here, 64 - offset, 0)
                beside = beside + pltpu.roll(here, offset, 1) + pltpu.roll(here, 128 - offset, 1)
                if x + offset < 4:
                    beside = beside + layers[x + offset]
                if x - offset >= 0:
                    beside = beside + layers[x - offset]
                total = total + stencil_weights[offset] * beside
            out[i, x] = -0.5 * total + v_ref[x] * here
        return carry

    lax.fori_loop(0, BLK, body, 0)
    if sums:

        def row(i):
            return lambda c: f_ref[i, c // 8, pl.ds(pl.multiple_of((c % 8) * 8, 8), 8), :]

        load = {n: row(n - 16) for n in OWN}
        sums[0][...] = pair_sums([[(q, r) for q in OWN for r in range(16, q + 1)]], load, 32)


def edged(inner, x, left, right):
    total = None
    for offset in range(1, 5):
        if x + offset >= 4:
            term = stencil_weights[offset] * right(x + offset - 4)
            total = term if total is None else total + term
        if x - offset < 0:
            term = stencil_weights[offset] * left(x - offset + 4)
            total = term if total is None else total + term
    return inner - 0.5 * total


def add_edges(inner, across, beside, odd, out):
    def run(left, right):
        def body(i, carry):
            for x in range(4):
                part = pl.ds(64 * x, 64)
                out[i, part, :] = edged(
                    inner[i, part, :],
                    x,
                    lambda n: left[i, pl.ds(64 * n, 64), :],
                    lambda n: right[i, pl.ds(64 * n, 64), :],
                )
            return carry

        lax.fori_loop(0, BLK, body, 0)

    pl.when(odd == 0)(lambda: run(across, beside))
    pl.when(odd == 1)(lambda: run(beside, across))


def image_kernel(words, own, inner, across, beside, out, sums):
    add_edges(inner, across, beside, words[1], out)
    load = {n: loader(own, n - 16) for n in OWN}
    load |= {n: loader(out, n - 24) for n in IMAGE}
    jobs = [[(q, r) for q in IMAGE for r in OWN if r <= q - 8]]
    sums[...] = pair_sums(jobs, load, own.shape[1] // 8)


def dot(left, right, turn_left=False, turn_right=False):
    dims = (((0 if turn_left else 1,), (1 if turn_right else 0,)), ((), ()))
    return lax.dot_general(
        left, right, dims, precision=lax.Precision.HIGHEST, preferred_element_type=F32
    )


def places(y, home=None):
    row = lax.broadcasted_iota(jnp.int32, (128, 128), 0)
    lane = lax.broadcasted_iota(jnp.int32, (128, 128), 1)
    distance = (row + 2) >> 2
    distance = jnp.where((((row + 2) >> 1) & 1) == (y & 1), distance, -distance)
    piece = (y + distance) & 7
    target = (piece & 1) * 8 + (piece >> 1) * 2 + (row & 1)
    if home is None:
        target = jnp.where(row < 16, target, row)
    else:
        target = jnp.where((piece & 1) == home, -1, target)
        target = jnp.where(row < 16, target, row - 16 + 8 * home)
    return jnp.where((lane == target) & (row < 24), 1.0, 0.0)


def coeff_kernel(band_ref, weights_ref, gram_ref, own_ref, near_ref, far_ref, out):
    lane, sub = lanes(), subs()
    wide = lax.broadcasted_iota(jnp.int32, (128, 128), 1)
    row = lax.broadcasted_iota(jnp.int32, (128, 128), 0)
    place = places(band_ref[0] & 7)
    weights = jnp.where(lane < 24, pltpu.roll(weights_ref[...], 104, 1), 0.0)
    weights = dot(weights, place)

    def with_mirror(packed):
        tiles = unpacked(packed)
        mirror = jnp.transpose(tall([move(tiles[2], 24, 0)]))[0:8]
        tiles[2] = tiles[2] + move(jnp.where(lane == sub, 0.0, mirror), 0, 24)
        return tall(tiles)

    def image_columns(matrix, place, source, target):
        columns = dot(place, matrix, turn_left=True)
        columns = pltpu.roll(columns, (target - source) % 128, 1)
        return jnp.where((wide >= target) & (wide < target + 8), columns, 0.0)

    def visiting(n):
        packed = jnp.where(band_ref[0] < RING, near_ref[n], far_ref[n])
        return image_columns(with_mirror(packed), places(n, n), 24, 8 * n)

    block0, block1 = visiting(0), visiting(1)
    block = image_columns(with_mirror(own_ref[...]), place, 24, 16)
    half = dot(weights, block0 + block1 + block)
    half = half + dot(weights, jnp.where(row < 16, block, 0.0), turn_right=True)
    theta = dot(half, tall([weights]), turn_right=True)
    work = gram_ref[...] + move(theta, 0, 8)
    for k in range(8):
        line = work[k : k + 1, :]
        line = jnp.broadcast_to(line / jnp.broadcast_to(line[:, k : k + 1], (1, 128)), (8, 128))
        work = jnp.where(sub == k, line, work - spread_lane(work, k) * line)
    for j in range(8):
        out[j] = spread_lane(work, 8 + j)


def partial_kernel(f_ref, inner_ref, splat, out):
    def body(c, carry):
        part = pl.ds(pl.multiple_of(c * 32, 32), 32)
        for low in (0, 4):
            totals = [inner_ref[low + k, part, :] for k in range(4)]
            for i in range(BLK):
                cells = f_ref[i, part, :]
                totals = [
                    t - splat[low + k, pl.ds(i, 1), :] * cells for k, t in enumerate(totals)
                ]
            for k in range(4):
                out[low + k, part, :] = totals[k]
        return carry

    lax.fori_loop(0, f_ref.shape[1] // 32, body, 0)


def edge_kernel(words, partial, across, beside, out):
    add_edges(partial, across, beside, words[1], out)


def domain_parts(copies):
    return lax.all_to_all(copies, "domain", 0, 0)


def ring_exchange(block, odd):
    pairs = []
    for z in range(2):
        for y in range(odd, RING, 2):
            here, there = z * RING + y, z * RING + (y + 1) % RING
            pairs += [(here, there), (there, here)]
    return lax.ppermute(block, "band", pairs)


def neighbours(block):
    count = lax.axis_size("domain")
    across = [(i, (i + 1 if i % 2 else i - 1) % count) for i in range(count)]
    beside = [(i, i ^ 1) for i in range(count)]
    return lax.ppermute(block, "domain", across), lax.ppermute(block, "domain", beside)


def local(orbitals, potential):
    blocks, slab_width, rows_y, rows_z = orbitals.shape
    domain = lax.axis_size("domain")
    cells_total = float(slab_width * rows_y * rows_z * domain)
    band = lax.axis_index("band")
    words = jnp.stack([band, lax.axis_index("domain") & 1]).astype(jnp.int32)
    flat = (blocks, slab_width * rows_y, rows_z)
    big = flat[0] * flat[1] * flat[2]
    slab = jax.ShapeDtypeStruct(flat, F32)
    field = jax.ShapeDtypeStruct(orbitals.shape, F32)
    tile = jax.ShapeDtypeStruct((8, 128), F32)

    def inner_part(block, *sums):
        return call(
            inner_kernel,
            (field, *sums),
            specs=[VMEM] * 2,
            flops=60 * big,
            bytes_moved=8 * big,
        )(block, potential)

    own = orbitals.reshape(flat)
    quarters = [own[2 * k : 2 * k + 2] for k in range(4)]
    arrived = [
        lax.ppermute(quarters[k], "band", [(0, 2 * k), (1, 2 * k + 1)]) for k in (1, 3, 2)
    ]
    inner, sums = inner_part(orbitals, tile)
    arrived, inner, sums, words = lax.optimization_barrier((arrived, inner, sums, words))
    piece = jnp.where(band < 2, quarters[0], 0.0)
    for part in arrived:
        piece = piece + part
    across, beside = neighbours(own)
    crossed = lax.ppermute(piece, "band", [(y, y + RING) for y in range(RING)])
    piece = jnp.where(band < RING, piece, crossed)

    def stage(fresh, imaged, pieces, *sums, last=False):
        sources = (*pieces, own, *((image,) if imaged else ()), *sums)
        return call(
            lambda *refs: stage_kernel(len(pieces), fresh, imaged, last, *refs),
            jax.ShapeDtypeStruct((domain, 8, 128), F32) if last else tile,
            specs=[VMEM] * len(sources),
            flops=20 * big,
            bytes_moved=10 * big,
        )(*sources)

    pieces = [piece]
    up, down = ring_exchange(piece, 0), ring_exchange(piece, 1)
    pieces += [up, down]
    up, down = ring_exchange(down, 0), ring_exchange(up, 1)
    sums = stage(range(6), (), pieces, sums)
    down, sums = lax.optimization_barrier((down, sums))
    pieces += [up, down]
    up, down = ring_exchange(down, 0), ring_exchange(up, 1)
    sums = stage(range(6, 10), (), pieces, sums)
    down, sums, across, beside = lax.optimization_barrier((down, sums, across, beside))
    pieces += [up, down]
    up, down = ring_exchange(down[:1], 0), ring_exchange(up[1:], 1)
    image, image_sums = call(
        image_kernel,
        (slab, tile),
        specs=[SMEM] + [VMEM] * 4,
        flops=50 * big,
        bytes_moved=20 * big,
    )(words, own, inner.reshape(flat), across, beside)
    sums = stage(range(10, 14), range(14), pieces, sums, image_sums)
    pieces += [up, down]
    sums = stage(range(14, 16), range(14, 16), pieces, sums, last=True)
    sums = call(
        lambda *refs: total_kernel(cells_total, *refs),
        tile,
        specs=[VMEM],
        flops=40 * 1024,
        bytes_moved=160 * 1024,
    )(domain_parts(sums))
    basis, weights, gram = call(
        combine_kernel,
        (slab, tile, tile),
        scratch=[pltpu.VMEM((24, 8, 128), F32)],
        specs=[SMEM] + [VMEM] * 11,
        flops=48 * big,
        bytes_moved=16 * big,
    )(words, sums, *pieces, own)
    across, beside = neighbours(basis)
    inner = inner_part(basis.reshape(orbitals.shape))[0].reshape(flat)
    shared = sums
    other = lax.ppermute(shared, "band", [(0, 1), (1, 0)])
    shared = jnp.stack([jnp.where(band == 0, shared, other), jnp.where(band == 0, other, shared)])
    shared = jnp.where(band < 2, shared, 0.0)
    shared = shared + lax.ppermute(shared, "band", [(0, 4), (1, 5)])
    shared = shared + lax.ppermute(shared, "band", [(0, 2), (1, 3), (4, 6), (5, 7)])
    shared, inner = lax.optimization_barrier((shared, inner))
    far = lax.ppermute(shared, "band", [(y, y + RING) for y in range(RING)])
    splat = call(
        coeff_kernel, jax.ShapeDtypeStruct((8, 8, 128), F32), specs=[SMEM] + [VMEM] * 5
    )(words, weights, gram, sums, shared, far)
    partial = call(
        partial_kernel, slab, specs=[VMEM] * 3, flops=16 * big, bytes_moved=12 * big
    )(basis, inner, splat)
    residual = call(
        edge_kernel, slab, specs=[SMEM] + [VMEM] * 3, flops=20 * big, bytes_moved=16 * big
    )(words, partial, across, beside)
    return (basis.reshape(orbitals.shape), residual.reshape(orbitals.shape))


def solution(mesh):
    return jax.shard_map(
        local,
        mesh=mesh,
        in_specs=(P("band", "domain", None, None), P("domain", None, None)),
        out_specs=(P("band", "domain", None, None), P("band", "domain", None, None)),
        check_vma=False,
    )
```

```python
import jax
import jax.numpy as jnp
from jax import lax
from jax.experimental import pallas as pl
from jax.experimental.pallas import tpu as pltpu
from jax.sharding import PartitionSpec as P

stencil_weights = (-205.0 / 72.0, 8.0 / 5.0, -1.0 / 5.0, 8.0 / 315.0, -1.0 / 560.0)
BLK = 8
RING = 8
F32 = jnp.float32
VMEM = pl.BlockSpec(memory_space=pltpu.VMEM)
SMEM = pl.BlockSpec(memory_space=pltpu.SMEM)


def call(kernel, outs, scratch=(), specs=None, flops=0, bytes_moved=0):
    return pl.pallas_call(
        kernel,
        out_shape=outs,
        in_specs=specs,
        out_specs=jax.tree.map(lambda _: VMEM, outs),
        scratch_shapes=scratch,
        compiler_params=pltpu.CompilerParams(vmem_limit_bytes=32 * 1024 * 1024),
        cost_estimate=pl.CostEstimate(flops=flops, bytes_accessed=bytes_moved, transcendentals=0),
    )


def lanes():
    return lax.broadcasted_iota(jnp.int32, (8, 128), 1)


def subs():
    return lax.broadcasted_iota(jnp.int32, (8, 128), 0)


def folded(rows):
    sub = subs()
    step = 4
    while step:
        lower = (sub & step) == 0
        merged = []
        for first, second in zip(rows[:step], rows[step:]):
            if first is not None:
                first = first + pltpu.roll(first, 8 - step, 0)
            if second is not None:
                second = second + pltpu.roll(second, step, 0)
            if first is None and second is None:
                merged.append(None)
            else:
                merged.append(
                    jnp.where(lower, 0.0 if first is None else first, 0.0 if second is None else second)
                )
        rows = merged
        step //= 2
    return rows[0]


def pair_sums(jobs, load, chunks):
    lane = lanes()
    result = jnp.zeros((8, 128), F32)
    for pairs in jobs:
        used = sorted({n for pair in pairs for n in pair})

        def body(c, sums, pairs=pairs, used=used):
            for step in range(4):
                rows = {n: load[n](4 * c + step) for n in used}
                sums = tuple(s + rows[q] * rows[r] for s, (q, r) in zip(sums, pairs))
            return sums

        zero = jnp.zeros((8, 128), F32)
        sums = lax.fori_loop(0, chunks // 4, body, (zero,) * len(pairs))
        columns = {}
        for s, (q, r) in zip(sums, pairs):
            columns.setdefault(32 * (r // 8) + q, [None] * 8)[r % 8] = s
        for place, rows in columns.items():
            column = jnp.sum(folded(rows), axis=1, keepdims=True)
            result = result + jnp.where(lane == place, column, 0.0)
    return result


def loader(ref, index):
    return lambda c: ref[index, pl.ds(pl.multiple_of(c * 8, 8), 8), :]


def move(tile, source, target):
    lane = lanes()
    if source != target:
        tile = pltpu.roll(tile, (target - source) % 128, 1)
    return jnp.where((lane >= target) & (lane < target + 8), tile, 0.0)


def spread_lane(tile, k):
    return jnp.broadcast_to(tile[:, k : k + 1], (8, 128))


def rows_of(refs):
    return [(r, i) for r in refs for i in range(r.shape[0])]


def unpacked(sums):
    lane = lanes()
    parts = [sums] + [pltpu.roll(sums, 128 - 32 * n, 1) for n in (1, 2)]
    return [jnp.where(lane < 32, part, 0.0) for part in parts]


def tall(tiles):
    return jnp.concatenate(tiles + [jnp.zeros((128 - 8 * len(tiles), 128), F32)], axis=0)


OWN = list(range(16, 24))
IMAGE = list(range(24, 32))


def split(pairs, size=36):
    if not pairs:
        return []
    count = -(-len(pairs) // size)
    size = -(-len(pairs) // count)
    return [pairs[n : n + size] for n in range(0, len(pairs), size)]


def stage_kernel(parts, fresh, imaged, last, *refs):
    out = refs[-1]
    pieces, refs = refs[:parts], refs[parts:-1]
    own, image, before = (refs[0], refs[1], refs[2:]) if imaged else (refs[0], None, refs[1:])
    chunks = own.shape[1] // 8
    load = {n: loader(r, i) for n, (r, i) in enumerate(rows_of(pieces))}
    load |= {n: loader(own, n - 16) for n in OWN}
    if imaged:
        load |= {n: loader(image, n - 24) for n in IMAGE}
    jobs = split([(q, r) for q in OWN for r in fresh])
    jobs += split([(q, r) for q in fresh for r in range(q + 1)])
    jobs += split([(q, r) for q in IMAGE for r in imaged])
    total = pair_sums(jobs, load, chunks)
    for part in before:
        total = total + part[...]
    if last:
        for n in range(out.shape[0]):
            out[n] = total
    else:
        out[...] = total


def total_kernel(cells_total, parts_ref, out):
    out[...] = jnp.sum(parts_ref[...], axis=0) / cells_total


def combine_kernel(band_ref, sums_ref, *refs):
    *pieces, own, out, weights_ref, gram_ref, splat = refs
    band = band_ref[0]
    lane, sub = lanes(), subs()
    tiles = unpacked(sums_ref[...])
    turned = jnp.transpose(tall(tiles))
    w0, w1, w2 = (
        jnp.where(lane < 24, tile + jnp.where(lane == sub + 8 * n, 0.0, turned[8 * n : 8 * n + 8]), 0.0)
        for n, tile in enumerate(tiles)
    )
    later = band >= 2
    second = band == 1

    def taken(position):
        place = position & 7
        return later | (second & (place >= 2) & (place <= 5))

    row_in = taken(sub)
    lane_in = (lane >= 16) | taken(lane)
    kept = row_in & lane_in
    w0 = jnp.where(kept, w0, jnp.where(lane == sub, 1.0, 0.0))
    w1 = jnp.where(kept, w1, jnp.where(lane == 8 + sub, 1.0, 0.0))
    w0 = w0 + jnp.where(lane == 24 + sub, 1.0, 0.0)
    w1 = w1 + jnp.where(lane == 32 + sub, 1.0, 0.0)
    w2 = jnp.where(lane_in, w2, 0.0) + jnp.where(lane == 40 + sub, 1.0, 0.0)
    tiles = [w0, w1, w2]
    for k in range(16):
        v, s = divmod(k, 8)
        row = tiles[v][s : s + 1, :]
        row = row / jnp.broadcast_to(row[:, k : k + 1], (1, 128))
        row = jnp.broadcast_to(row, (8, 128))
        for u in range(v, 3):
            column = spread_lane(tiles[u], k)
            if u == v:
                column = jnp.where(sub > s, column, 0.0)
            tiles[u] = tiles[u] - column * row
    plain = tiles[2]
    scaled = plain
    for k in range(8):
        row = scaled[k : k + 1, :]
        row = row / jnp.broadcast_to(row[:, 16 + k : 17 + k], (1, 128))
        column = jnp.where(sub > k, spread_lane(scaled, 16 + k), 0.0)
        scaled = scaled - column * jnp.broadcast_to(row, (8, 128))
    pivots = jnp.sum(jnp.where(lane == 16 + sub, scaled, 0.0), axis=1, keepdims=True)
    scaled = scaled / jnp.sqrt(jnp.broadcast_to(pivots, (8, 128)))
    weights = jnp.where(later, plain, scaled)
    weights_ref[...] = weights
    gram_ref[...] = jnp.where(later, move(plain, 16, 0), jnp.where(lane == sub, 1.0, 0.0))
    for c in range(24):
        splat[c] = spread_lane(weights, 24 + c)
    rows = rows_of(pieces) + [(own, i) for i in range(BLK)]

    def combine(places, plus_own):
        def body(c, carry):
            part = pl.ds(pl.multiple_of(c * 32, 32), 32)
            for low in (0, 4):
                if plus_own:
                    totals = [own[low + k, part, :] for k in range(4)]
                else:
                    totals = [jnp.zeros((32, 128), F32)] * 4
                for n in places:
                    r, i = rows[n]
                    cells = r[i, part, :]
                    totals = [
                        t + splat[n, pl.ds(low + k, 1), :] * cells for k, t in enumerate(totals)
                    ]
                for k in range(4):
                    out[low + k, part, :] = totals[k]
            return carry

        lax.fori_loop(0, own.shape[1] // 32, body, 0)

    pl.when(later)(lambda: combine(range(16), True))
    pl.when(second)(lambda: combine((2, 3, 4, 5, 10, 11, 12, 13, *OWN), False))
    pl.when(band == 0)(lambda: combine(OWN, False))


def inner_kernel(f_ref, v_ref, out, *sums):
    def body(i, carry):
        layers = [f_ref[i, x] for x in range(4)]
        for x in range(4):
            here = layers[x]
            total = 3.0 * stencil_weights[0] * here
            for offset in range(1, 5):
                beside = pltpu.roll(here, offset, 0) + pltpu.roll(here, 64 - offset, 0)
                beside = beside + pltpu.roll(here, offset, 1) + pltpu.roll(here, 128 - offset, 1)
                if x + offset < 4:
                    beside = beside + layers[x + offset]
                if x - offset >= 0:
                    beside = beside + layers[x - offset]
                total = total + stencil_weights[offset] * beside
            out[i, x] = -0.5 * total + v_ref[x] * here
        return carry

    lax.fori_loop(0, BLK, body, 0)
    if sums:

        def row(i):
            return lambda c: f_ref[i, c // 8, pl.ds(pl.multiple_of((c % 8) * 8, 8), 8), :]

        load = {n: row(n - 16) for n in OWN}
        sums[0][...] = pair_sums([[(q, r) for q in OWN for r in range(16, q + 1)]], load, 32)


def edged(inner, x, left, right):
    total = None
    for offset in range(1, 5):
        if x + offset >= 4:
            term = stencil_weights[offset] * right(x + offset - 4)
            total = term if total is None else total + term
        if x - offset < 0:
            term = stencil_weights[offset] * left(x - offset + 4)
            total = term if total is None else total + term
    return inner - 0.5 * total


def add_edges(inner, across, beside, odd, out):
    def run(left, right):
        def body(i, carry):
            for x in range(4):
                part = pl.ds(64 * x, 64)
                out[i, part, :] = edged(
                    inner[i, part, :],
                    x,
                    lambda n: left[i, pl.ds(64 * n, 64), :],
                    lambda n: right[i, pl.ds(64 * n, 64), :],
                )
            return carry

        lax.fori_loop(0, BLK, body, 0)

    pl.when(odd == 0)(lambda: run(across, beside))
    pl.when(odd == 1)(lambda: run(beside, across))


def image_kernel(words, own, inner, across, beside, out, sums):
    add_edges(inner, across, beside, words[1], out)
    load = {n: loader(own, n - 16) for n in OWN}
    load |= {n: loader(out, n - 24) for n in IMAGE}
    jobs = [[(q, r) for q in IMAGE for r in OWN if r <= q - 8]]
    sums[...] = pair_sums(jobs, load, own.shape[1] // 8)


def dot(left, right, turn_left=False, turn_right=False):
    dims = (((0 if turn_left else 1,), (1 if turn_right else 0,)), ((), ()))
    return lax.dot_general(
        left, right, dims, precision=lax.Precision.HIGHEST, preferred_element_type=F32
    )


def places(y, home=None):
    row = lax.broadcasted_iota(jnp.int32, (128, 128), 0)
    lane = lax.broadcasted_iota(jnp.int32, (128, 128), 1)
    distance = (row + 2) >> 2
    distance = jnp.where(((row + 2) & 2) == 0, -distance, distance)
    piece = (y + distance) & 7
    target = (piece & 1) * 8 + (piece >> 1) * 2 + (row & 1)
    if home is None:
        target = jnp.where(row < 16, target, row)
    else:
        target = jnp.where((piece & 1) == home, -1, target)
        target = jnp.where(row < 16, target, row - 16 + 8 * home)
    return jnp.where((lane == target) & (row < 24), 1.0, 0.0)


def coeff_kernel(band_ref, weights_ref, gram_ref, own_ref, near_ref, far_ref, out):
    lane, sub = lanes(), subs()
    wide = lax.broadcasted_iota(jnp.int32, (128, 128), 1)
    row = lax.broadcasted_iota(jnp.int32, (128, 128), 0)
    place = places(band_ref[0] & 7)
    weights = jnp.where(lane < 24, pltpu.roll(weights_ref[...], 104, 1), 0.0)
    weights = dot(weights, place)

    def with_mirror(packed):
        tiles = unpacked(packed)
        mirror = jnp.transpose(tall([move(tiles[2], 24, 0)]))[0:8]
        tiles[2] = tiles[2] + move(jnp.where(lane == sub, 0.0, mirror), 0, 24)
        return tall(tiles)

    def image_columns(matrix, place, source, target):
        columns = dot(place, matrix, turn_left=True)
        columns = pltpu.roll(columns, (target - source) % 128, 1)
        return jnp.where((wide >= target) & (wide < target + 8), columns, 0.0)

    def visiting(n):
        packed = jnp.where(band_ref[0] < RING, near_ref[n], far_ref[n])
        return image_columns(with_mirror(packed), places(n, n), 24, 8 * n)

    block0, block1 = visiting(0), visiting(1)
    block = image_columns(with_mirror(own_ref[...]), place, 24, 16)
    half = dot(weights, block0 + block1 + block)
    half = half + dot(weights, jnp.where(row < 16, block, 0.0), turn_right=True)
    theta = dot(half, tall([weights]), turn_right=True)
    work = gram_ref[...] + move(theta, 0, 8)
    for k in range(8):
        line = work[k : k + 1, :]
        line = jnp.broadcast_to(line / jnp.broadcast_to(line[:, k : k + 1], (1, 128)), (8, 128))
        work = jnp.where(sub == k, line, work - spread_lane(work, k) * line)
    for j in range(8):
        out[j] = spread_lane(work, 8 + j)


def partial_kernel(f_ref, inner_ref, splat, out):
    def body(c, carry):
        part = pl.ds(pl.multiple_of(c * 32, 32), 32)
        for low in (0, 4):
            totals = [inner_ref[low + k, part, :] for k in range(4)]
            for i in range(BLK):
                cells = f_ref[i, part, :]
                totals = [
                    t - splat[low + k, pl.ds(i, 1), :] * cells for k, t in enumerate(totals)
                ]
            for k in range(4):
                out[low + k, part, :] = totals[k]
        return carry

    lax.fori_loop(0, f_ref.shape[1] // 32, body, 0)


def edge_kernel(words, partial, across, beside, out):
    add_edges(partial, across, beside, words[1], out)


def domain_parts(copies):
    return lax.all_to_all(copies, "domain", 0, 0)


def ring_shift(block, step):
    pairs = [(z * RING + y, z * RING + (y + step) % RING) for z in range(2) for y in range(RING)]
    return lax.ppermute(block, "band", pairs)


def neighbours(block):
    count = lax.axis_size("domain")
    across = [(i, (i + 1 if i % 2 else i - 1) % count) for i in range(count)]
    beside = [(i, i ^ 1) for i in range(count)]
    return lax.ppermute(block, "domain", across), lax.ppermute(block, "domain", beside)


def local(orbitals, potential):
    blocks, slab_width, rows_y, rows_z = orbitals.shape
    domain = lax.axis_size("domain")
    cells_total = float(slab_width * rows_y * rows_z * domain)
    band = lax.axis_index("band")
    words = jnp.stack([band, lax.axis_index("domain") & 1]).astype(jnp.int32)
    flat = (blocks, slab_width * rows_y, rows_z)
    big = flat[0] * flat[1] * flat[2]
    slab = jax.ShapeDtypeStruct(flat, F32)
    field = jax.ShapeDtypeStruct(orbitals.shape, F32)
    tile = jax.ShapeDtypeStruct((8, 128), F32)

    def inner_part(block, *sums):
        return call(
            inner_kernel,
            (field, *sums),
            specs=[VMEM] * 2,
            flops=60 * big,
            bytes_moved=8 * big,
        )(block, potential)

    own = orbitals.reshape(flat)
    quarters = [own[2 * k : 2 * k + 2] for k in range(4)]
    arrived = [
        lax.ppermute(quarters[k], "band", [(0, 2 * k), (1, 2 * k + 1)]) for k in (1, 3, 2)
    ]
    inner, sums = inner_part(orbitals, tile)
    arrived, inner, sums, words = lax.optimization_barrier((arrived, inner, sums, words))
    piece = jnp.where(band < 2, quarters[0], 0.0)
    for part in arrived:
        piece = piece + part
    across, beside = neighbours(own)
    crossed = lax.ppermute(piece, "band", [(y, y + RING) for y in range(RING)])
    piece = jnp.where(band < RING, piece, crossed)

    def stage(fresh, imaged, pieces, *sums, last=False):
        sources = (*pieces, own, *((image,) if imaged else ()), *sums)
        return call(
            lambda *refs: stage_kernel(len(pieces), fresh, imaged, last, *refs),
            jax.ShapeDtypeStruct((domain, 8, 128), F32) if last else tile,
            specs=[VMEM] * len(sources),
            flops=20 * big,
            bytes_moved=10 * big,
        )(*sources)

    pieces = [piece]
    up, down = ring_shift(piece, 1), ring_shift(piece, -1)
    pieces += [up, down]
    up, down = ring_shift(up, 1), ring_shift(down, -1)
    image, image_sums = call(
        image_kernel,
        (slab, tile),
        specs=[SMEM] + [VMEM] * 4,
        flops=50 * big,
        bytes_moved=20 * big,
    )(words, own, inner.reshape(flat), across, beside)
    down, image, image_sums = lax.optimization_barrier((down, image, image_sums))
    pieces += [up, down]
    up, down = ring_shift(up, 1), ring_shift(down, -1)
    sums = stage(range(10), (), pieces, sums)
    down, sums = lax.optimization_barrier((down, sums))
    pieces += [up, down]
    up, down = ring_shift(up[:1], 1), ring_shift(down[1:], -1)
    sums = stage(range(10, 14), range(14), pieces, sums, image_sums)
    pieces += [up, down]
    sums = stage(range(14, 16), range(14, 16), pieces, sums, last=True)
    sums = call(
        lambda *refs: total_kernel(cells_total, *refs),
        tile,
        specs=[VMEM],
        flops=40 * 1024,
        bytes_moved=160 * 1024,
    )(domain_parts(sums))
    basis, weights, gram = call(
        combine_kernel,
        (slab, tile, tile),
        scratch=[pltpu.VMEM((24, 8, 128), F32)],
        specs=[SMEM] + [VMEM] * 11,
        flops=48 * big,
        bytes_moved=16 * big,
    )(words, sums, *pieces, own)
    across, beside = neighbours(basis)
    inner = inner_part(basis.reshape(orbitals.shape))[0].reshape(flat)
    shared = sums
    other = lax.ppermute(shared, "band", [(0, 1), (1, 0)])
    shared = jnp.stack([jnp.where(band == 0, shared, other), jnp.where(band == 0, other, shared)])
    shared = jnp.where(band < 2, shared, 0.0)
    shared = shared + lax.ppermute(shared, "band", [(0, 4), (1, 5)])
    shared = shared + lax.ppermute(shared, "band", [(0, 2), (1, 3), (4, 6), (5, 7)])
    shared, inner = lax.optimization_barrier((shared, inner))
    far = lax.ppermute(shared, "band", [(y, y + RING) for y in range(RING)])
    splat = call(
        coeff_kernel, jax.ShapeDtypeStruct((8, 8, 128), F32), specs=[SMEM] + [VMEM] * 5
    )(words, weights, gram, sums, shared, far)
    partial = call(
        partial_kernel, slab, specs=[VMEM] * 3, flops=16 * big, bytes_moved=12 * big
    )(basis, inner, splat)
    residual = call(
        edge_kernel, slab, specs=[SMEM] + [VMEM] * 3, flops=20 * big, bytes_moved=16 * big
    )(words, partial, across, beside)
    return (basis.reshape(orbitals.shape), residual.reshape(orbitals.shape))


def solution(mesh):
    return jax.shard_map(
        local,
        mesh=mesh,
        in_specs=(P("band", "domain", None, None), P("domain", None, None)),
        out_specs=(P("band", "domain", None, None), P("band", "domain", None, None)),
        check_vma=False,
    )
```

```python
import jax
import jax.numpy as jnp
from jax import lax
from jax.experimental import pallas as pl
from jax.experimental.pallas import tpu as pltpu
from jax.sharding import PartitionSpec as P

stencil_weights = (-205.0 / 72.0, 8.0 / 5.0, -1.0 / 5.0, 8.0 / 315.0, -1.0 / 560.0)
BLK = 8
RING = 8
F32 = jnp.float32
VMEM = pl.BlockSpec(memory_space=pltpu.VMEM)
SMEM = pl.BlockSpec(memory_space=pltpu.SMEM)


def call(kernel, outs, scratch=(), specs=None, flops=0, bytes_moved=0):
    return pl.pallas_call(
        kernel,
        out_shape=outs,
        in_specs=specs,
        out_specs=jax.tree.map(lambda _: VMEM, outs),
        scratch_shapes=scratch,
        compiler_params=pltpu.CompilerParams(vmem_limit_bytes=32 * 1024 * 1024),
        cost_estimate=pl.CostEstimate(flops=flops, bytes_accessed=bytes_moved, transcendentals=0),
    )


def lanes():
    return lax.broadcasted_iota(jnp.int32, (8, 128), 1)


def subs():
    return lax.broadcasted_iota(jnp.int32, (8, 128), 0)


def folded(rows):
    sub = subs()
    step = 4
    while step:
        lower = (sub & step) == 0
        merged = []
        for first, second in zip(rows[:step], rows[step:]):
            if first is not None:
                first = first + pltpu.roll(first, 8 - step, 0)
            if second is not None:
                second = second + pltpu.roll(second, step, 0)
            if first is None and second is None:
                merged.append(None)
            else:
                merged.append(
                    jnp.where(lower, 0.0 if first is None else first, 0.0 if second is None else second)
                )
        rows = merged
        step //= 2
    return rows[0]


def pair_sums(jobs, load, chunks):
    lane = lanes()
    result = jnp.zeros((8, 128), F32)
    for pairs in jobs:
        used = sorted({n for pair in pairs for n in pair})

        def body(c, sums, pairs=pairs, used=used):
            for step in range(4):
                rows = {n: load[n](4 * c + step) for n in used}
                sums = tuple(s + rows[q] * rows[r] for s, (q, r) in zip(sums, pairs))
            return sums

        zero = jnp.zeros((8, 128), F32)
        sums = lax.fori_loop(0, chunks // 4, body, (zero,) * len(pairs))
        columns = {}
        for s, (q, r) in zip(sums, pairs):
            columns.setdefault(32 * (r // 8) + q, [None] * 8)[r % 8] = s
        for place, rows in columns.items():
            column = jnp.sum(folded(rows), axis=1, keepdims=True)
            result = result + jnp.where(lane == place, column, 0.0)
    return result


def loader(ref, index):
    return lambda c: ref[index, pl.ds(pl.multiple_of(c * 8, 8), 8), :]


def move(tile, source, target):
    lane = lanes()
    if source != target:
        tile = pltpu.roll(tile, (target - source) % 128, 1)
    return jnp.where((lane >= target) & (lane < target + 8), tile, 0.0)


def spread_lane(tile, k):
    return jnp.broadcast_to(tile[:, k : k + 1], (8, 128))


def rows_of(refs):
    return [(r, i) for r in refs for i in range(r.shape[0])]


def unpacked(sums):
    lane = lanes()
    parts = [sums] + [pltpu.roll(sums, 128 - 32 * n, 1) for n in (1, 2)]
    return [jnp.where(lane < 32, part, 0.0) for part in parts]


def tall(tiles):
    return jnp.concatenate(tiles + [jnp.zeros((128 - 8 * len(tiles), 128), F32)], axis=0)


OWN = list(range(16, 24))
IMAGE = list(range(24, 32))


def split(pairs, size=36):
    if not pairs:
        return []
    count = -(-len(pairs) // size)
    size = -(-len(pairs) // count)
    return [pairs[n : n + size] for n in range(0, len(pairs), size)]


def stage_kernel(parts, fresh, imaged, last, *refs):
    out = refs[-1]
    pieces, refs = refs[:parts], refs[parts:-1]
    own, image, before = (refs[0], refs[1], refs[2:]) if imaged else (refs[0], None, refs[1:])
    chunks = own.shape[1] // 8
    load = {n: loader(r, i) for n, (r, i) in enumerate(rows_of(pieces))}
    load |= {n: loader(own, n - 16) for n in OWN}
    if imaged:
        load |= {n: loader(image, n - 24) for n in IMAGE}
    jobs = split([(q, r) for q in OWN for r in fresh])
    jobs += split([(q, r) for q in fresh for r in range(q + 1)])
    jobs += split([(q, r) for q in IMAGE for r in imaged])
    total = pair_sums(jobs, load, chunks)
    for part in before:
        total = total + part[...]
    if last:
        for n in range(out.shape[0]):
            out[n] = total
    else:
        out[...] = total


def total_kernel(cells_total, parts_ref, out):
    out[...] = jnp.sum(parts_ref[...], axis=0) / cells_total


def combine_kernel(band_ref, sums_ref, *refs):
    *pieces, own, out, weights_ref, gram_ref, splat = refs
    band = band_ref[0]
    lane, sub = lanes(), subs()
    tiles = unpacked(sums_ref[...])
    turned = jnp.transpose(tall(tiles))
    w0, w1, w2 = (
        jnp.where(lane < 24, tile + jnp.where(lane == sub + 8 * n, 0.0, turned[8 * n : 8 * n + 8]), 0.0)
        for n, tile in enumerate(tiles)
    )
    later = band >= 2
    second = band == 1

    def taken(position):
        place = position & 7
        return later | (second & (place >= 2) & (place <= 5))

    row_in = taken(sub)
    lane_in = (lane >= 16) | taken(lane)
    kept = row_in & lane_in
    w0 = jnp.where(kept, w0, jnp.where(lane == sub, 1.0, 0.0))
    w1 = jnp.where(kept, w1, jnp.where(lane == 8 + sub, 1.0, 0.0))
    w0 = w0 + jnp.where(lane == 24 + sub, 1.0, 0.0)
    w1 = w1 + jnp.where(lane == 32 + sub, 1.0, 0.0)
    w2 = jnp.where(lane_in, w2, 0.0) + jnp.where(lane == 40 + sub, 1.0, 0.0)
    tiles = [w0, w1, w2]
    for k in range(16):
        v, s = divmod(k, 8)
        row = tiles[v][s : s + 1, :]
        row = row / jnp.broadcast_to(row[:, k : k + 1], (1, 128))
        row = jnp.broadcast_to(row, (8, 128))
        for u in range(v, 3):
            column = spread_lane(tiles[u], k)
            if u == v:
                column = jnp.where(sub > s, column, 0.0)
            tiles[u] = tiles[u] - column * row
    plain = tiles[2]
    scaled = plain
    for k in range(8):
        row = scaled[k : k + 1, :]
        row = row / jnp.broadcast_to(row[:, 16 + k : 17 + k], (1, 128))
        column = jnp.where(sub > k, spread_lane(scaled, 16 + k), 0.0)
        scaled = scaled - column * jnp.broadcast_to(row, (8, 128))
    pivots = jnp.sum(jnp.where(lane == 16 + sub, scaled, 0.0), axis=1, keepdims=True)
    scaled = scaled / jnp.sqrt(jnp.broadcast_to(pivots, (8, 128)))
    weights = jnp.where(later, plain, scaled)
    weights_ref[...] = weights
    gram_ref[...] = jnp.where(later, move(plain, 16, 0), jnp.where(lane == sub, 1.0, 0.0))
    for c in range(24):
        splat[c] = spread_lane(weights, 24 + c)
    rows = rows_of(pieces) + [(own, i) for i in range(BLK)]

    def combine(places, plus_own):
        def body(c, carry):
            part = pl.ds(pl.multiple_of(c * 32, 32), 32)
            for low in (0, 4):
                if plus_own:
                    totals = [own[low + k, part, :] for k in range(4)]
                else:
                    totals = [jnp.zeros((32, 128), F32)] * 4
                for n in places:
                    r, i = rows[n]
                    cells = r[i, part, :]
                    totals = [
                        t + splat[n, pl.ds(low + k, 1), :] * cells for k, t in enumerate(totals)
                    ]
                for k in range(4):
                    out[low + k, part, :] = totals[k]
            return carry

        lax.fori_loop(0, own.shape[1] // 32, body, 0)

    pl.when(later)(lambda: combine(range(16), True))
    pl.when(second)(lambda: combine((2, 3, 4, 5, 10, 11, 12, 13, *OWN), False))
    pl.when(band == 0)(lambda: combine(OWN, False))


def inner_kernel(f_ref, v_ref, out, *sums):
    def body(i, carry):
        layers = [f_ref[i, x] for x in range(4)]
        for x in range(4):
            here = layers[x]
            total = 3.0 * stencil_weights[0] * here
            for offset in range(1, 5):
                beside = pltpu.roll(here, offset, 0) + pltpu.roll(here, 64 - offset, 0)
                beside = beside + pltpu.roll(here, offset, 1) + pltpu.roll(here, 128 - offset, 1)
                if x + offset < 4:
                    beside = beside + layers[x + offset]
                if x - offset >= 0:
                    beside = beside + layers[x - offset]
                total = total + stencil_weights[offset] * beside
            out[i, x] = -0.5 * total + v_ref[x] * here
        return carry

    lax.fori_loop(0, BLK, body, 0)
    if sums:

        def row(i):
            return lambda c: f_ref[i, c // 8, pl.ds(pl.multiple_of((c % 8) * 8, 8), 8), :]

        load = {n: row(n - 16) for n in OWN}
        sums[0][...] = pair_sums([[(q, r) for q in OWN for r in range(16, q + 1)]], load, 32)


def edged(inner, x, left, right):
    total = None
    for offset in range(1, 5):
        if x + offset >= 4:
            term = stencil_weights[offset] * right(x + offset - 4)
            total = term if total is None else total + term
        if x - offset < 0:
            term = stencil_weights[offset] * left(x - offset + 4)
            total = term if total is None else total + term
    return inner - 0.5 * total


def add_edges(inner, across, beside, odd, out):
    def run(left, right):
        def body(i, carry):
            for x in range(4):
                part = pl.ds(64 * x, 64)
                out[i, part, :] = edged(
                    inner[i, part, :],
                    x,
                    lambda n: left[i, pl.ds(64 * n, 64), :],
                    lambda n: right[i, pl.ds(64 * n, 64), :],
                )
            return carry

        lax.fori_loop(0, BLK, body, 0)

    pl.when(odd == 0)(lambda: run(across, beside))
    pl.when(odd == 1)(lambda: run(beside, across))


def image_kernel(words, own, inner, across, beside, out, sums):
    add_edges(inner, across, beside, words[1], out)
    load = {n: loader(own, n - 16) for n in OWN}
    load |= {n: loader(out, n - 24) for n in IMAGE}
    jobs = [[(q, r) for q in IMAGE for r in OWN if r <= q - 8]]
    sums[...] = pair_sums(jobs, load, own.shape[1] // 8)


def dot(left, right, turn_left=False, turn_right=False):
    dims = (((0 if turn_left else 1,), (1 if turn_right else 0,)), ((), ()))
    return lax.dot_general(
        left, right, dims, precision=lax.Precision.HIGHEST, preferred_element_type=F32
    )


def places(y, home=None):
    row = lax.broadcasted_iota(jnp.int32, (128, 128), 0)
    lane = lax.broadcasted_iota(jnp.int32, (128, 128), 1)
    distance = (row + 2) >> 2
    distance = jnp.where(((row + 2) & 2) == 0, -distance, distance)
    piece = (y + distance) & 7
    target = (piece & 1) * 8 + (piece >> 1) * 2 + (row & 1)
    if home is None:
        target = jnp.where(row < 16, target, row)
    else:
        target = jnp.where((piece & 1) == home, -1, target)
        target = jnp.where(row < 16, target, row - 16 + 8 * home)
    return jnp.where((lane == target) & (row < 24), 1.0, 0.0)


def coeff_kernel(band_ref, weights_ref, gram_ref, own_ref, near_ref, far_ref, out):
    lane, sub = lanes(), subs()
    wide = lax.broadcasted_iota(jnp.int32, (128, 128), 1)
    row = lax.broadcasted_iota(jnp.int32, (128, 128), 0)
    place = places(band_ref[0] & 7)
    weights = jnp.where(lane < 24, pltpu.roll(weights_ref[...], 104, 1), 0.0)
    weights = dot(weights, place)

    def with_mirror(packed):
        tiles = unpacked(packed)
        mirror = jnp.transpose(tall([move(tiles[2], 24, 0)]))[0:8]
        tiles[2] = tiles[2] + move(jnp.where(lane == sub, 0.0, mirror), 0, 24)
        return tall(tiles)

    def image_columns(matrix, place, source, target):
        columns = dot(place, matrix, turn_left=True)
        columns = pltpu.roll(columns, (target - source) % 128, 1)
        return jnp.where((wide >= target) & (wide < target + 8), columns, 0.0)

    def visiting(n):
        packed = jnp.where(band_ref[0] < RING, near_ref[n], far_ref[n])
        return image_columns(with_mirror(packed), places(n, n), 24, 8 * n)

    block0, block1 = visiting(0), visiting(1)
    block = image_columns(with_mirror(own_ref[...]), place, 24, 16)
    half = dot(weights, block0 + block1 + block)
    half = half + dot(weights, jnp.where(row < 16, block, 0.0), turn_right=True)
    theta = dot(half, tall([weights]), turn_right=True)
    work = gram_ref[...] + move(theta, 0, 8)
    for k in range(8):
        line = work[k : k + 1, :]
        line = jnp.broadcast_to(line / jnp.broadcast_to(line[:, k : k + 1], (1, 128)), (8, 128))
        work = jnp.where(sub == k, line, work - spread_lane(work, k) * line)
    for j in range(8):
        out[j] = spread_lane(work, 8 + j)


def partial_kernel(f_ref, inner_ref, splat, out):
    def body(c, carry):
        part = pl.ds(pl.multiple_of(c * 32, 32), 32)
        for low in (0, 4):
            totals = [inner_ref[low + k, part, :] for k in range(4)]
            for i in range(BLK):
                cells = f_ref[i, part, :]
                totals = [
                    t - splat[low + k, pl.ds(i, 1), :] * cells for k, t in enumerate(totals)
                ]
            for k in range(4):
                out[low + k, part, :] = totals[k]
        return carry

    lax.fori_loop(0, f_ref.shape[1] // 32, body, 0)


def edge_kernel(words, partial, across, beside, out):
    add_edges(partial, across, beside, words[1], out)


def domain_parts(copies):
    return lax.all_to_all(copies, "domain", 0, 0)


def ring_shift(block, step):
    pairs = [(z * RING + y, z * RING + (y + step) % RING) for z in range(2) for y in range(RING)]
    return lax.ppermute(block, "band", pairs)


def neighbours(block):
    count = lax.axis_size("domain")
    across = [(i, (i + 1 if i % 2 else i - 1) % count) for i in range(count)]
    beside = [(i, i ^ 1) for i in range(count)]
    return lax.ppermute(block, "domain", across), lax.ppermute(block, "domain", beside)


def local(orbitals, potential):
    blocks, slab_width, rows_y, rows_z = orbitals.shape
    domain = lax.axis_size("domain")
    cells_total = float(slab_width * rows_y * rows_z * domain)
    band = lax.axis_index("band")
    words = jnp.stack([band, lax.axis_index("domain") & 1]).astype(jnp.int32)
    flat = (blocks, slab_width * rows_y, rows_z)
    big = flat[0] * flat[1] * flat[2]
    slab = jax.ShapeDtypeStruct(flat, F32)
    field = jax.ShapeDtypeStruct(orbitals.shape, F32)
    tile = jax.ShapeDtypeStruct((8, 128), F32)

    def inner_part(block, *sums):
        return call(
            inner_kernel,
            (field, *sums),
            specs=[VMEM] * 2,
            flops=60 * big,
            bytes_moved=8 * big,
        )(block, potential)

    own = orbitals.reshape(flat)
    quarters = [own[2 * k : 2 * k + 2] for k in range(4)]
    arrived = [
        lax.ppermute(quarters[k], "band", [(0, 2 * k), (1, 2 * k + 1)]) for k in (1, 3, 2)
    ]
    inner, sums = inner_part(orbitals, tile)
    arrived, inner, sums, words = lax.optimization_barrier((arrived, inner, sums, words))
    piece = jnp.where(band < 2, quarters[0], 0.0)
    for part in arrived:
        piece = piece + part
    crossed = lax.ppermute(piece, "band", [(y, y + RING) for y in range(RING)])
    piece = jnp.where(band < RING, piece, crossed)
    piece, raw = lax.optimization_barrier((piece, own))
    across, beside = neighbours(raw)

    def stage(fresh, imaged, pieces, *sums, last=False):
        sources = (*pieces, own, *((image,) if imaged else ()), *sums)
        return call(
            lambda *refs: stage_kernel(len(pieces), fresh, imaged, last, *refs),
            jax.ShapeDtypeStruct((domain, 8, 128), F32) if last else tile,
            specs=[VMEM] * len(sources),
            flops=20 * big,
            bytes_moved=10 * big,
        )(*sources)

    pieces = [piece]
    up, down = ring_shift(piece, 1), ring_shift(piece, -1)
    pieces += [up, down]
    up, down = ring_shift(up, 1), ring_shift(down, -1)
    sums = stage(range(6), (), pieces, sums)
    down, sums = lax.optimization_barrier((down, sums))
    pieces += [up, down]
    up, down = ring_shift(up, 1), ring_shift(down, -1)
    sums = stage(range(6, 10), (), pieces, sums)
    down, sums = lax.optimization_barrier((down, sums))
    pieces += [up, down]
    up, down = ring_shift(up[:1], 1), ring_shift(down[1:], -1)
    image, image_sums = call(
        image_kernel,
        (slab, tile),
        specs=[SMEM] + [VMEM] * 4,
        flops=50 * big,
        bytes_moved=20 * big,
    )(words, own, inner.reshape(flat), across, beside)
    sums = stage(range(10, 14), range(14), pieces, sums, image_sums)
    pieces += [up, down]
    sums = stage(range(14, 16), range(14, 16), pieces, sums, last=True)
    sums = call(
        lambda *refs: total_kernel(cells_total, *refs),
        tile,
        specs=[VMEM],
        flops=40 * 1024,
        bytes_moved=160 * 1024,
    )(domain_parts(sums))
    basis, weights, gram = call(
        combine_kernel,
        (slab, tile, tile),
        scratch=[pltpu.VMEM((24, 8, 128), F32)],
        specs=[SMEM] + [VMEM] * 11,
        flops=48 * big,
        bytes_moved=16 * big,
    )(words, sums, *pieces, own)
    across, beside = neighbours(basis)
    inner = inner_part(basis.reshape(orbitals.shape))[0].reshape(flat)
    shared = sums
    other = lax.ppermute(shared, "band", [(0, 1), (1, 0)])
    shared = jnp.stack([jnp.where(band == 0, shared, other), jnp.where(band == 0, other, shared)])
    shared = jnp.where(band < 2, shared, 0.0)
    shared = shared + lax.ppermute(shared, "band", [(0, 4), (1, 5)])
    shared = shared + lax.ppermute(shared, "band", [(0, 2), (1, 3), (4, 6), (5, 7)])
    shared, inner = lax.optimization_barrier((shared, inner))
    far = lax.ppermute(shared, "band", [(y, y + RING) for y in range(RING)])
    splat = call(
        coeff_kernel, jax.ShapeDtypeStruct((8, 8, 128), F32), specs=[SMEM] + [VMEM] * 5
    )(words, weights, gram, sums, shared, far)
    partial = call(
        partial_kernel, slab, specs=[VMEM] * 3, flops=16 * big, bytes_moved=12 * big
    )(basis, inner, splat)
    residual = call(
        edge_kernel, slab, specs=[SMEM] + [VMEM] * 3, flops=20 * big, bytes_moved=16 * big
    )(words, partial, across, beside)
    return (basis.reshape(orbitals.shape), residual.reshape(orbitals.shape))


def solution(mesh):
    return jax.shard_map(
        local,
        mesh=mesh,
        in_specs=(P("band", "domain", None, None), P("domain", None, None)),
        out_specs=(P("band", "domain", None, None), P("band", "domain", None, None)),
        check_vma=False,
    )
```

```python
import jax
import jax.numpy as jnp
from jax import lax
from jax.experimental import pallas as pl
from jax.experimental.pallas import tpu as pltpu
from jax.sharding import PartitionSpec as P

stencil_weights = (-205.0 / 72.0, 8.0 / 5.0, -1.0 / 5.0, 8.0 / 315.0, -1.0 / 560.0)
BLK = 8
RING = 8
F32 = jnp.float32
VMEM = pl.BlockSpec(memory_space=pltpu.VMEM)
SMEM = pl.BlockSpec(memory_space=pltpu.SMEM)


def call(kernel, outs, scratch=(), specs=None, flops=0, bytes_moved=0):
    return pl.pallas_call(
        kernel,
        out_shape=outs,
        in_specs=specs,
        out_specs=jax.tree.map(lambda _: VMEM, outs),
        scratch_shapes=scratch,
        compiler_params=pltpu.CompilerParams(vmem_limit_bytes=32 * 1024 * 1024),
        cost_estimate=pl.CostEstimate(flops=flops, bytes_accessed=bytes_moved, transcendentals=0),
    )


def lanes():
    return lax.broadcasted_iota(jnp.int32, (8, 128), 1)


def subs():
    return lax.broadcasted_iota(jnp.int32, (8, 128), 0)


def folded(rows):
    sub = subs()
    step = 4
    while step:
        lower = (sub & step) == 0
        merged = []
        for first, second in zip(rows[:step], rows[step:]):
            if first is not None:
                first = first + pltpu.roll(first, 8 - step, 0)
            if second is not None:
                second = second + pltpu.roll(second, step, 0)
            if first is None and second is None:
                merged.append(None)
            else:
                merged.append(
                    jnp.where(lower, 0.0 if first is None else first, 0.0 if second is None else second)
                )
        rows = merged
        step //= 2
    return rows[0]


def pair_sums(jobs, load, chunks):
    lane = lanes()
    result = jnp.zeros((8, 128), F32)
    for pairs in jobs:
        used = sorted({n for pair in pairs for n in pair})

        def body(c, sums, pairs=pairs, used=used):
            for step in range(4):
                rows = {n: load[n](4 * c + step) for n in used}
                sums = tuple(s + rows[q] * rows[r] for s, (q, r) in zip(sums, pairs))
            return sums

        zero = jnp.zeros((8, 128), F32)
        sums = lax.fori_loop(0, chunks // 4, body, (zero,) * len(pairs))
        columns = {}
        for s, (q, r) in zip(sums, pairs):
            columns.setdefault(32 * (r // 8) + q, [None] * 8)[r % 8] = s
        for place, rows in columns.items():
            column = jnp.sum(folded(rows), axis=1, keepdims=True)
            result = result + jnp.where(lane == place, column, 0.0)
    return result


def loader(ref, index):
    return lambda c: ref[index, pl.ds(pl.multiple_of(c * 8, 8), 8), :]


def move(tile, source, target):
    lane = lanes()
    if source != target:
        tile = pltpu.roll(tile, (target - source) % 128, 1)
    return jnp.where((lane >= target) & (lane < target + 8), tile, 0.0)


def spread_lane(tile, k):
    return jnp.broadcast_to(tile[:, k : k + 1], (8, 128))


def rows_of(refs):
    return [(r, i) for r in refs for i in range(r.shape[0])]


def unpacked(sums):
    lane = lanes()
    parts = [sums] + [pltpu.roll(sums, 128 - 32 * n, 1) for n in (1, 2)]
    return [jnp.where(lane < 32, part, 0.0) for part in parts]


def tall(tiles):
    return jnp.concatenate(tiles + [jnp.zeros((128 - 8 * len(tiles), 128), F32)], axis=0)


OWN = list(range(16, 24))
IMAGE = list(range(24, 32))


def split(pairs, size=36):
    if not pairs:
        return []
    count = -(-len(pairs) // size)
    size = -(-len(pairs) // count)
    return [pairs[n : n + size] for n in range(0, len(pairs), size)]


def stage_kernel(parts, fresh, imaged, last, *refs):
    out = refs[-1]
    pieces, refs = refs[:parts], refs[parts:-1]
    own, image, before = (refs[0], refs[1], refs[2:]) if imaged else (refs[0], None, refs[1:])
    chunks = own.shape[1] // 8
    load = {n: loader(r, i) for n, (r, i) in enumerate(rows_of(pieces))}
    load |= {n: loader(own, n - 16) for n in OWN}
    if imaged:
        load |= {n: loader(image, n - 24) for n in IMAGE}
    jobs = split([(q, r) for q in OWN for r in fresh])
    jobs += split([(q, r) for q in fresh for r in range(q + 1)])
    jobs += split([(q, r) for q in IMAGE for r in imaged])
    total = pair_sums(jobs, load, chunks)
    for part in before:
        total = total + part[...]
    if last:
        for n in range(out.shape[0]):
            out[n] = total
    else:
        out[...] = total


def total_kernel(cells_total, parts_ref, out):
    out[...] = jnp.sum(parts_ref[...], axis=0) / cells_total


def combine_kernel(band_ref, sums_ref, *refs):
    *pieces, own, out, weights_ref, gram_ref, splat = refs
    band = band_ref[0]
    lane, sub = lanes(), subs()
    tiles = unpacked(sums_ref[...])
    turned = jnp.transpose(tall(tiles))
    w0, w1, w2 = (
        jnp.where(lane < 24, tile + jnp.where(lane == sub + 8 * n, 0.0, turned[8 * n : 8 * n + 8]), 0.0)
        for n, tile in enumerate(tiles)
    )
    later = band >= 2
    second = band == 1

    def taken(position):
        place = position & 7
        return later | (second & (place >= 2) & (place <= 5))

    row_in = taken(sub)
    lane_in = (lane >= 16) | taken(lane)
    kept = row_in & lane_in
    w0 = jnp.where(kept, w0, jnp.where(lane == sub, 1.0, 0.0))
    w1 = jnp.where(kept, w1, jnp.where(lane == 8 + sub, 1.0, 0.0))
    w0 = w0 + jnp.where(lane == 24 + sub, 1.0, 0.0)
    w1 = w1 + jnp.where(lane == 32 + sub, 1.0, 0.0)
    w2 = jnp.where(lane_in, w2, 0.0) + jnp.where(lane == 40 + sub, 1.0, 0.0)
    tiles = [w0, w1, w2]
    for k in range(16):
        v, s = divmod(k, 8)
        row = tiles[v][s : s + 1, :]
        row = row / jnp.broadcast_to(row[:, k : k + 1], (1, 128))
        row = jnp.broadcast_to(row, (8, 128))
        for u in range(v, 3):
            column = spread_lane(tiles[u], k)
            if u == v:
                column = jnp.where(sub > s, column, 0.0)
            tiles[u] = tiles[u] - column * row
    plain = tiles[2]
    scaled = plain
    for k in range(8):
        row = scaled[k : k + 1, :]
        row = row / jnp.broadcast_to(row[:, 16 + k : 17 + k], (1, 128))
        column = jnp.where(sub > k, spread_lane(scaled, 16 + k), 0.0)
        scaled = scaled - column * jnp.broadcast_to(row, (8, 128))
    pivots = jnp.sum(jnp.where(lane == 16 + sub, scaled, 0.0), axis=1, keepdims=True)
    scaled = scaled / jnp.sqrt(jnp.broadcast_to(pivots, (8, 128)))
    weights = jnp.where(later, plain, scaled)
    weights_ref[...] = weights
    gram_ref[...] = jnp.where(later, move(plain, 16, 0), jnp.where(lane == sub, 1.0, 0.0))
    for c in range(24):
        splat[c] = spread_lane(weights, 24 + c)
    rows = rows_of(pieces) + [(own, i) for i in range(BLK)]

    def combine(places, plus_own):
        def body(c, carry):
            part = pl.ds(pl.multiple_of(c * 32, 32), 32)
            for low in (0, 4):
                if plus_own:
                    totals = [own[low + k, part, :] for k in range(4)]
                else:
                    totals = [jnp.zeros((32, 128), F32)] * 4
                for n in places:
                    r, i = rows[n]
                    cells = r[i, part, :]
                    totals = [
                        t + splat[n, pl.ds(low + k, 1), :] * cells for k, t in enumerate(totals)
                    ]
                for k in range(4):
                    out[low + k, part, :] = totals[k]
            return carry

        lax.fori_loop(0, own.shape[1] // 32, body, 0)

    pl.when(later)(lambda: combine(range(16), True))
    pl.when(second)(lambda: combine((2, 3, 4, 5, 10, 11, 12, 13, *OWN), False))
    pl.when(band == 0)(lambda: combine(OWN, False))


def inner_kernel(f_ref, v_ref, out, *sums):
    def body(i, carry):
        layers = [f_ref[i, x] for x in range(4)]
        for x in range(4):
            here = layers[x]
            total = 3.0 * stencil_weights[0] * here
            for offset in range(1, 5):
                beside = pltpu.roll(here, offset, 0) + pltpu.roll(here, 64 - offset, 0)
                beside = beside + pltpu.roll(here, offset, 1) + pltpu.roll(here, 128 - offset, 1)
                if x + offset < 4:
                    beside = beside + layers[x + offset]
                if x - offset >= 0:
                    beside = beside + layers[x - offset]
                total = total + stencil_weights[offset] * beside
            out[i, x] = -0.5 * total + v_ref[x] * here
        return carry

    lax.fori_loop(0, BLK, body, 0)
    if sums:

        def row(i):
            return lambda c: f_ref[i, c // 8, pl.ds(pl.multiple_of((c % 8) * 8, 8), 8), :]

        load = {n: row(n - 16) for n in OWN}
        sums[0][...] = pair_sums([[(q, r) for q in OWN for r in range(16, q + 1)]], load, 32)


def edged(inner, x, left, right):
    total = None
    for offset in range(1, 5):
        if x + offset >= 4:
            term = stencil_weights[offset] * right(x + offset - 4)
            total = term if total is None else total + term
        if x - offset < 0:
            term = stencil_weights[offset] * left(x - offset + 4)
            total = term if total is None else total + term
    return inner - 0.5 * total


def image_kernel(own, inner, left, right, out, sums):
    def body(i, carry):
        for x in range(4):
            part = pl.ds(64 * x, 64)
            out[i, part, :] = edged(
                inner[i, part, :],
                x,
                lambda n: left[i, pl.ds(64 * n, 64), :],
                lambda n: right[i, pl.ds(64 * n, 64), :],
            )
        return carry

    lax.fori_loop(0, BLK, body, 0)
    load = {n: loader(own, n - 16) for n in OWN}
    load |= {n: loader(out, n - 24) for n in IMAGE}
    jobs = [[(q, r) for q in IMAGE for r in OWN if r <= q - 8]]
    sums[...] = pair_sums(jobs, load, own.shape[1] // 8)


def dot(left, right, turn_left=False, turn_right=False):
    dims = (((0 if turn_left else 1,), (1 if turn_right else 0,)), ((), ()))
    return lax.dot_general(
        left, right, dims, precision=lax.Precision.HIGHEST, preferred_element_type=F32
    )


def places(y, home=None):
    row = lax.broadcasted_iota(jnp.int32, (128, 128), 0)
    lane = lax.broadcasted_iota(jnp.int32, (128, 128), 1)
    distance = (row + 2) >> 2
    distance = jnp.where(((row + 2) & 2) == 0, -distance, distance)
    piece = (y + distance) & 7
    target = (piece & 1) * 8 + (piece >> 1) * 2 + (row & 1)
    if home is None:
        target = jnp.where(row < 16, target, row)
    else:
        target = jnp.where((piece & 1) == home, -1, target)
        target = jnp.where(row < 16, target, row - 16 + 8 * home)
    return jnp.where((lane == target) & (row < 24), 1.0, 0.0)


def coeff_kernel(band_ref, weights_ref, gram_ref, own_ref, near_ref, far_ref, out):
    lane, sub = lanes(), subs()
    wide = lax.broadcasted_iota(jnp.int32, (128, 128), 1)
    row = lax.broadcasted_iota(jnp.int32, (128, 128), 0)
    place = places(band_ref[0] & 7)
    weights = jnp.where(lane < 24, pltpu.roll(weights_ref[...], 104, 1), 0.0)
    weights = dot(weights, place)

    def with_mirror(packed):
        tiles = unpacked(packed)
        mirror = jnp.transpose(tall([move(tiles[2], 24, 0)]))[0:8]
        tiles[2] = tiles[2] + move(jnp.where(lane == sub, 0.0, mirror), 0, 24)
        return tall(tiles)

    def image_columns(matrix, place, source, target):
        columns = dot(place, matrix, turn_left=True)
        columns = pltpu.roll(columns, (target - source) % 128, 1)
        return jnp.where((wide >= target) & (wide < target + 8), columns, 0.0)

    def visiting(n):
        packed = jnp.where(band_ref[0] < RING, near_ref[n], far_ref[n])
        return image_columns(with_mirror(packed), places(n, n), 24, 8 * n)

    block0, block1 = visiting(0), visiting(1)
    block = image_columns(with_mirror(own_ref[...]), place, 24, 16)
    half = dot(weights, block0 + block1 + block)
    half = half + dot(weights, jnp.where(row < 16, block, 0.0), turn_right=True)
    theta = dot(half, tall([weights]), turn_right=True)
    work = gram_ref[...] + move(theta, 0, 8)
    for k in range(8):
        line = work[k : k + 1, :]
        line = jnp.broadcast_to(line / jnp.broadcast_to(line[:, k : k + 1], (1, 128)), (8, 128))
        work = jnp.where(sub == k, line, work - spread_lane(work, k) * line)
    for j in range(8):
        out[j] = spread_lane(work, 8 + j)


def partial_kernel(f_ref, inner_ref, splat, out):
    def body(c, carry):
        part = pl.ds(pl.multiple_of(c * 32, 32), 32)
        for low in (0, 4):
            totals = [inner_ref[low + k, part, :] for k in range(4)]
            for i in range(BLK):
                cells = f_ref[i, part, :]
                totals = [
                    t - splat[low + k, pl.ds(i, 1), :] * cells for k, t in enumerate(totals)
                ]
            for k in range(4):
                out[low + k, part, :] = totals[k]
        return carry

    lax.fori_loop(0, f_ref.shape[1] // 32, body, 0)


def edge_kernel(words, partial, across, beside, out):
    def run(left, right):
        def body(i, carry):
            for x in range(4):
                part = pl.ds(64 * x, 64)
                out[i, part, :] = edged(
                    partial[i, part, :],
                    x,
                    lambda n: left[i, pl.ds(64 * n, 64), :],
                    lambda n: right[i, pl.ds(64 * n, 64), :],
                )
            return carry

        lax.fori_loop(0, BLK, body, 0)

    pl.when(words[1] == 0)(lambda: run(across, beside))
    pl.when(words[1] == 1)(lambda: run(beside, across))


def domain_parts(copies):
    return lax.all_to_all(copies, "domain", 0, 0)


def ring_shift(block, step):
    pairs = [(z * RING + y, z * RING + (y + step) % RING) for z in range(2) for y in range(RING)]
    return lax.ppermute(block, "band", pairs)


def neighbours(block):
    count = lax.axis_size("domain")
    left = lax.ppermute(block, "domain", [(i, (i + 1) % count) for i in range(count)])
    right = lax.ppermute(block, "domain", [((i + 1) % count, i) for i in range(count)])
    return left, right


def exchanged(block):
    count = lax.axis_size("domain")
    across = [(i, (i + 1 if i % 2 else i - 1) % count) for i in range(count)]
    beside = [(i, i ^ 1) for i in range(count)]
    return lax.ppermute(block, "domain", across), lax.ppermute(block, "domain", beside)


def local(orbitals, potential):
    blocks, slab_width, rows_y, rows_z = orbitals.shape
    domain = lax.axis_size("domain")
    cells_total = float(slab_width * rows_y * rows_z * domain)
    band = lax.axis_index("band")
    words = jnp.stack([band, lax.axis_index("domain") & 1]).astype(jnp.int32)
    flat = (blocks, slab_width * rows_y, rows_z)
    big = flat[0] * flat[1] * flat[2]
    slab = jax.ShapeDtypeStruct(flat, F32)
    field = jax.ShapeDtypeStruct(orbitals.shape, F32)
    tile = jax.ShapeDtypeStruct((8, 128), F32)

    def inner_part(block, *sums):
        return call(
            inner_kernel,
            (field, *sums),
            specs=[VMEM] * 2,
            flops=60 * big,
            bytes_moved=8 * big,
        )(block, potential)

    own = orbitals.reshape(flat)
    quarters = [own[2 * k : 2 * k + 2] for k in range(4)]
    arrived = [
        lax.ppermute(quarters[k], "band", [(0, 2 * k), (1, 2 * k + 1)]) for k in (1, 3, 2)
    ]
    inner, sums = inner_part(orbitals, tile)
    arrived, inner, sums, words = lax.optimization_barrier((arrived, inner, sums, words))
    piece = jnp.where(band < 2, quarters[0], 0.0)
    for part in arrived:
        piece = piece + part
    left, right = neighbours(own)
    crossed = lax.ppermute(piece, "band", [(y, y + RING) for y in range(RING)])
    piece = jnp.where(band < RING, piece, crossed)

    def stage(fresh, imaged, pieces, *sums, last=False):
        sources = (*pieces, own, *((image,) if imaged else ()), *sums)
        return call(
            lambda *refs: stage_kernel(len(pieces), fresh, imaged, last, *refs),
            jax.ShapeDtypeStruct((domain, 8, 128), F32) if last else tile,
            specs=[VMEM] * len(sources),
            flops=20 * big,
            bytes_moved=10 * big,
        )(*sources)

    pieces = [piece]
    up, down = ring_shift(piece, 1), ring_shift(piece, -1)
    pieces += [up, down]
    up, down = ring_shift(up, 1), ring_shift(down, -1)
    sums = stage(range(6), (), pieces, sums)
    down, sums = lax.optimization_barrier((down, sums))
    pieces += [up, down]
    up, down = ring_shift(up, 1), ring_shift(down, -1)
    sums = stage(range(6, 10), (), pieces, sums)
    down, sums, left, right = lax.optimization_barrier((down, sums, left, right))
    pieces += [up, down]
    up, down = ring_shift(up[:1], 1), ring_shift(down[1:], -1)
    image, image_sums = call(
        image_kernel, (slab, tile), specs=[VMEM] * 4, flops=50 * big, bytes_moved=20 * big
    )(own, inner.reshape(flat), left, right)
    sums = stage(range(10, 14), range(14), pieces, sums, image_sums)
    pieces += [up, down]
    sums = stage(range(14, 16), range(14, 16), pieces, sums, last=True)
    sums = call(
        lambda *refs: total_kernel(cells_total, *refs),
        tile,
        specs=[VMEM],
        flops=40 * 1024,
        bytes_moved=160 * 1024,
    )(domain_parts(sums))
    basis, weights, gram = call(
        combine_kernel,
        (slab, tile, tile),
        scratch=[pltpu.VMEM((24, 8, 128), F32)],
        specs=[SMEM] + [VMEM] * 11,
        flops=48 * big,
        bytes_moved=16 * big,
    )(words, sums, *pieces, own)
    across, beside = exchanged(basis)
    inner = inner_part(basis.reshape(orbitals.shape))[0].reshape(flat)
    shared = sums
    other = lax.ppermute(shared, "band", [(0, 1), (1, 0)])
    shared = jnp.stack([jnp.where(band == 0, shared, other), jnp.where(band == 0, other, shared)])
    shared = jnp.where(band < 2, shared, 0.0)
    shared = shared + lax.ppermute(shared, "band", [(0, 4), (1, 5)])
    shared = shared + lax.ppermute(shared, "band", [(0, 2), (1, 3), (4, 6), (5, 7)])
    far = lax.ppermute(shared, "band", [(y, y + RING) for y in range(RING)])
    splat = call(
        coeff_kernel, jax.ShapeDtypeStruct((8, 8, 128), F32), specs=[SMEM] + [VMEM] * 5
    )(words, weights, gram, sums, shared, far)
    partial = call(
        partial_kernel, slab, specs=[VMEM] * 3, flops=16 * big, bytes_moved=12 * big
    )(basis, inner, splat)
    residual = call(
        edge_kernel, slab, specs=[SMEM] + [VMEM] * 3, flops=20 * big, bytes_moved=16 * big
    )(words, partial, across, beside)
    return (basis.reshape(orbitals.shape), residual.reshape(orbitals.shape))


def solution(mesh):
    return jax.shard_map(
        local,
        mesh=mesh,
        in_specs=(P("band", "domain", None, None), P("domain", None, None)),
        out_specs=(P("band", "domain", None, None), P("band", "domain", None, None)),
        check_vma=False,
    )
```

```python
import jax
import jax.numpy as jnp
from jax import lax
from jax.experimental import pallas as pl
from jax.experimental.pallas import tpu as pltpu
from jax.sharding import PartitionSpec as P

stencil_weights = (-205.0 / 72.0, 8.0 / 5.0, -1.0 / 5.0, 8.0 / 315.0, -1.0 / 560.0)
BLK = 8
RING = 8
F32 = jnp.float32
VMEM = pl.BlockSpec(memory_space=pltpu.VMEM)


def call(kernel, outs, scratch=(), specs=None, flops=0, bytes_moved=0):
    return pl.pallas_call(
        kernel,
        out_shape=outs,
        in_specs=specs,
        out_specs=jax.tree.map(lambda _: VMEM, outs),
        scratch_shapes=scratch,
        compiler_params=pltpu.CompilerParams(vmem_limit_bytes=32 * 1024 * 1024),
        cost_estimate=pl.CostEstimate(flops=flops, bytes_accessed=bytes_moved, transcendentals=0),
    )


def lanes():
    return lax.broadcasted_iota(jnp.int32, (8, 128), 1)


def subs():
    return lax.broadcasted_iota(jnp.int32, (8, 128), 0)


def folded(rows):
    sub = subs()
    step = 4
    while step:
        lower = (sub & step) == 0
        merged = []
        for first, second in zip(rows[:step], rows[step:]):
            if first is not None:
                first = first + pltpu.roll(first, 8 - step, 0)
            if second is not None:
                second = second + pltpu.roll(second, step, 0)
            if first is None and second is None:
                merged.append(None)
            else:
                merged.append(
                    jnp.where(lower, 0.0 if first is None else first, 0.0 if second is None else second)
                )
        rows = merged
        step //= 2
    return rows[0]


def pair_sums(jobs, load, chunks):
    lane = lanes()
    result = jnp.zeros((8, 128), F32)
    for pairs in jobs:
        used = sorted({n for pair in pairs for n in pair})

        def body(c, sums, pairs=pairs, used=used):
            for step in range(4):
                rows = {n: load[n](4 * c + step) for n in used}
                sums = tuple(s + rows[q] * rows[r] for s, (q, r) in zip(sums, pairs))
            return sums

        zero = jnp.zeros((8, 128), F32)
        sums = lax.fori_loop(0, chunks // 4, body, (zero,) * len(pairs))
        columns = {}
        for s, (q, r) in zip(sums, pairs):
            columns.setdefault(32 * (r // 8) + q, [None] * 8)[r % 8] = s
        for place, rows in columns.items():
            column = jnp.sum(folded(rows), axis=1, keepdims=True)
            result = result + jnp.where(lane == place, column, 0.0)
    return result


def loader(ref, index):
    return lambda c: ref[index, pl.ds(pl.multiple_of(c * 8, 8), 8), :]


def move(tile, source, target):
    lane = lanes()
    if source != target:
        tile = pltpu.roll(tile, (target - source) % 128, 1)
    return jnp.where((lane >= target) & (lane < target + 8), tile, 0.0)


def spread_lane(tile, k):
    return jnp.broadcast_to(tile[:, k : k + 1], (8, 128))


def rows_of(refs):
    return [(r, i) for r in refs for i in range(r.shape[0])]


def unpacked(sums):
    lane = lanes()
    parts = [sums] + [pltpu.roll(sums, 128 - 32 * n, 1) for n in (1, 2)]
    return [jnp.where(lane < 32, part, 0.0) for part in parts]


def tall(tiles):
    return jnp.concatenate(tiles + [jnp.zeros((128 - 8 * len(tiles), 128), F32)], axis=0)


OWN = list(range(16, 24))
IMAGE = list(range(24, 32))


def split(pairs, size=36):
    if not pairs:
        return []
    count = -(-len(pairs) // size)
    size = -(-len(pairs) // count)
    return [pairs[n : n + size] for n in range(0, len(pairs), size)]


def stage_kernel(parts, fresh, imaged, last, *refs):
    out = refs[-1]
    pieces, refs = refs[:parts], refs[parts:-1]
    own, image, before = (refs[0], refs[1], refs[2:]) if imaged else (refs[0], None, refs[1:])
    chunks = own.shape[1] // 8
    load = {n: loader(r, i) for n, (r, i) in enumerate(rows_of(pieces))}
    load |= {n: loader(own, n - 16) for n in OWN}
    if imaged:
        load |= {n: loader(image, n - 24) for n in IMAGE}
    jobs = split([(q, r) for q in OWN for r in fresh])
    jobs += split([(q, r) for q in fresh for r in range(q + 1)])
    jobs += split([(q, r) for q in IMAGE for r in imaged])
    total = pair_sums(jobs, load, chunks)
    for part in before:
        total = total + part[...]
    if last:
        for n in range(out.shape[0]):
            out[n] = total
    else:
        out[...] = total


def total_kernel(cells_total, parts_ref, out):
    out[...] = jnp.sum(parts_ref[...], axis=0) / cells_total


def combine_kernel(sums_ref, *refs):
    *pieces, own, out, weights_ref, gram_ref, splat = refs
    band = lax.axis_index("band")
    lane, sub = lanes(), subs()
    tiles = unpacked(sums_ref[...])
    turned = jnp.transpose(tall(tiles))
    w0, w1, w2 = (
        jnp.where(lane < 24, tile + jnp.where(lane == sub + 8 * n, 0.0, turned[8 * n : 8 * n + 8]), 0.0)
        for n, tile in enumerate(tiles)
    )
    later = band >= 2
    second = band == 1

    def taken(position):
        place = position & 7
        return later | (second & (place >= 2) & (place <= 5))

    row_in = taken(sub)
    lane_in = (lane >= 16) | taken(lane)
    kept = row_in & lane_in
    w0 = jnp.where(kept, w0, jnp.where(lane == sub, 1.0, 0.0))
    w1 = jnp.where(kept, w1, jnp.where(lane == 8 + sub, 1.0, 0.0))
    w0 = w0 + jnp.where(lane == 24 + sub, 1.0, 0.0)
    w1 = w1 + jnp.where(lane == 32 + sub, 1.0, 0.0)
    w2 = jnp.where(lane_in, w2, 0.0) + jnp.where(lane == 40 + sub, 1.0, 0.0)
    tiles = [w0, w1, w2]
    for k in range(16):
        v, s = divmod(k, 8)
        row = tiles[v][s : s + 1, :]
        row = row / jnp.broadcast_to(row[:, k : k + 1], (1, 128))
        row = jnp.broadcast_to(row, (8, 128))
        for u in range(v, 3):
            column = spread_lane(tiles[u], k)
            if u == v:
                column = jnp.where(sub > s, column, 0.0)
            tiles[u] = tiles[u] - column * row
    plain = tiles[2]
    scaled = plain
    for k in range(8):
        row = scaled[k : k + 1, :]
        row = row / jnp.broadcast_to(row[:, 16 + k : 17 + k], (1, 128))
        column = jnp.where(sub > k, spread_lane(scaled, 16 + k), 0.0)
        scaled = scaled - column * jnp.broadcast_to(row, (8, 128))
    pivots = jnp.sum(jnp.where(lane == 16 + sub, scaled, 0.0), axis=1, keepdims=True)
    scaled = scaled / jnp.sqrt(jnp.broadcast_to(pivots, (8, 128)))
    weights = jnp.where(later, plain, scaled)
    weights_ref[...] = weights
    gram_ref[...] = jnp.where(later, move(plain, 16, 0), jnp.where(lane == sub, 1.0, 0.0))
    for c in range(24):
        splat[c] = spread_lane(weights, 24 + c)
    rows = rows_of(pieces) + [(own, i) for i in range(BLK)]

    def combine(places, plus_own):
        def body(c, carry):
            part = pl.ds(pl.multiple_of(c * 32, 32), 32)
            for low in (0, 4):
                if plus_own:
                    totals = [own[low + k, part, :] for k in range(4)]
                else:
                    totals = [jnp.zeros((32, 128), F32)] * 4
                for n in places:
                    r, i = rows[n]
                    cells = r[i, part, :]
                    totals = [
                        t + splat[n, pl.ds(low + k, 1), :] * cells for k, t in enumerate(totals)
                    ]
                for k in range(4):
                    out[low + k, part, :] = totals[k]
            return carry

        lax.fori_loop(0, own.shape[1] // 32, body, 0)

    pl.when(later)(lambda: combine(range(16), True))
    pl.when(second)(lambda: combine((2, 3, 4, 5, 10, 11, 12, 13, *OWN), False))
    pl.when(band == 0)(lambda: combine(OWN, False))


def inner_kernel(f_ref, v_ref, out, *sums):
    def body(i, carry):
        layers = [f_ref[i, x] for x in range(4)]
        for x in range(4):
            here = layers[x]
            total = 3.0 * stencil_weights[0] * here
            for offset in range(1, 5):
                beside = pltpu.roll(here, offset, 0) + pltpu.roll(here, 64 - offset, 0)
                beside = beside + pltpu.roll(here, offset, 1) + pltpu.roll(here, 128 - offset, 1)
                if x + offset < 4:
                    beside = beside + layers[x + offset]
                if x - offset >= 0:
                    beside = beside + layers[x - offset]
                total = total + stencil_weights[offset] * beside
            out[i, x] = -0.5 * total + v_ref[x] * here
        return carry

    lax.fori_loop(0, BLK, body, 0)
    if sums:

        def row(i):
            return lambda c: f_ref[i, c // 8, pl.ds(pl.multiple_of((c % 8) * 8, 8), 8), :]

        load = {n: row(n - 16) for n in OWN}
        sums[0][...] = pair_sums([[(q, r) for q in OWN for r in range(16, q + 1)]], load, 32)


def edged(inner, x, left, right):
    total = None
    for offset in range(1, 5):
        if x + offset >= 4:
            term = stencil_weights[offset] * right(x + offset - 4)
            total = term if total is None else total + term
        if x - offset < 0:
            term = stencil_weights[offset] * left(x - offset + 4)
            total = term if total is None else total + term
    return inner - 0.5 * total


def image_kernel(own, inner, left, right, out, sums):
    def body(i, carry):
        for x in range(4):
            part = pl.ds(64 * x, 64)
            out[i, part, :] = edged(
                inner[i, part, :],
                x,
                lambda n: left[i, pl.ds(64 * n, 64), :],
                lambda n: right[i, pl.ds(64 * n, 64), :],
            )
        return carry

    lax.fori_loop(0, BLK, body, 0)
    load = {n: loader(own, n - 16) for n in OWN}
    load |= {n: loader(out, n - 24) for n in IMAGE}
    jobs = [[(q, r) for q in IMAGE for r in OWN if r <= q - 8]]
    sums[...] = pair_sums(jobs, load, own.shape[1] // 8)


def dot(left, right, turn_left=False, turn_right=False):
    dims = (((0 if turn_left else 1,), (1 if turn_right else 0,)), ((), ()))
    return lax.dot_general(
        left, right, dims, precision=lax.Precision.HIGHEST, preferred_element_type=F32
    )


def places(y, home=None):
    row = lax.broadcasted_iota(jnp.int32, (128, 128), 0)
    lane = lax.broadcasted_iota(jnp.int32, (128, 128), 1)
    distance = (row + 2) >> 2
    distance = jnp.where(((row + 2) & 2) == 0, -distance, distance)
    piece = (y + distance) & 7
    target = (piece & 1) * 8 + (piece >> 1) * 2 + (row & 1)
    if home is None:
        target = jnp.where(row < 16, target, row)
    else:
        target = jnp.where((piece & 1) == home, -1, target)
        target = jnp.where(row < 16, target, row - 16 + 8 * home)
    return jnp.where((lane == target) & (row < 24), 1.0, 0.0)


def with_mirror(packed):
    lane, sub = lanes(), subs()
    tiles = unpacked(packed)
    mirror = jnp.transpose(tall([move(tiles[2], 24, 0)]))[0:8]
    tiles[2] = tiles[2] + move(jnp.where(lane == sub, 0.0, mirror), 0, 24)
    return tall(tiles)


def image_columns(packed, place, target):
    wide = lax.broadcasted_iota(jnp.int32, (128, 128), 1)
    columns = dot(place, with_mirror(packed), turn_left=True)
    columns = pltpu.roll(columns, (target - 24) % 128, 1)
    return jnp.where((wide >= target) & (wide < target + 8), columns, 0.0)


def prepare_kernel(weights_ref, own_ref, ordered_ref, half_ref):
    lane = lanes()
    row = lax.broadcasted_iota(jnp.int32, (128, 128), 0)
    place = places(lax.axis_index("band") & 7)
    weights = jnp.where(lane < 24, pltpu.roll(weights_ref[...], 104, 1), 0.0)
    weights = dot(weights, place)
    block = image_columns(own_ref[...], place, 16)
    half = dot(weights, block)
    half_ref[...] = half + dot(weights, jnp.where(row < 16, block, 0.0), turn_right=True)
    ordered_ref[...] = weights


def coeff_kernel(weights_ref, half_ref, gram_ref, near_ref, far_ref, out):
    lane, sub = lanes(), subs()
    row = lax.broadcasted_iota(jnp.int32, (128, 128), 0)
    near = lax.axis_index("band") < RING
    weights = weights_ref[...]

    def visiting(n):
        packed = jnp.where(near, near_ref[n], far_ref[n])
        return image_columns(packed, places(n, n), 8 * n)

    half = half_ref[...] + dot(weights, jnp.where(row < 16, visiting(0) + visiting(1), 0.0))
    theta = dot(half, tall([weights]), turn_right=True)
    work = gram_ref[...] + move(theta, 0, 8)
    for k in range(8):
        line = work[k : k + 1, :]
        line = jnp.broadcast_to(line / jnp.broadcast_to(line[:, k : k + 1], (1, 128)), (8, 128))
        work = jnp.where(sub == k, line, work - spread_lane(work, k) * line)
    for j in range(8):
        out[j] = spread_lane(work, 8 + j)


def partial_kernel(f_ref, inner_ref, splat, out):
    def body(c, carry):
        part = pl.ds(pl.multiple_of(c * 32, 32), 32)
        for low in (0, 4):
            totals = [inner_ref[low + k, part, :] for k in range(4)]
            for i in range(BLK):
                cells = f_ref[i, part, :]
                totals = [
                    t - splat[low + k, pl.ds(i, 1), :] * cells for k, t in enumerate(totals)
                ]
            for k in range(4):
                out[low + k, part, :] = totals[k]
        return carry

    lax.fori_loop(0, f_ref.shape[1] // 32, body, 0)


def edge_kernel(partial, across, beside, out):
    def run(left, right):
        def body(i, carry):
            for x in range(4):
                part = pl.ds(64 * x, 64)
                out[i, part, :] = edged(
                    partial[i, part, :],
                    x,
                    lambda n: left[i, pl.ds(64 * n, 64), :],
                    lambda n: right[i, pl.ds(64 * n, 64), :],
                )
            return carry

        lax.fori_loop(0, BLK, body, 0)

    odd = lax.axis_index("domain") & 1
    pl.when(odd == 0)(lambda: run(across, beside))
    pl.when(odd == 1)(lambda: run(beside, across))


def domain_parts(copies):
    return lax.all_to_all(copies, "domain", 0, 0)


def ring_shift(block, step):
    pairs = [(z * RING + y, z * RING + (y + step) % RING) for z in range(2) for y in range(RING)]
    return lax.ppermute(block, "band", pairs)


def neighbours(block):
    count = lax.axis_size("domain")
    left = lax.ppermute(block, "domain", [(i, (i + 1) % count) for i in range(count)])
    right = lax.ppermute(block, "domain", [((i + 1) % count, i) for i in range(count)])
    return left, right


def exchanged(block):
    count = lax.axis_size("domain")
    across = [(i, (i + 1 if i % 2 else i - 1) % count) for i in range(count)]
    beside = [(i, i ^ 1) for i in range(count)]
    return lax.ppermute(block, "domain", across), lax.ppermute(block, "domain", beside)


def local(orbitals, potential):
    blocks, slab_width, rows_y, rows_z = orbitals.shape
    domain = lax.axis_size("domain")
    cells_total = float(slab_width * rows_y * rows_z * domain)
    band = lax.axis_index("band")
    flat = (blocks, slab_width * rows_y, rows_z)
    big = flat[0] * flat[1] * flat[2]
    slab = jax.ShapeDtypeStruct(flat, F32)
    field = jax.ShapeDtypeStruct(orbitals.shape, F32)
    tile = jax.ShapeDtypeStruct((8, 128), F32)

    def inner_part(block, *sums):
        return call(
            inner_kernel,
            (field, *sums),
            specs=[VMEM] * 2,
            flops=60 * big,
            bytes_moved=8 * big,
        )(block, potential)

    own = orbitals.reshape(flat)
    quarters = [own[2 * k : 2 * k + 2] for k in range(4)]
    arrived = [
        lax.ppermute(quarters[k], "band", [(0, 2 * k), (1, 2 * k + 1)]) for k in (1, 3, 2)
    ]
    inner, sums = inner_part(orbitals, tile)
    arrived, inner, sums = lax.optimization_barrier((arrived, inner, sums))
    piece = jnp.where(band < 2, quarters[0], 0.0)
    for part in arrived:
        piece = piece + part
    left, right = neighbours(own)
    crossed = lax.ppermute(piece, "band", [(y, y + RING) for y in range(RING)])
    piece = jnp.where(band < RING, piece, crossed)

    def stage(fresh, imaged, pieces, *sums, last=False):
        sources = (*pieces, own, *((image,) if imaged else ()), *sums)
        return call(
            lambda *refs: stage_kernel(len(pieces), fresh, imaged, last, *refs),
            jax.ShapeDtypeStruct((domain, 8, 128), F32) if last else tile,
            specs=[VMEM] * len(sources),
            flops=20 * big,
            bytes_moved=10 * big,
        )(*sources)

    pieces = [piece]
    up, down = ring_shift(piece, 1), ring_shift(piece, -1)
    pieces += [up, down]
    up, down = ring_shift(up, 1), ring_shift(down, -1)
    sums = stage(range(6), (), pieces, sums)
    down, sums = lax.optimization_barrier((down, sums))
    pieces += [up, down]
    up, down = ring_shift(up, 1), ring_shift(down, -1)
    sums = stage(range(6, 10), (), pieces, sums)
    down, sums, left, right = lax.optimization_barrier((down, sums, left, right))
    pieces += [up, down]
    up, down = ring_shift(up[:1], 1), ring_shift(down[1:], -1)
    image, image_sums = call(
        image_kernel, (slab, tile), specs=[VMEM] * 4, flops=50 * big, bytes_moved=20 * big
    )(own, inner.reshape(flat), left, right)
    sums = stage(range(10, 14), range(14), pieces, sums, image_sums)
    pieces += [up, down]
    sums = stage(range(14, 16), range(14, 16), pieces, sums, last=True)
    sums = call(
        lambda *refs: total_kernel(cells_total, *refs),
        tile,
        specs=[VMEM],
        flops=40 * 1024,
        bytes_moved=160 * 1024,
    )(domain_parts(sums))
    basis, weights, gram = call(
        combine_kernel,
        (slab, tile, tile),
        scratch=[pltpu.VMEM((24, 8, 128), F32)],
        specs=[VMEM] * 11,
        flops=48 * big,
        bytes_moved=16 * big,
    )(sums, *pieces, own)
    across, beside = exchanged(basis)
    inner = inner_part(basis.reshape(orbitals.shape))[0].reshape(flat)
    shared = sums
    other = lax.ppermute(shared, "band", [(0, 1), (1, 0)])
    shared = jnp.stack([jnp.where(band == 0, shared, other), jnp.where(band == 0, other, shared)])
    shared = jnp.where(band < 2, shared, 0.0)
    shared = shared + lax.ppermute(shared, "band", [(0, 4), (1, 5)])
    shared = shared + lax.ppermute(shared, "band", [(0, 2), (1, 3), (4, 6), (5, 7)])
    far = lax.ppermute(shared, "band", [(y, y + RING) for y in range(RING)])
    ordered, half = call(prepare_kernel, (tile, tile), specs=[VMEM] * 2)(weights, sums)
    splat = call(coeff_kernel, jax.ShapeDtypeStruct((8, 8, 128), F32), specs=[VMEM] * 5)(
        ordered, half, gram, shared, far
    )
    partial = call(
        partial_kernel, slab, specs=[VMEM] * 3, flops=16 * big, bytes_moved=12 * big
    )(basis, inner, splat)
    residual = call(
        edge_kernel, slab, specs=[VMEM] * 3, flops=20 * big, bytes_moved=16 * big
    )(partial, across, beside)
    return (basis.reshape(orbitals.shape), residual.reshape(orbitals.shape))


def solution(mesh):
    return jax.shard_map(
        local,
        mesh=mesh,
        in_specs=(P("band", "domain", None, None), P("domain", None, None)),
        out_specs=(P("band", "domain", None, None), P("band", "domain", None, None)),
        check_vma=False,
    )
```

```python
import jax
import jax.numpy as jnp
from jax import lax
from jax.experimental import pallas as pl
from jax.experimental.pallas import tpu as pltpu
from jax.sharding import PartitionSpec as P

stencil_weights = (-205.0 / 72.0, 8.0 / 5.0, -1.0 / 5.0, 8.0 / 315.0, -1.0 / 560.0)
BLK = 8
RING = 8
F32 = jnp.float32
VMEM = pl.BlockSpec(memory_space=pltpu.VMEM)


def call(kernel, outs, scratch=(), specs=None, flops=0, bytes_moved=0):
    return pl.pallas_call(
        kernel,
        out_shape=outs,
        in_specs=specs,
        out_specs=jax.tree.map(lambda _: VMEM, outs),
        scratch_shapes=scratch,
        compiler_params=pltpu.CompilerParams(vmem_limit_bytes=32 * 1024 * 1024),
        cost_estimate=pl.CostEstimate(flops=flops, bytes_accessed=bytes_moved, transcendentals=0),
    )


def lanes():
    return lax.broadcasted_iota(jnp.int32, (8, 128), 1)


def subs():
    return lax.broadcasted_iota(jnp.int32, (8, 128), 0)


def folded(rows):
    sub = subs()
    step = 4
    while step:
        lower = (sub & step) == 0
        merged = []
        for first, second in zip(rows[:step], rows[step:]):
            if first is not None:
                first = first + pltpu.roll(first, 8 - step, 0)
            if second is not None:
                second = second + pltpu.roll(second, step, 0)
            if first is None and second is None:
                merged.append(None)
            else:
                merged.append(
                    jnp.where(lower, 0.0 if first is None else first, 0.0 if second is None else second)
                )
        rows = merged
        step //= 2
    return rows[0]


def pair_sums(jobs, load, chunks):
    lane = lanes()
    result = jnp.zeros((8, 128), F32)
    for pairs in jobs:
        used = sorted({n for pair in pairs for n in pair})

        def body(c, sums, pairs=pairs, used=used):
            for step in range(4):
                rows = {n: load[n](4 * c + step) for n in used}
                sums = tuple(s + rows[q] * rows[r] for s, (q, r) in zip(sums, pairs))
            return sums

        zero = jnp.zeros((8, 128), F32)
        sums = lax.fori_loop(0, chunks // 4, body, (zero,) * len(pairs))
        columns = {}
        for s, (q, r) in zip(sums, pairs):
            columns.setdefault(32 * (r // 8) + q, [None] * 8)[r % 8] = s
        for place, rows in columns.items():
            column = jnp.sum(folded(rows), axis=1, keepdims=True)
            result = result + jnp.where(lane == place, column, 0.0)
    return result


def loader(ref, index):
    return lambda c: ref[index, pl.ds(pl.multiple_of(c * 8, 8), 8), :]


def move(tile, source, target):
    lane = lanes()
    if source != target:
        tile = pltpu.roll(tile, (target - source) % 128, 1)
    return jnp.where((lane >= target) & (lane < target + 8), tile, 0.0)


def spread_lane(tile, k):
    return jnp.broadcast_to(tile[:, k : k + 1], (8, 128))


def rows_of(refs):
    return [(r, i) for r in refs for i in range(r.shape[0])]


def unpacked(sums):
    lane = lanes()
    parts = [sums] + [pltpu.roll(sums, 128 - 32 * n, 1) for n in (1, 2)]
    return [jnp.where(lane < 32, part, 0.0) for part in parts]


def tall(tiles):
    return jnp.concatenate(tiles + [jnp.zeros((128 - 8 * len(tiles), 128), F32)], axis=0)


OWN = list(range(16, 24))
IMAGE = list(range(24, 32))


def split(pairs, size=36):
    if not pairs:
        return []
    count = -(-len(pairs) // size)
    size = -(-len(pairs) // count)
    return [pairs[n : n + size] for n in range(0, len(pairs), size)]


def stage_kernel(parts, fresh, imaged, last, *refs):
    out = refs[-1]
    pieces, refs = refs[:parts], refs[parts:-1]
    own, image, before = (refs[0], refs[1], refs[2:]) if imaged else (refs[0], None, refs[1:])
    chunks = own.shape[1] // 8
    load = {n: loader(r, i) for n, (r, i) in enumerate(rows_of(pieces))}
    load |= {n: loader(own, n - 16) for n in OWN}
    if imaged:
        load |= {n: loader(image, n - 24) for n in IMAGE}
    jobs = split([(q, r) for q in OWN for r in fresh])
    jobs += split([(q, r) for q in fresh for r in range(q + 1)])
    jobs += split([(q, r) for q in IMAGE for r in imaged])
    total = pair_sums(jobs, load, chunks)
    for part in before:
        total = total + part[...]
    if last:
        for n in range(out.shape[0]):
            out[n] = total
    else:
        out[...] = total


def total_kernel(cells_total, parts_ref, out):
    out[...] = jnp.sum(parts_ref[...], axis=0) / cells_total


def combine_kernel(sums_ref, *refs):
    *pieces, own, out, weights_ref, gram_ref, splat = refs
    band = lax.axis_index("band")
    lane, sub = lanes(), subs()
    tiles = unpacked(sums_ref[...])
    turned = jnp.transpose(tall(tiles))
    w0, w1, w2 = (
        jnp.where(lane < 24, tile + jnp.where(lane == sub + 8 * n, 0.0, turned[8 * n : 8 * n + 8]), 0.0)
        for n, tile in enumerate(tiles)
    )
    later = band >= 2
    second = band == 1

    def taken(position):
        place = position & 7
        return later | (second & (place >= 2) & (place <= 5))

    row_in = taken(sub)
    lane_in = (lane >= 16) | taken(lane)
    kept = row_in & lane_in
    w0 = jnp.where(kept, w0, jnp.where(lane == sub, 1.0, 0.0))
    w1 = jnp.where(kept, w1, jnp.where(lane == 8 + sub, 1.0, 0.0))
    w0 = w0 + jnp.where(lane == 24 + sub, 1.0, 0.0)
    w1 = w1 + jnp.where(lane == 32 + sub, 1.0, 0.0)
    w2 = jnp.where(lane_in, w2, 0.0) + jnp.where(lane == 40 + sub, 1.0, 0.0)
    tiles = [w0, w1, w2]
    for k in range(16):
        v, s = divmod(k, 8)
        row = tiles[v][s : s + 1, :]
        row = row / jnp.broadcast_to(row[:, k : k + 1], (1, 128))
        row = jnp.broadcast_to(row, (8, 128))
        for u in range(v, 3):
            column = spread_lane(tiles[u], k)
            if u == v:
                column = jnp.where(sub > s, column, 0.0)
            tiles[u] = tiles[u] - column * row
    plain = tiles[2]
    scaled = plain
    for k in range(8):
        row = scaled[k : k + 1, :]
        row = row / jnp.broadcast_to(row[:, 16 + k : 17 + k], (1, 128))
        column = jnp.where(sub > k, spread_lane(scaled, 16 + k), 0.0)
        scaled = scaled - column * jnp.broadcast_to(row, (8, 128))
    pivots = jnp.sum(jnp.where(lane == 16 + sub, scaled, 0.0), axis=1, keepdims=True)
    scaled = scaled / jnp.sqrt(jnp.broadcast_to(pivots, (8, 128)))
    weights = jnp.where(later, plain, scaled)
    weights_ref[...] = weights
    gram_ref[...] = jnp.where(later, move(plain, 16, 0), jnp.where(lane == sub, 1.0, 0.0))
    for c in range(24):
        splat[c] = spread_lane(weights, 24 + c)
    rows = rows_of(pieces) + [(own, i) for i in range(BLK)]

    def combine(places, plus_own):
        def body(c, carry):
            part = pl.ds(pl.multiple_of(c * 32, 32), 32)
            for low in (0, 4):
                if plus_own:
                    totals = [own[low + k, part, :] for k in range(4)]
                else:
                    totals = [jnp.zeros((32, 128), F32)] * 4
                for n in places:
                    r, i = rows[n]
                    cells = r[i, part, :]
                    totals = [
                        t + splat[n, pl.ds(low + k, 1), :] * cells for k, t in enumerate(totals)
                    ]
                for k in range(4):
                    out[low + k, part, :] = totals[k]
            return carry

        lax.fori_loop(0, own.shape[1] // 32, body, 0)

    pl.when(later)(lambda: combine(range(16), True))
    pl.when(second)(lambda: combine((2, 3, 4, 5, 10, 11, 12, 13, *OWN), False))
    pl.when(band == 0)(lambda: combine(OWN, False))


def inner_kernel(f_ref, v_ref, out, *sums):
    def body(i, carry):
        layers = [f_ref[i, x] for x in range(4)]
        for x in range(4):
            here = layers[x]
            total = 3.0 * stencil_weights[0] * here
            for offset in range(1, 5):
                beside = pltpu.roll(here, offset, 0) + pltpu.roll(here, 64 - offset, 0)
                beside = beside + pltpu.roll(here, offset, 1) + pltpu.roll(here, 128 - offset, 1)
                if x + offset < 4:
                    beside = beside + layers[x + offset]
                if x - offset >= 0:
                    beside = beside + layers[x - offset]
                total = total + stencil_weights[offset] * beside
            out[i, x] = -0.5 * total + v_ref[x] * here
        return carry

    lax.fori_loop(0, BLK, body, 0)
    if sums:

        def row(i):
            return lambda c: f_ref[i, c // 8, pl.ds(pl.multiple_of((c % 8) * 8, 8), 8), :]

        load = {n: row(n - 16) for n in OWN}
        sums[0][...] = pair_sums([[(q, r) for q in OWN for r in range(16, q + 1)]], load, 32)


def edged(inner, x, left, right):
    total = None
    for offset in range(1, 5):
        if x + offset >= 4:
            term = stencil_weights[offset] * right(x + offset - 4)
            total = term if total is None else total + term
        if x - offset < 0:
            term = stencil_weights[offset] * left(x - offset + 4)
            total = term if total is None else total + term
    return inner - 0.5 * total


def image_kernel(own, inner, left, right, out, sums):
    def body(i, carry):
        for x in range(4):
            part = pl.ds(64 * x, 64)
            out[i, part, :] = edged(
                inner[i, part, :],
                x,
                lambda n: left[i, pl.ds(64 * n, 64), :],
                lambda n: right[i, pl.ds(64 * n, 64), :],
            )
        return carry

    lax.fori_loop(0, BLK, body, 0)
    load = {n: loader(own, n - 16) for n in OWN}
    load |= {n: loader(out, n - 24) for n in IMAGE}
    jobs = [[(q, r) for q in IMAGE for r in OWN if r <= q - 8]]
    sums[...] = pair_sums(jobs, load, own.shape[1] // 8)


def dot(left, right, turn_left=False, turn_right=False):
    dims = (((0 if turn_left else 1,), (1 if turn_right else 0,)), ((), ()))
    return lax.dot_general(
        left, right, dims, precision=lax.Precision.HIGHEST, preferred_element_type=F32
    )


def places(y, home=None):
    row = lax.broadcasted_iota(jnp.int32, (128, 128), 0)
    lane = lax.broadcasted_iota(jnp.int32, (128, 128), 1)
    distance = (row + 2) >> 2
    distance = jnp.where(((row + 2) & 2) == 0, -distance, distance)
    piece = (y + distance) & 7
    target = (piece & 1) * 8 + (piece >> 1) * 2 + (row & 1)
    if home is None:
        target = jnp.where(row < 16, target, row)
    else:
        target = jnp.where((piece & 1) == home, -1, target)
        target = jnp.where(row < 16, target, row - 16 + 8 * home)
    return jnp.where((lane == target) & (row < 24), 1.0, 0.0)


def with_mirror(packed):
    lane, sub = lanes(), subs()
    tiles = unpacked(packed)
    mirror = jnp.transpose(tall([move(tiles[2], 24, 0)]))[0:8]
    tiles[2] = tiles[2] + move(jnp.where(lane == sub, 0.0, mirror), 0, 24)
    return tall(tiles)


def image_columns(packed, place, target):
    wide = lax.broadcasted_iota(jnp.int32, (128, 128), 1)
    columns = dot(place, with_mirror(packed), turn_left=True)
    columns = pltpu.roll(columns, (target - 24) % 128, 1)
    return jnp.where((wide >= target) & (wide < target + 8), columns, 0.0)


def prepare_kernel(weights_ref, own_ref, ordered_ref, half_ref):
    lane = lanes()
    row = lax.broadcasted_iota(jnp.int32, (128, 128), 0)
    place = places(lax.axis_index("band") & 7)
    weights = jnp.where(lane < 24, pltpu.roll(weights_ref[...], 104, 1), 0.0)
    weights = dot(weights, place)
    block = image_columns(own_ref[...], place, 16)
    half = dot(weights, block)
    half_ref[...] = half + dot(weights, jnp.where(row < 16, block, 0.0), turn_right=True)
    ordered_ref[...] = weights


def coeff_kernel(weights_ref, half_ref, gram_ref, near_ref, far_ref, out):
    lane, sub = lanes(), subs()
    row = lax.broadcasted_iota(jnp.int32, (128, 128), 0)
    near = lax.axis_index("band") < RING
    weights = weights_ref[...]

    def visiting(n):
        packed = jnp.where(near, near_ref[n], far_ref[n])
        return image_columns(packed, places(n, n), 8 * n)

    half = half_ref[...] + dot(weights, jnp.where(row < 16, visiting(0) + visiting(1), 0.0))
    theta = dot(half, tall([weights]), turn_right=True)
    work = gram_ref[...] + move(theta, 0, 8)
    for k in range(8):
        line = work[k : k + 1, :]
        line = jnp.broadcast_to(line / jnp.broadcast_to(line[:, k : k + 1], (1, 128)), (8, 128))
        work = jnp.where(sub == k, line, work - spread_lane(work, k) * line)
    for j in range(8):
        out[j] = spread_lane(work, 8 + j)


def partial_kernel(f_ref, inner_ref, splat, out):
    def body(c, carry):
        part = pl.ds(pl.multiple_of(c * 32, 32), 32)
        for low in (0, 4):
            totals = [inner_ref[low + k, part, :] for k in range(4)]
            for i in range(BLK):
                cells = f_ref[i, part, :]
                totals = [
                    t - splat[low + k, pl.ds(i, 1), :] * cells for k, t in enumerate(totals)
                ]
            for k in range(4):
                out[low + k, part, :] = totals[k]
        return carry

    lax.fori_loop(0, f_ref.shape[1] // 32, body, 0)


def edge_kernel(partial, across, beside, out):
    def run(left, right):
        def body(i, carry):
            for x in range(4):
                part = pl.ds(64 * x, 64)
                out[i, part, :] = edged(
                    partial[i, part, :],
                    x,
                    lambda n: left[i, pl.ds(64 * n, 64), :],
                    lambda n: right[i, pl.ds(64 * n, 64), :],
                )
            return carry

        lax.fori_loop(0, BLK, body, 0)

    odd = lax.axis_index("domain") & 1
    pl.when(odd == 0)(lambda: run(across, beside))
    pl.when(odd == 1)(lambda: run(beside, across))


def domain_parts(copies):
    return lax.all_to_all(copies, "domain", 0, 0)


def ring_shift(block, step):
    pairs = [(z * RING + y, z * RING + (y + step) % RING) for z in range(2) for y in range(RING)]
    return lax.ppermute(block, "band", pairs)


def neighbours(block):
    count = lax.axis_size("domain")
    left = lax.ppermute(block, "domain", [(i, (i + 1) % count) for i in range(count)])
    right = lax.ppermute(block, "domain", [((i + 1) % count, i) for i in range(count)])
    return left, right


def exchanged(block):
    count = lax.axis_size("domain")
    across = [(i, (i + 1 if i % 2 else i - 1) % count) for i in range(count)]
    beside = [(i, i ^ 1) for i in range(count)]
    return lax.ppermute(block, "domain", across), lax.ppermute(block, "domain", beside)


def local(orbitals, potential):
    blocks, slab_width, rows_y, rows_z = orbitals.shape
    domain = lax.axis_size("domain")
    cells_total = float(slab_width * rows_y * rows_z * domain)
    band = lax.axis_index("band")
    flat = (blocks, slab_width * rows_y, rows_z)
    big = flat[0] * flat[1] * flat[2]
    slab = jax.ShapeDtypeStruct(flat, F32)
    field = jax.ShapeDtypeStruct(orbitals.shape, F32)
    tile = jax.ShapeDtypeStruct((8, 128), F32)

    def inner_part(block, *sums):
        return call(
            inner_kernel,
            (field, *sums),
            specs=[VMEM] * 2,
            flops=60 * big,
            bytes_moved=8 * big,
        )(block, potential)

    own = orbitals.reshape(flat)
    quarters = [own[2 * k : 2 * k + 2] for k in range(4)]
    arrived = [
        lax.ppermute(quarters[k], "band", [(0, place), (1, place + 1)])
        for k, place in ((1, 2), (3, 6), (2, RING + 4))
    ]
    inner, sums = inner_part(orbitals, tile)
    arrived, inner, sums = lax.optimization_barrier((arrived, inner, sums))
    piece = jnp.where(band < 2, quarters[0], 0.0)
    for part in arrived:
        piece = piece + part
    left, right = neighbours(own)
    far_first = (4, 5)
    pairs = [(y + RING, y) if y in far_first else (y, y + RING) for y in range(RING)]
    crossed = lax.ppermute(piece, "band", pairs)
    from_far = ((band & 7) == far_first[0]) | ((band & 7) == far_first[1])
    piece = jnp.where((band < RING) != from_far, piece, crossed)

    def stage(fresh, imaged, pieces, *sums, last=False):
        sources = (*pieces, own, *((image,) if imaged else ()), *sums)
        return call(
            lambda *refs: stage_kernel(len(pieces), fresh, imaged, last, *refs),
            jax.ShapeDtypeStruct((domain, 8, 128), F32) if last else tile,
            specs=[VMEM] * len(sources),
            flops=20 * big,
            bytes_moved=10 * big,
        )(*sources)

    pieces = [piece]
    up, down = ring_shift(piece, 1), ring_shift(piece, -1)
    pieces += [up, down]
    up, down = ring_shift(up, 1), ring_shift(down, -1)
    sums = stage(range(6), (), pieces, sums)
    down, sums = lax.optimization_barrier((down, sums))
    pieces += [up, down]
    up, down = ring_shift(up, 1), ring_shift(down, -1)
    sums = stage(range(6, 10), (), pieces, sums)
    down, sums, left, right = lax.optimization_barrier((down, sums, left, right))
    pieces += [up, down]
    up, down = ring_shift(up[:1], 1), ring_shift(down[1:], -1)
    image, image_sums = call(
        image_kernel, (slab, tile), specs=[VMEM] * 4, flops=50 * big, bytes_moved=20 * big
    )(own, inner.reshape(flat), left, right)
    sums = stage(range(10, 14), range(14), pieces, sums, image_sums)
    pieces += [up, down]
    sums = stage(range(14, 16), range(14, 16), pieces, sums, last=True)
    sums = call(
        lambda *refs: total_kernel(cells_total, *refs),
        tile,
        specs=[VMEM],
        flops=40 * 1024,
        bytes_moved=160 * 1024,
    )(domain_parts(sums))
    basis, weights, gram = call(
        combine_kernel,
        (slab, tile, tile),
        scratch=[pltpu.VMEM((24, 8, 128), F32)],
        specs=[VMEM] * 11,
        flops=48 * big,
        bytes_moved=16 * big,
    )(sums, *pieces, own)
    across, beside = exchanged(basis)
    inner = inner_part(basis.reshape(orbitals.shape))[0].reshape(flat)
    shared = sums
    other = lax.ppermute(shared, "band", [(0, 1), (1, 0)])
    shared = jnp.stack([jnp.where(band == 0, shared, other), jnp.where(band == 0, other, shared)])
    shared = jnp.where(band < 2, shared, 0.0)
    shared = shared + lax.ppermute(shared, "band", [(0, 4), (1, 5)])
    shared = shared + lax.ppermute(shared, "band", [(0, 2), (1, 3), (4, 6), (5, 7)])
    far = lax.ppermute(shared, "band", [(y, y + RING) for y in range(RING)])
    ordered, half = call(prepare_kernel, (tile, tile), specs=[VMEM] * 2)(weights, sums)
    splat = call(coeff_kernel, jax.ShapeDtypeStruct((8, 8, 128), F32), specs=[VMEM] * 5)(
        ordered, half, gram, shared, far
    )
    partial = call(
        partial_kernel, slab, specs=[VMEM] * 3, flops=16 * big, bytes_moved=12 * big
    )(basis, inner, splat)
    residual = call(
        edge_kernel, slab, specs=[VMEM] * 3, flops=20 * big, bytes_moved=16 * big
    )(partial, across, beside)
    return (basis.reshape(orbitals.shape), residual.reshape(orbitals.shape))


def solution(mesh):
    return jax.shard_map(
        local,
        mesh=mesh,
        in_specs=(P("band", "domain", None, None), P("domain", None, None)),
        out_specs=(P("band", "domain", None, None), P("band", "domain", None, None)),
        check_vma=False,
    )
```

```python
import jax
import jax.numpy as jnp
from jax import lax
from jax.experimental import pallas as pl
from jax.experimental.pallas import tpu as pltpu
from jax.sharding import PartitionSpec as P

stencil_weights = (-205.0 / 72.0, 8.0 / 5.0, -1.0 / 5.0, 8.0 / 315.0, -1.0 / 560.0)
BLK = 8
RING = 8
F32 = jnp.float32
VMEM = pl.BlockSpec(memory_space=pltpu.VMEM)


def call(kernel, outs, scratch=(), specs=None, flops=0, bytes_moved=0):
    return pl.pallas_call(
        kernel,
        out_shape=outs,
        in_specs=specs,
        out_specs=jax.tree.map(lambda _: VMEM, outs),
        scratch_shapes=scratch,
        compiler_params=pltpu.CompilerParams(vmem_limit_bytes=32 * 1024 * 1024),
        cost_estimate=pl.CostEstimate(flops=flops, bytes_accessed=bytes_moved, transcendentals=0),
    )


def lanes():
    return lax.broadcasted_iota(jnp.int32, (8, 128), 1)


def subs():
    return lax.broadcasted_iota(jnp.int32, (8, 128), 0)


def folded(rows):
    sub = subs()
    step = 4
    while step:
        lower = (sub & step) == 0
        merged = []
        for first, second in zip(rows[:step], rows[step:]):
            if first is not None:
                first = first + pltpu.roll(first, 8 - step, 0)
            if second is not None:
                second = second + pltpu.roll(second, step, 0)
            if first is None and second is None:
                merged.append(None)
            else:
                merged.append(
                    jnp.where(lower, 0.0 if first is None else first, 0.0 if second is None else second)
                )
        rows = merged
        step //= 2
    return rows[0]


def pair_sums(jobs, load, chunks):
    lane = lanes()
    result = jnp.zeros((8, 128), F32)
    for pairs in jobs:
        used = sorted({n for pair in pairs for n in pair})

        def body(c, sums, pairs=pairs, used=used):
            for step in range(4):
                rows = {n: load[n](4 * c + step) for n in used}
                sums = tuple(s + rows[q] * rows[r] for s, (q, r) in zip(sums, pairs))
            return sums

        zero = jnp.zeros((8, 128), F32)
        sums = lax.fori_loop(0, chunks // 4, body, (zero,) * len(pairs))
        columns = {}
        for s, (q, r) in zip(sums, pairs):
            columns.setdefault(32 * (r // 8) + q, [None] * 8)[r % 8] = s
        for place, rows in columns.items():
            column = jnp.sum(folded(rows), axis=1, keepdims=True)
            result = result + jnp.where(lane == place, column, 0.0)
    return result


def loader(ref, index):
    return lambda c: ref[index, pl.ds(pl.multiple_of(c * 8, 8), 8), :]


def move(tile, source, target):
    lane = lanes()
    if source != target:
        tile = pltpu.roll(tile, (target - source) % 128, 1)
    return jnp.where((lane >= target) & (lane < target + 8), tile, 0.0)


def spread_lane(tile, k):
    return jnp.broadcast_to(tile[:, k : k + 1], (8, 128))


def rows_of(refs):
    return [(r, i) for r in refs for i in range(r.shape[0])]


def unpacked(sums):
    lane = lanes()
    parts = [sums] + [pltpu.roll(sums, 128 - 32 * n, 1) for n in (1, 2)]
    return [jnp.where(lane < 32, part, 0.0) for part in parts]


def tall(tiles):
    return jnp.concatenate(tiles + [jnp.zeros((128 - 8 * len(tiles), 128), F32)], axis=0)


OWN = list(range(16, 24))
IMAGE = list(range(24, 32))
BLOCK0_ROWS = (2, 3, 4, 5, 10, 11, 12, 13)


def split(pairs, size=36):
    if not pairs:
        return []
    count = -(-len(pairs) // size)
    size = -(-len(pairs) // count)
    return [pairs[n : n + size] for n in range(0, len(pairs), size)]


def stage_kernel(parts, fresh, imaged, last, *refs):
    out = refs[-1]
    pieces, refs = refs[:parts], refs[parts:-1]
    own, image, before = (refs[0], refs[1], refs[2:]) if imaged else (refs[0], None, refs[1:])
    chunks = own.shape[1] // 8
    load = {n: loader(r, i) for n, (r, i) in enumerate(rows_of(pieces))}
    load |= {n: loader(own, n - 16) for n in OWN}
    if imaged:
        load |= {n: loader(image, n - 24) for n in IMAGE}
    jobs = split([(q, r) for q in OWN for r in fresh])
    jobs += split([(q, r) for q in fresh for r in range(q + 1)])
    jobs += split([(q, r) for q in IMAGE for r in imaged])
    total = pair_sums(jobs, load, chunks)
    for part in before:
        total = total + part[...]
    if last:
        for n in range(out.shape[0]):
            out[n] = total
    else:
        out[...] = total


def total_kernel(cells_total, parts_ref, out):
    out[...] = jnp.sum(parts_ref[...], axis=0) / cells_total


def combine_kernel(sums_ref, *refs):
    *pieces, own, out, weights_ref, gram_ref, splat = refs
    band = lax.axis_index("band")
    lane, sub = lanes(), subs()
    tiles = unpacked(sums_ref[...])
    turned = jnp.transpose(tall(tiles))
    w0, w1, w2 = (
        jnp.where(lane < 24, tile + jnp.where(lane == sub + 8 * n, 0.0, turned[8 * n : 8 * n + 8]), 0.0)
        for n, tile in enumerate(tiles)
    )
    later = band >= 2
    second = band == 1

    def taken(position):
        place = position & 7
        return later | (second & (place >= 2) & (place <= 5))

    row_in = taken(sub)
    lane_in = (lane >= 16) | taken(lane)
    kept = row_in & lane_in
    w0 = jnp.where(kept, w0, jnp.where(lane == sub, 1.0, 0.0))
    w1 = jnp.where(kept, w1, jnp.where(lane == 8 + sub, 1.0, 0.0))
    w0 = w0 + jnp.where(lane == 24 + sub, 1.0, 0.0)
    w1 = w1 + jnp.where(lane == 32 + sub, 1.0, 0.0)
    w2 = jnp.where(lane_in, w2, 0.0) + jnp.where(lane == 40 + sub, 1.0, 0.0)
    def subtracted(steps):
        tiles = [w0, w1, w2]
        for k in steps:
            v, s = divmod(k, 8)
            row = tiles[v][s : s + 1, :]
            row = row / jnp.broadcast_to(row[:, k : k + 1], (1, 128))
            row = jnp.broadcast_to(row, (8, 128))
            for u in range(v, 3):
                column = spread_lane(tiles[u], k)
                if u == v:
                    column = jnp.where(sub > s, column, 0.0)
                tiles[u] = tiles[u] - column * row
        return tiles[2]

    def normalised(scaled):
        for k in range(8):
            row = scaled[k : k + 1, :]
            row = row / jnp.broadcast_to(row[:, 16 + k : 17 + k], (1, 128))
            column = jnp.where(sub > k, spread_lane(scaled, 16 + k), 0.0)
            scaled = scaled - column * jnp.broadcast_to(row, (8, 128))
        pivots = jnp.sum(jnp.where(lane == 16 + sub, scaled, 0.0), axis=1, keepdims=True)
        return scaled / jnp.sqrt(jnp.broadcast_to(pivots, (8, 128)))

    plain = lax.cond(
        later,
        lambda: subtracted(range(16)),
        lambda: lax.cond(second, lambda: normalised(subtracted(BLOCK0_ROWS)), lambda: normalised(w2)),
    )
    weights = plain
    weights_ref[...] = weights
    gram_ref[...] = jnp.where(later, move(plain, 16, 0), jnp.where(lane == sub, 1.0, 0.0))
    for c in range(24):
        splat[c] = spread_lane(weights, 24 + c)
    rows = rows_of(pieces) + [(own, i) for i in range(BLK)]

    def combine(places, plus_own):
        def body(c, carry):
            part = pl.ds(pl.multiple_of(c * 32, 32), 32)
            for low in (0, 4):
                if plus_own:
                    totals = [own[low + k, part, :] for k in range(4)]
                else:
                    totals = [jnp.zeros((32, 128), F32)] * 4
                for n in places:
                    r, i = rows[n]
                    cells = r[i, part, :]
                    totals = [
                        t + splat[n, pl.ds(low + k, 1), :] * cells for k, t in enumerate(totals)
                    ]
                for k in range(4):
                    out[low + k, part, :] = totals[k]
            return carry

        lax.fori_loop(0, own.shape[1] // 32, body, 0)

    pl.when(later)(lambda: combine(range(16), True))
    pl.when(second)(lambda: combine((*BLOCK0_ROWS, *OWN), False))
    pl.when(band == 0)(lambda: combine(OWN, False))


def inner_kernel(f_ref, v_ref, out, *sums):
    def body(i, carry):
        layers = [f_ref[i, x] for x in range(4)]
        for x in range(4):
            here = layers[x]
            total = 3.0 * stencil_weights[0] * here
            for offset in range(1, 5):
                beside = pltpu.roll(here, offset, 0) + pltpu.roll(here, 64 - offset, 0)
                beside = beside + pltpu.roll(here, offset, 1) + pltpu.roll(here, 128 - offset, 1)
                if x + offset < 4:
                    beside = beside + layers[x + offset]
                if x - offset >= 0:
                    beside = beside + layers[x - offset]
                total = total + stencil_weights[offset] * beside
            out[i, x] = -0.5 * total + v_ref[x] * here
        return carry

    lax.fori_loop(0, BLK, body, 0)
    if sums:

        def row(i):
            return lambda c: f_ref[i, c // 8, pl.ds(pl.multiple_of((c % 8) * 8, 8), 8), :]

        load = {n: row(n - 16) for n in OWN}
        sums[0][...] = pair_sums([[(q, r) for q in OWN for r in range(16, q + 1)]], load, 32)


def edged(inner, x, left, right):
    total = None
    for offset in range(1, 5):
        if x + offset >= 4:
            term = stencil_weights[offset] * right(x + offset - 4)
            total = term if total is None else total + term
        if x - offset < 0:
            term = stencil_weights[offset] * left(x - offset + 4)
            total = term if total is None else total + term
    return inner - 0.5 * total


def image_kernel(own, inner, left, right, out, sums):
    def body(i, carry):
        for x in range(4):
            part = pl.ds(64 * x, 64)
            out[i, part, :] = edged(
                inner[i, part, :],
                x,
                lambda n: left[i, pl.ds(64 * n, 64), :],
                lambda n: right[i, pl.ds(64 * n, 64), :],
            )
        return carry

    lax.fori_loop(0, BLK, body, 0)
    load = {n: loader(own, n - 16) for n in OWN}
    load |= {n: loader(out, n - 24) for n in IMAGE}
    jobs = [[(q, r) for q in IMAGE for r in OWN if r <= q - 8]]
    sums[...] = pair_sums(jobs, load, own.shape[1] // 8)


def dot(left, right, turn_left=False, turn_right=False):
    dims = (((0 if turn_left else 1,), (1 if turn_right else 0,)), ((), ()))
    return lax.dot_general(
        left, right, dims, precision=lax.Precision.HIGHEST, preferred_element_type=F32
    )


def places(y, home=None):
    row = lax.broadcasted_iota(jnp.int32, (128, 128), 0)
    lane = lax.broadcasted_iota(jnp.int32, (128, 128), 1)
    distance = (row + 2) >> 2
    distance = jnp.where(((row + 2) & 2) == 0, -distance, distance)
    piece = (y + distance) & 7
    target = (piece & 1) * 8 + (piece >> 1) * 2 + (row & 1)
    if home is None:
        target = jnp.where(row < 16, target, row)
    else:
        target = jnp.where((piece & 1) == home, -1, target)
        target = jnp.where(row < 16, target, row - 16 + 8 * home)
    return jnp.where((lane == target) & (row < 24), 1.0, 0.0)


def with_mirror(packed):
    lane, sub = lanes(), subs()
    tiles = unpacked(packed)
    mirror = jnp.transpose(tall([move(tiles[2], 24, 0)]))[0:8]
    tiles[2] = tiles[2] + move(jnp.where(lane == sub, 0.0, mirror), 0, 24)
    return tall(tiles)


def image_columns(packed, place, target):
    wide = lax.broadcasted_iota(jnp.int32, (128, 128), 1)
    columns = dot(place, with_mirror(packed), turn_left=True)
    columns = pltpu.roll(columns, (target - 24) % 128, 1)
    return jnp.where((wide >= target) & (wide < target + 8), columns, 0.0)


def prepare_kernel(weights_ref, own_ref, ordered_ref, half_ref):
    lane = lanes()
    row = lax.broadcasted_iota(jnp.int32, (128, 128), 0)
    place = places(lax.axis_index("band") & 7)
    weights = jnp.where(lane < 24, pltpu.roll(weights_ref[...], 104, 1), 0.0)
    weights = dot(weights, place)
    block = image_columns(own_ref[...], place, 16)
    half = dot(weights, block)
    half_ref[...] = half + dot(weights, jnp.where(row < 16, block, 0.0), turn_right=True)
    ordered_ref[...] = weights


def coeff_kernel(weights_ref, half_ref, gram_ref, near_ref, far_ref, out):
    lane, sub = lanes(), subs()
    row = lax.broadcasted_iota(jnp.int32, (128, 128), 0)
    near = lax.axis_index("band") < RING
    weights = weights_ref[...]

    def visiting(n):
        packed = jnp.where(near, near_ref[n], far_ref[n])
        return image_columns(packed, places(n, n), 8 * n)

    half = half_ref[...] + dot(weights, jnp.where(row < 16, visiting(0) + visiting(1), 0.0))
    theta = dot(half, tall([weights]), turn_right=True)
    work = gram_ref[...] + move(theta, 0, 8)
    for k in range(8):
        line = work[k : k + 1, :]
        line = jnp.broadcast_to(line / jnp.broadcast_to(line[:, k : k + 1], (1, 128)), (8, 128))
        work = jnp.where(sub == k, line, work - spread_lane(work, k) * line)
    for j in range(8):
        out[j] = spread_lane(work, 8 + j)


def partial_kernel(f_ref, inner_ref, splat, out):
    def body(c, carry):
        part = pl.ds(pl.multiple_of(c * 32, 32), 32)
        for low in (0, 4):
            totals = [inner_ref[low + k, part, :] for k in range(4)]
            for i in range(BLK):
                cells = f_ref[i, part, :]
                totals = [
                    t - splat[low + k, pl.ds(i, 1), :] * cells for k, t in enumerate(totals)
                ]
            for k in range(4):
                out[low + k, part, :] = totals[k]
        return carry

    lax.fori_loop(0, f_ref.shape[1] // 32, body, 0)


def edge_kernel(partial, across, beside, out):
    def run(left, right):
        def body(i, carry):
            for x in range(4):
                part = pl.ds(64 * x, 64)
                out[i, part, :] = edged(
                    partial[i, part, :],
                    x,
                    lambda n: left[i, pl.ds(64 * n, 64), :],
                    lambda n: right[i, pl.ds(64 * n, 64), :],
                )
            return carry

        lax.fori_loop(0, BLK, body, 0)

    odd = lax.axis_index("domain") & 1
    pl.when(odd == 0)(lambda: run(across, beside))
    pl.when(odd == 1)(lambda: run(beside, across))


def domain_parts(copies):
    return lax.all_to_all(copies, "domain", 0, 0)


def ring_shift(block, step):
    pairs = [(z * RING + y, z * RING + (y + step) % RING) for z in range(2) for y in range(RING)]
    return lax.ppermute(block, "band", pairs)


def neighbours(block):
    count = lax.axis_size("domain")
    left = lax.ppermute(block, "domain", [(i, (i + 1) % count) for i in range(count)])
    right = lax.ppermute(block, "domain", [((i + 1) % count, i) for i in range(count)])
    return left, right


def exchanged(block):
    count = lax.axis_size("domain")
    across = [(i, (i + 1 if i % 2 else i - 1) % count) for i in range(count)]
    beside = [(i, i ^ 1) for i in range(count)]
    return lax.ppermute(block, "domain", across), lax.ppermute(block, "domain", beside)


def local(orbitals, potential):
    blocks, slab_width, rows_y, rows_z = orbitals.shape
    domain = lax.axis_size("domain")
    cells_total = float(slab_width * rows_y * rows_z * domain)
    band = lax.axis_index("band")
    flat = (blocks, slab_width * rows_y, rows_z)
    big = flat[0] * flat[1] * flat[2]
    slab = jax.ShapeDtypeStruct(flat, F32)
    field = jax.ShapeDtypeStruct(orbitals.shape, F32)
    tile = jax.ShapeDtypeStruct((8, 128), F32)

    def inner_part(block, *sums):
        return call(
            inner_kernel,
            (field, *sums),
            specs=[VMEM] * 2,
            flops=60 * big,
            bytes_moved=8 * big,
        )(block, potential)

    own = orbitals.reshape(flat)
    quarters = [own[2 * k : 2 * k + 2] for k in range(4)]
    arrived = [
        lax.ppermute(quarters[k], "band", [(0, 2 * k), (1, 2 * k + 1)]) for k in (1, 3, 2)
    ]
    inner, sums = inner_part(orbitals, tile)
    arrived, inner, sums = lax.optimization_barrier((arrived, inner, sums))
    piece = jnp.where(band < 2, quarters[0], 0.0)
    for part in arrived:
        piece = piece + part
    left, right = neighbours(own)
    crossed = lax.ppermute(piece, "band", [(y, y + RING) for y in range(RING)])
    piece = jnp.where(band < RING, piece, crossed)

    def stage(fresh, imaged, pieces, *sums, last=False):
        sources = (*pieces, own, *((image,) if imaged else ()), *sums)
        return call(
            lambda *refs: stage_kernel(len(pieces), fresh, imaged, last, *refs),
            jax.ShapeDtypeStruct((domain, 8, 128), F32) if last else tile,
            specs=[VMEM] * len(sources),
            flops=20 * big,
            bytes_moved=10 * big,
        )(*sources)

    pieces = [piece]
    up, down = ring_shift(piece, 1), ring_shift(piece, -1)
    pieces += [up, down]
    up, down = ring_shift(up, 1), ring_shift(down, -1)
    sums = stage(range(6), (), pieces, sums)
    down, sums = lax.optimization_barrier((down, sums))
    pieces += [up, down]
    up, down = ring_shift(up, 1), ring_shift(down, -1)
    sums = stage(range(6, 10), (), pieces, sums)
    down, sums, left, right = lax.optimization_barrier((down, sums, left, right))
    pieces += [up, down]
    up, down = ring_shift(up[:1], 1), ring_shift(down[1:], -1)
    image, image_sums = call(
        image_kernel, (slab, tile), specs=[VMEM] * 4, flops=50 * big, bytes_moved=20 * big
    )(own, inner.reshape(flat), left, right)
    sums = stage(range(10, 14), range(14), pieces, sums, image_sums)
    pieces += [up, down]
    sums = stage(range(14, 16), range(14, 16), pieces, sums, last=True)
    sums = call(
        lambda *refs: total_kernel(cells_total, *refs),
        tile,
        specs=[VMEM],
        flops=40 * 1024,
        bytes_moved=160 * 1024,
    )(domain_parts(sums))
    basis, weights, gram = call(
        combine_kernel,
        (slab, tile, tile),
        scratch=[pltpu.VMEM((24, 8, 128), F32)],
        specs=[VMEM] * 11,
        flops=48 * big,
        bytes_moved=16 * big,
    )(sums, *pieces, own)
    across, beside = exchanged(basis)
    inner = inner_part(basis.reshape(orbitals.shape))[0].reshape(flat)
    shared = sums
    other = lax.ppermute(shared, "band", [(0, 1), (1, 0)])
    shared = jnp.stack([jnp.where(band == 0, shared, other), jnp.where(band == 0, other, shared)])
    shared = jnp.where(band < 2, shared, 0.0)
    shared = shared + lax.ppermute(shared, "band", [(0, 4), (1, 5)])
    shared = shared + lax.ppermute(shared, "band", [(0, 2), (1, 3), (4, 6), (5, 7)])
    far = lax.ppermute(shared, "band", [(y, y + RING) for y in range(RING)])
    ordered, half = call(prepare_kernel, (tile, tile), specs=[VMEM] * 2)(weights, sums)
    splat = call(coeff_kernel, jax.ShapeDtypeStruct((8, 8, 128), F32), specs=[VMEM] * 5)(
        ordered, half, gram, shared, far
    )
    partial = call(
        partial_kernel, slab, specs=[VMEM] * 3, flops=16 * big, bytes_moved=12 * big
    )(basis, inner, splat)
    residual = call(
        edge_kernel, slab, specs=[VMEM] * 3, flops=20 * big, bytes_moved=16 * big
    )(partial, across, beside)
    return (basis.reshape(orbitals.shape), residual.reshape(orbitals.shape))


def solution(mesh):
    return jax.shard_map(
        local,
        mesh=mesh,
        in_specs=(P("band", "domain", None, None), P("domain", None, None)),
        out_specs=(P("band", "domain", None, None), P("band", "domain", None, None)),
        check_vma=False,
    )
```

```python
import jax
import jax.numpy as jnp
from jax import lax
from jax.experimental import pallas as pl
from jax.experimental.pallas import tpu as pltpu
from jax.sharding import PartitionSpec as P

stencil_weights = (-205.0 / 72.0, 8.0 / 5.0, -1.0 / 5.0, 8.0 / 315.0, -1.0 / 560.0)
BLK = 8
RING = 8
F32 = jnp.float32
VMEM = pl.BlockSpec(memory_space=pltpu.VMEM)
ANY = pl.BlockSpec(memory_space=pl.ANY)


def call(kernel, outs, scratch=(), specs=None, flops=0, bytes_moved=0, out_specs=None):
    return pl.pallas_call(
        kernel,
        out_shape=outs,
        in_specs=specs,
        out_specs=out_specs or jax.tree.map(lambda _: VMEM, outs),
        scratch_shapes=scratch,
        compiler_params=pltpu.CompilerParams(vmem_limit_bytes=32 * 1024 * 1024),
        cost_estimate=pl.CostEstimate(flops=flops, bytes_accessed=bytes_moved, transcendentals=0),
    )


def lanes():
    return lax.broadcasted_iota(jnp.int32, (8, 128), 1)


def subs():
    return lax.broadcasted_iota(jnp.int32, (8, 128), 0)


def folded(rows):
    sub = subs()
    step = 4
    while step:
        lower = (sub & step) == 0
        merged = []
        for first, second in zip(rows[:step], rows[step:]):
            if first is not None:
                first = first + pltpu.roll(first, 8 - step, 0)
            if second is not None:
                second = second + pltpu.roll(second, step, 0)
            if first is None and second is None:
                merged.append(None)
            else:
                merged.append(
                    jnp.where(lower, 0.0 if first is None else first, 0.0 if second is None else second)
                )
        rows = merged
        step //= 2
    return rows[0]


def pair_sums(jobs, load, chunks):
    lane = lanes()
    result = jnp.zeros((8, 128), F32)
    for pairs in jobs:
        used = sorted({n for pair in pairs for n in pair})

        def body(c, sums, pairs=pairs, used=used):
            for step in range(4):
                rows = {n: load[n](4 * c + step) for n in used}
                sums = tuple(s + rows[q] * rows[r] for s, (q, r) in zip(sums, pairs))
            return sums

        zero = jnp.zeros((8, 128), F32)
        sums = lax.fori_loop(0, chunks // 4, body, (zero,) * len(pairs))
        columns = {}
        for s, (q, r) in zip(sums, pairs):
            columns.setdefault(32 * (r // 8) + q, [None] * 8)[r % 8] = s
        for place, rows in columns.items():
            column = jnp.sum(folded(rows), axis=1, keepdims=True)
            result = result + jnp.where(lane == place, column, 0.0)
    return result


def loader(ref, index):
    return lambda c: ref[index, pl.ds(pl.multiple_of(c * 8, 8), 8), :]


def move(tile, source, target):
    lane = lanes()
    if source != target:
        tile = pltpu.roll(tile, (target - source) % 128, 1)
    return jnp.where((lane >= target) & (lane < target + 8), tile, 0.0)


def spread_lane(tile, k):
    return jnp.broadcast_to(tile[:, k : k + 1], (8, 128))


def rows_of(refs):
    return [(r, i) for r in refs for i in range(r.shape[0])]


def unpacked(sums):
    lane = lanes()
    parts = [sums] + [pltpu.roll(sums, 128 - 32 * n, 1) for n in (1, 2)]
    return [jnp.where(lane < 32, part, 0.0) for part in parts]


def tall(tiles):
    return jnp.concatenate(tiles + [jnp.zeros((128 - 8 * len(tiles), 128), F32)], axis=0)


OWN = list(range(16, 24))
IMAGE = list(range(24, 32))
BLOCK0_ROWS = (2, 3, 4, 5, 10, 11, 12, 13)


def split(pairs, size=36):
    if not pairs:
        return []
    count = -(-len(pairs) // size)
    size = -(-len(pairs) // count)
    return [pairs[n : n + size] for n in range(0, len(pairs), size)]


def stage_kernel(parts, fresh, imaged, last, *refs):
    out = refs[-1]
    pieces, refs = refs[:parts], refs[parts:-1]
    own, image, before = (refs[0], refs[1], refs[2:]) if imaged else (refs[0], None, refs[1:])
    chunks = own.shape[1] // 8
    load = {n: loader(r, i) for n, (r, i) in enumerate(rows_of(pieces))}
    load |= {n: loader(own, n - 16) for n in OWN}
    if imaged:
        load |= {n: loader(image, n - 24) for n in IMAGE}
    jobs = split([(q, r) for q in OWN for r in fresh])
    jobs += split([(q, r) for q in fresh for r in range(q + 1)])
    jobs += split([(q, r) for q in IMAGE for r in imaged])
    total = pair_sums(jobs, load, chunks)
    for part in before:
        total = total + part[...]
    if last:
        for n in range(out.shape[0]):
            out[n] = total
    else:
        out[...] = total


def total_kernel(cells_total, parts_ref, out):
    out[...] = jnp.sum(parts_ref[...], axis=0) / cells_total


def combine_kernel(sums_ref, *refs):
    *pieces, own, result, weights_ref, gram_ref, splat, out, sems = refs
    band = lax.axis_index("band")
    lane, sub = lanes(), subs()
    tiles = unpacked(sums_ref[...])
    turned = jnp.transpose(tall(tiles))
    w0, w1, w2 = (
        jnp.where(lane < 24, tile + jnp.where(lane == sub + 8 * n, 0.0, turned[8 * n : 8 * n + 8]), 0.0)
        for n, tile in enumerate(tiles)
    )
    later = band >= 2
    second = band == 1

    def taken(position):
        place = position & 7
        return later | (second & (place >= 2) & (place <= 5))

    row_in = taken(sub)
    lane_in = (lane >= 16) | taken(lane)
    kept = row_in & lane_in
    w0 = jnp.where(kept, w0, jnp.where(lane == sub, 1.0, 0.0))
    w1 = jnp.where(kept, w1, jnp.where(lane == 8 + sub, 1.0, 0.0))
    w0 = w0 + jnp.where(lane == 24 + sub, 1.0, 0.0)
    w1 = w1 + jnp.where(lane == 32 + sub, 1.0, 0.0)
    w2 = jnp.where(lane_in, w2, 0.0) + jnp.where(lane == 40 + sub, 1.0, 0.0)
    def subtracted(steps):
        tiles = [w0, w1, w2]
        for k in steps:
            v, s = divmod(k, 8)
            row = tiles[v][s : s + 1, :]
            row = row / jnp.broadcast_to(row[:, k : k + 1], (1, 128))
            row = jnp.broadcast_to(row, (8, 128))
            for u in range(v, 3):
                column = spread_lane(tiles[u], k)
                if u == v:
                    column = jnp.where(sub > s, column, 0.0)
                tiles[u] = tiles[u] - column * row
        return tiles[2]

    def normalised(scaled):
        for k in range(8):
            row = scaled[k : k + 1, :]
            row = row / jnp.broadcast_to(row[:, 16 + k : 17 + k], (1, 128))
            column = jnp.where(sub > k, spread_lane(scaled, 16 + k), 0.0)
            scaled = scaled - column * jnp.broadcast_to(row, (8, 128))
        pivots = jnp.sum(jnp.where(lane == 16 + sub, scaled, 0.0), axis=1, keepdims=True)
        return scaled / jnp.sqrt(jnp.broadcast_to(pivots, (8, 128)))

    plain = lax.cond(
        later,
        lambda: subtracted(range(16)),
        lambda: lax.cond(second, lambda: normalised(subtracted(BLOCK0_ROWS)), lambda: normalised(w2)),
    )
    weights = plain
    weights_ref[...] = weights
    gram_ref[...] = jnp.where(later, move(plain, 16, 0), jnp.where(lane == sub, 1.0, 0.0))
    for c in range(24):
        splat[c] = spread_lane(weights, 24 + c)
    rows = rows_of(pieces) + [(own, i) for i in range(BLK)]

    def copy(c):
        part = pl.ds(pl.multiple_of(c * 32, 32), 32)
        return pltpu.make_async_copy(out.at[:, part, :], result.at[:, part, :], sems.at[c])

    def combine(places, plus_own):
        def body(c, carry):
            part = pl.ds(pl.multiple_of(c * 32, 32), 32)
            for low in (0, 4):
                if plus_own:
                    totals = [own[low + k, part, :] for k in range(4)]
                else:
                    totals = [jnp.zeros((32, 128), F32)] * 4
                for n in places:
                    r, i = rows[n]
                    cells = r[i, part, :]
                    totals = [
                        t + splat[n, pl.ds(low + k, 1), :] * cells for k, t in enumerate(totals)
                    ]
                for k in range(4):
                    out[low + k, part, :] = totals[k]
            copy(c).start()
            return carry

        lax.fori_loop(0, own.shape[1] // 32, body, 0)

    pl.when(later)(lambda: combine(range(16), True))
    pl.when(second)(lambda: combine((*BLOCK0_ROWS, *OWN), False))
    pl.when(band == 0)(lambda: combine(OWN, False))
    for c in range(8):
        copy(c).wait()


def inner_kernel(f_ref, v_ref, out, *sums):
    def body(i, carry):
        layers = [f_ref[i, x] for x in range(4)]
        for x in range(4):
            here = layers[x]
            total = 3.0 * stencil_weights[0] * here
            for offset in range(1, 5):
                beside = pltpu.roll(here, offset, 0) + pltpu.roll(here, 64 - offset, 0)
                beside = beside + pltpu.roll(here, offset, 1) + pltpu.roll(here, 128 - offset, 1)
                if x + offset < 4:
                    beside = beside + layers[x + offset]
                if x - offset >= 0:
                    beside = beside + layers[x - offset]
                total = total + stencil_weights[offset] * beside
            out[i, x] = -0.5 * total + v_ref[x] * here
        return carry

    lax.fori_loop(0, BLK, body, 0)
    if sums:

        def row(i):
            return lambda c: f_ref[i, c // 8, pl.ds(pl.multiple_of((c % 8) * 8, 8), 8), :]

        load = {n: row(n - 16) for n in OWN}
        sums[0][...] = pair_sums([[(q, r) for q in OWN for r in range(16, q + 1)]], load, 32)


def edged(inner, x, left, right):
    total = None
    for offset in range(1, 5):
        if x + offset >= 4:
            term = stencil_weights[offset] * right(x + offset - 4)
            total = term if total is None else total + term
        if x - offset < 0:
            term = stencil_weights[offset] * left(x - offset + 4)
            total = term if total is None else total + term
    return inner - 0.5 * total


def image_kernel(own, inner, left, right, out, sums):
    def body(i, carry):
        for x in range(4):
            part = pl.ds(64 * x, 64)
            out[i, part, :] = edged(
                inner[i, part, :],
                x,
                lambda n: left[i, pl.ds(64 * n, 64), :],
                lambda n: right[i, pl.ds(64 * n, 64), :],
            )
        return carry

    lax.fori_loop(0, BLK, body, 0)
    load = {n: loader(own, n - 16) for n in OWN}
    load |= {n: loader(out, n - 24) for n in IMAGE}
    jobs = [[(q, r) for q in IMAGE for r in OWN if r <= q - 8]]
    sums[...] = pair_sums(jobs, load, own.shape[1] // 8)


def dot(left, right, turn_left=False, turn_right=False):
    dims = (((0 if turn_left else 1,), (1 if turn_right else 0,)), ((), ()))
    return lax.dot_general(
        left, right, dims, precision=lax.Precision.HIGHEST, preferred_element_type=F32
    )


def places(y, home=None):
    row = lax.broadcasted_iota(jnp.int32, (128, 128), 0)
    lane = lax.broadcasted_iota(jnp.int32, (128, 128), 1)
    distance = (row + 2) >> 2
    distance = jnp.where(((row + 2) & 2) == 0, -distance, distance)
    piece = (y + distance) & 7
    target = (piece & 1) * 8 + (piece >> 1) * 2 + (row & 1)
    if home is None:
        target = jnp.where(row < 16, target, row)
    else:
        target = jnp.where((piece & 1) == home, -1, target)
        target = jnp.where(row < 16, target, row - 16 + 8 * home)
    return jnp.where((lane == target) & (row < 24), 1.0, 0.0)


def with_mirror(packed):
    lane, sub = lanes(), subs()
    tiles = unpacked(packed)
    mirror = jnp.transpose(tall([move(tiles[2], 24, 0)]))[0:8]
    tiles[2] = tiles[2] + move(jnp.where(lane == sub, 0.0, mirror), 0, 24)
    return tall(tiles)


def image_columns(packed, place, target):
    wide = lax.broadcasted_iota(jnp.int32, (128, 128), 1)
    columns = dot(place, with_mirror(packed), turn_left=True)
    columns = pltpu.roll(columns, (target - 24) % 128, 1)
    return jnp.where((wide >= target) & (wide < target + 8), columns, 0.0)


def prepare_kernel(weights_ref, own_ref, ordered_ref, half_ref):
    lane = lanes()
    row = lax.broadcasted_iota(jnp.int32, (128, 128), 0)
    place = places(lax.axis_index("band") & 7)
    weights = jnp.where(lane < 24, pltpu.roll(weights_ref[...], 104, 1), 0.0)
    weights = dot(weights, place)
    block = image_columns(own_ref[...], place, 16)
    half = dot(weights, block)
    half_ref[...] = half + dot(weights, jnp.where(row < 16, block, 0.0), turn_right=True)
    ordered_ref[...] = weights


def coeff_kernel(weights_ref, half_ref, gram_ref, near_ref, far_ref, out):
    lane, sub = lanes(), subs()
    row = lax.broadcasted_iota(jnp.int32, (128, 128), 0)
    near = lax.axis_index("band") < RING
    weights = weights_ref[...]

    def visiting(n):
        packed = jnp.where(near, near_ref[n], far_ref[n])
        return image_columns(packed, places(n, n), 8 * n)

    half = half_ref[...] + dot(weights, jnp.where(row < 16, visiting(0) + visiting(1), 0.0))
    theta = dot(half, tall([weights]), turn_right=True)
    work = gram_ref[...] + move(theta, 0, 8)
    for k in range(8):
        line = work[k : k + 1, :]
        line = jnp.broadcast_to(line / jnp.broadcast_to(line[:, k : k + 1], (1, 128)), (8, 128))
        work = jnp.where(sub == k, line, work - spread_lane(work, k) * line)
    for j in range(8):
        out[j] = spread_lane(work, 8 + j)


def partial_kernel(f_ref, inner_ref, splat, out):
    def body(c, carry):
        part = pl.ds(pl.multiple_of(c * 32, 32), 32)
        for low in (0, 4):
            totals = [inner_ref[low + k, part, :] for k in range(4)]
            for i in range(BLK):
                cells = f_ref[i, part, :]
                totals = [
                    t - splat[low + k, pl.ds(i, 1), :] * cells for k, t in enumerate(totals)
                ]
            for k in range(4):
                out[low + k, part, :] = totals[k]
        return carry

    lax.fori_loop(0, f_ref.shape[1] // 32, body, 0)


def edge_kernel(partial, across, beside, result, out, sems):
    def copy(i):
        return pltpu.make_async_copy(out.at[i], result.at[i], sems.at[i])

    def run(left, right):
        def body(i, carry):
            for x in range(4):
                part = pl.ds(64 * x, 64)
                out[i, part, :] = edged(
                    partial[i, part, :],
                    x,
                    lambda n: left[i, pl.ds(64 * n, 64), :],
                    lambda n: right[i, pl.ds(64 * n, 64), :],
                )
            copy(i).start()
            return carry

        lax.fori_loop(0, BLK, body, 0)

    odd = lax.axis_index("domain") & 1
    pl.when(odd == 0)(lambda: run(across, beside))
    pl.when(odd == 1)(lambda: run(beside, across))
    for i in range(BLK):
        copy(i).wait()


def domain_parts(copies):
    return lax.all_to_all(copies, "domain", 0, 0)


def ring_shift(block, step):
    pairs = [(z * RING + y, z * RING + (y + step) % RING) for z in range(2) for y in range(RING)]
    return lax.ppermute(block, "band", pairs)


def neighbours(block):
    count = lax.axis_size("domain")
    left = lax.ppermute(block, "domain", [(i, (i + 1) % count) for i in range(count)])
    right = lax.ppermute(block, "domain", [((i + 1) % count, i) for i in range(count)])
    return left, right


def exchanged(block):
    count = lax.axis_size("domain")
    across = [(i, (i + 1 if i % 2 else i - 1) % count) for i in range(count)]
    beside = [(i, i ^ 1) for i in range(count)]
    return lax.ppermute(block, "domain", across), lax.ppermute(block, "domain", beside)


def local(orbitals, potential):
    blocks, slab_width, rows_y, rows_z = orbitals.shape
    domain = lax.axis_size("domain")
    cells_total = float(slab_width * rows_y * rows_z * domain)
    band = lax.axis_index("band")
    flat = (blocks, slab_width * rows_y, rows_z)
    big = flat[0] * flat[1] * flat[2]
    slab = jax.ShapeDtypeStruct(flat, F32)
    field = jax.ShapeDtypeStruct(orbitals.shape, F32)
    tile = jax.ShapeDtypeStruct((8, 128), F32)

    def inner_part(block, *sums):
        return call(
            inner_kernel,
            (field, *sums),
            specs=[VMEM] * 2,
            flops=60 * big,
            bytes_moved=8 * big,
        )(block, potential)

    own = orbitals.reshape(flat)
    quarters = [own[2 * k : 2 * k + 2] for k in range(4)]
    arrived = [
        lax.ppermute(quarters[k], "band", [(0, 2 * k), (1, 2 * k + 1)]) for k in (1, 3, 2)
    ]
    inner, sums = inner_part(orbitals, tile)
    arrived, inner, sums = lax.optimization_barrier((arrived, inner, sums))
    piece = jnp.where(band < 2, quarters[0], 0.0)
    for part in arrived:
        piece = piece + part
    left, right = neighbours(own)
    crossed = lax.ppermute(piece, "band", [(y, y + RING) for y in range(RING)])
    piece = jnp.where(band < RING, piece, crossed)

    def stage(fresh, imaged, pieces, *sums, last=False):
        sources = (*pieces, own, *((image,) if imaged else ()), *sums)
        return call(
            lambda *refs: stage_kernel(len(pieces), fresh, imaged, last, *refs),
            jax.ShapeDtypeStruct((domain, 8, 128), F32) if last else tile,
            specs=[VMEM] * len(sources),
            flops=20 * big,
            bytes_moved=10 * big,
        )(*sources)

    pieces = [piece]
    up, down = ring_shift(piece, 1), ring_shift(piece, -1)
    pieces += [up, down]
    up, down = ring_shift(up, 1), ring_shift(down, -1)
    sums = stage(range(6), (), pieces, sums)
    down, sums = lax.optimization_barrier((down, sums))
    pieces += [up, down]
    up, down = ring_shift(up, 1), ring_shift(down, -1)
    sums = stage(range(6, 10), (), pieces, sums)
    down, sums, left, right = lax.optimization_barrier((down, sums, left, right))
    pieces += [up, down]
    up, down = ring_shift(up[:1], 1), ring_shift(down[1:], -1)
    image, image_sums = call(
        image_kernel, (slab, tile), specs=[VMEM] * 4, flops=50 * big, bytes_moved=20 * big
    )(own, inner.reshape(flat), left, right)
    sums = stage(range(10, 14), range(14), pieces, sums, image_sums)
    pieces += [up, down]
    sums = stage(range(14, 16), range(14, 16), pieces, sums, last=True)
    sums = call(
        lambda *refs: total_kernel(cells_total, *refs),
        tile,
        specs=[VMEM],
        flops=40 * 1024,
        bytes_moved=160 * 1024,
    )(domain_parts(sums))
    basis, weights, gram = call(
        combine_kernel,
        (slab, tile, tile),
        scratch=[
            pltpu.VMEM((24, 8, 128), F32),
            pltpu.VMEM(flat, F32),
            pltpu.SemaphoreType.DMA((8,)),
        ],
        out_specs=(ANY, VMEM, VMEM),
        specs=[VMEM] * 11,
        flops=48 * big,
        bytes_moved=16 * big,
    )(sums, *pieces, own)
    across, beside = exchanged(basis)
    inner = inner_part(basis.reshape(orbitals.shape))[0].reshape(flat)
    shared = sums
    other = lax.ppermute(shared, "band", [(0, 1), (1, 0)])
    shared = jnp.stack([jnp.where(band == 0, shared, other), jnp.where(band == 0, other, shared)])
    shared = jnp.where(band < 2, shared, 0.0)
    shared = shared + lax.ppermute(shared, "band", [(0, 4), (1, 5)])
    shared = shared + lax.ppermute(shared, "band", [(0, 2), (1, 3), (4, 6), (5, 7)])
    far = lax.ppermute(shared, "band", [(y, y + RING) for y in range(RING)])
    ordered, half = call(prepare_kernel, (tile, tile), specs=[VMEM] * 2)(weights, sums)
    splat = call(coeff_kernel, jax.ShapeDtypeStruct((8, 8, 128), F32), specs=[VMEM] * 5)(
        ordered, half, gram, shared, far
    )
    partial = call(
        partial_kernel, slab, specs=[VMEM] * 3, flops=16 * big, bytes_moved=12 * big
    )(basis, inner, splat)
    residual = call(
        edge_kernel,
        slab,
        scratch=[pltpu.VMEM(flat, F32), pltpu.SemaphoreType.DMA((BLK,))],
        specs=[VMEM] * 3,
        out_specs=ANY,
        flops=20 * big,
        bytes_moved=16 * big,
    )(partial, across, beside)
    return (basis.reshape(orbitals.shape), residual.reshape(orbitals.shape))


def solution(mesh):
    return jax.shard_map(
        local,
        mesh=mesh,
        in_specs=(P("band", "domain", None, None), P("domain", None, None)),
        out_specs=(P("band", "domain", None, None), P("band", "domain", None, None)),
        check_vma=False,
    )
```
